512 devices in a mesh: gx: 32 (over z, core), gy: 4 (over x), gz: 4 (over y).
Axes of the slice: x: 4, y: 4, z: 16, core: 2. Of those that a mesh axis runs over, the one named last changes fastest.
Arguments:
- fluid_temp: float32 [512, 256, 512], P('gx', 'gy', 'gz'), may hold values from -6 to 6
- liquid: int32 [512, 256, 512], P('gx', 'gy', 'gz'), may hold values 0 or 1
- face_src: int32 [1024, 4, 4, 128], P('gx', 'gy', 'gz'), may hold values from -1 to 131071, as said below
- face_dst: int32 [1024, 4, 4, 128], P('gx', 'gy', 'gz'), may hold values from -1 to 1023, as said below
- solid_old: float32 [16, 256, 128], P(('gy', 'gz'), 'gx'), may hold values from -6 to 6
- solid_diag: float32 [16, 256, 128], P(('gy', 'gz'), 'gx'), may hold values from 4 to 16
- blocks: float32 [16, 256, 5, 128, 128], P(('gy', 'gz'), 'gx'), may hold values from -0.25 to 0.25
- pattern: int32 [16, 256, 5], P(('gy', 'gz'), 'gx'), may hold values 0 or 1
Outputs:
- fluid_new: float32 [512, 256, 512], P('gx', 'gy', 'gz')
- solid_temp: float32 [16, 256, 128], P(('gy', 'gz'), 'gx')
The draws below stay inside these ranges and needn't reach their ends.
Inputs may be any that keep to these rules, and one draw needn't show every extreme that they name: `face_src`: entry q * 32 + r of slab (a, b) lists in its first c slots local cells of brick (q, a, b) whose temperatures go to run r, c from 1 to 128 and 128 in some blocks of every draw; the other slots hold -1; cells may repeat. `face_dst`: entry r * 32 + q of slab (a, b) names, slot by slot, the local solid cell of run r that receives the matching slot of face_src entry q * 32 + r, and -1 exactly where that slot of face_src is -1; cells may repeat.
All inputs are finite; a program needn't handle non-finite values. No bound on the sum of `liquid` or of `pattern` on one device may be relied on, other than what follows from the above.
Results may differ from the reference program's by a relative error of at most 0.00014.
Values sent between devices are 32-bit elements; how exact they have to be, the bound alone decides.
No kernel may reach another device: no remote copies, remote signals or barrier semaphores. Data moves between devices by JAX's collectives and lax.ppermute only.
A program may use at most 64 MiB of HBM per device.

```python
import math
import jax
import jax.numpy as jnp
from jax import lax

CX = 16
CY = 64
CZ = 128
TILE = 128
TILE_DEV = 8
REACH = 2
FACE_CAP = 128
SWEEPS = 4
NB = 5
SENDERS = 32
BRICKS_Y = 4
BRICKS_Z = 4
SLABS = 16
TILES = 256
NX = 512
NY = 256
NZ = 512


def face_lists(key):
    base = jax.random.fold_in(key, 7301)
    key_small, key_full, key_source, key_target = jax.random.split(base, 4)
    grid = (SENDERS, SENDERS, BRICKS_Y, BRICKS_Z)
    small = jax.random.randint(key_small, grid, 1, FACE_CAP // 2 + 1)
    full = jax.random.randint(key_full, grid, 0, 8) == 0
    counts = jnp.where(full, FACE_CAP, small)
    counts = counts.at[0, 0].set(FACE_CAP)
    slot_ids = jnp.arange(FACE_CAP, dtype=jnp.int32)
    live = slot_ids < counts[..., None]
    sources = jax.random.randint(key_source, grid + (FACE_CAP,), 0, CX * CY * CZ)
    targets = jax.random.randint(key_target, grid + (FACE_CAP,), 0, TILE_DEV * TILE)
    sources = sources.at[0, 0, :, :, 0].set(CX * CY * CZ - 1).at[0, 0, :, :, 1].set(0)
    targets = targets.at[0, 0, :, :, 0].set(TILE_DEV * TILE - 1).at[0, 0, :, :, 1].set(0)
    sources = jnp.where(live, sources, -1).astype(jnp.int32)
    targets = jnp.where(live, targets, -1).astype(jnp.int32)
    sources = sources.reshape(SENDERS * SENDERS, BRICKS_Y, BRICKS_Z, FACE_CAP)
    targets = jnp.transpose(targets, (1, 0, 2, 3, 4)).reshape(SENDERS * SENDERS, BRICKS_Y, BRICKS_Z, FACE_CAP)
    return (sources, targets)


def draw_face_src(key, part):
    return face_lists(key)[0]


def draw_face_dst(key, part):
    return face_lists(key)[1]


def touch_ends(entries, own_key, least, largest):
    extent = entries.shape
    place = [jax.random.randint(jax.random.fold_in(own_key, axis), (), 0, extent[axis]) for axis in range(len(extent))]
    entries = entries.at[tuple(place)].set(least)
    longest = extent.index(max(extent))
    place[longest] = (place[longest] + 1) % extent[longest]
    return entries.at[tuple(place)].set(largest)


def shard_levels(own_key, dims, cuts, smallest, largest):
    factor_of, own = 1.0, jax.random.fold_in(own_key, 6)
    for dim, blocks in cuts:
        heights = jnp.exp(jax.random.uniform(jax.random.fold_in(own, dim), (blocks,), jnp.float32, smallest / len(cuts), largest / len(cuts)))
        factor_of = factor_of * jnp.repeat(heights, dims[dim] // blocks).reshape([-1 if axis == dim else 1 for axis in range(len(dims))])
    return factor_of


def gaussian(stream_key, shape, scale, limit, cuts=(), held_as=jnp.bfloat16):
    drawn = jax.random.normal(stream_key, shape, jnp.float32) * scale
    if len(cuts) > 0:
        drawn = shard_levels(stream_key, shape, cuts, -0.22, 0.18) * drawn
    return jnp.clip(drawn, min=-limit, max=limit).astype(held_as)


def setup_inputs(seed: int = 0) -> dict:
    key_list = jax.random.split(jax.random.key(seed), 9)
    fluid_temp = gaussian(key_list[0], (NX, NY, NZ), 1.0, 6.0, ((0, 32), (1, 4), (2, 4)), jnp.float32)
    liquid = touch_ends((jax.random.randint(key_list[1], (NX, NY, NZ), 0, 2) < 1).astype(jnp.int32), jax.random.fold_in(key_list[1], 1), 0, 1)
    face_src = draw_face_src(jax.random.fold_in(key_list[8], 71), 0)
    face_dst = draw_face_dst(jax.random.fold_in(key_list[8], 71), 0)
    solid_old = gaussian(key_list[4], (SLABS, TILES, TILE), 1.0, 6.0, ((0, 16), (1, 32)), jnp.float32)
    solid_diag = jnp.clip(jnp.exp(math.log(16.0) - 1.3862944 * jax.random.uniform(key_list[5], (SLABS, TILES, TILE), jnp.float32) ** shard_levels(key_list[5], (SLABS, TILES, TILE), ((0, 16), (1, 32)), -0.2, 0.2)), 4.0, 16.0)
    blocks = gaussian(key_list[6], (SLABS, TILES, NB, TILE, TILE), (NB * TILE) ** -0.5, 0.25, ((0, 16), (1, 32)), jnp.float32)
    pattern = touch_ends((jax.random.randint(key_list[7], (SLABS, TILES, NB), 0, 4) < 3).astype(jnp.int32), jax.random.fold_in(key_list[7], 1), 0, 1)
    return dict(fluid_temp=fluid_temp, liquid=liquid, face_src=face_src, face_dst=face_dst, solid_old=solid_old, solid_diag=solid_diag, blocks=blocks, pattern=pattern)


DIFFUSION = 0.12
EVAPORATION = 0.5
SATURATION = 0.25
WALL_COUPLING = 0.2


def apply_tiles(values, blocks_slab, pattern_slab, diagonal):
    padded = jnp.pad(values, ((REACH, REACH), (0, 0)))
    summed = diagonal * values
    for offset in range(NB):
        neighbour = padded[offset:offset + TILES]
        product = jnp.einsum("tab,tb->ta", blocks_slab[:, offset], neighbour, precision=lax.Precision.HIGHEST)
        summed = summed + pattern_slab[:, offset][:, None].astype(jnp.float32) * product
    return summed


def solve_slab(operands):
    right_side, blocks_slab, pattern_slab, diagonal = operands
    inverse = 1.0 / diagonal
    iterate = inverse * right_side
    residual = right_side - apply_tiles(iterate, blocks_slab, pattern_slab, diagonal)
    update = inverse * residual
    iterate = iterate + update
    rho_old = 0.5
    for sweep in range(1, SWEEPS):
        rho_next = 1.0 / (4.0 - rho_old)
        residual = right_side - apply_tiles(iterate, blocks_slab, pattern_slab, diagonal)
        update = (rho_next * rho_old) * update + (4.0 * rho_next) * inverse * residual
        iterate = iterate + update
        rho_old = rho_next
    return iterate


def reference(fluid_temp, liquid, face_src, face_dst, solid_old, solid_diag, blocks, pattern):
    fluid_cells = NX * NY * NZ
    solid_total = SLABS * TILES * TILE
    sources = face_src.reshape(SENDERS, SENDERS, BRICKS_Y, BRICKS_Z, FACE_CAP)
    first_ids = jnp.arange(SENDERS, dtype=jnp.int32).reshape(-1, 1, 1, 1, 1)
    y_ids = jnp.arange(BRICKS_Y, dtype=jnp.int32).reshape(1, 1, -1, 1, 1)
    z_ids = jnp.arange(BRICKS_Z, dtype=jnp.int32).reshape(1, 1, 1, -1, 1)
    clipped = jnp.maximum(sources, 0)
    row_in = clipped // (CY * CZ)
    column = (clipped // CZ) % CY
    depth = clipped % CZ
    global_ids = ((first_ids * CX + row_in) * NY + y_ids * CY + column) * NZ + z_ids * CZ + depth
    global_ids = jnp.where(sources >= 0, global_ids, fluid_cells).astype(jnp.int32)
    flat_temp = jnp.concatenate([fluid_temp.reshape(-1), jnp.zeros((1,), jnp.float32)])
    outgoing = flat_temp[global_ids]
    targets = face_dst.reshape(SENDERS, SENDERS, BRICKS_Y, BRICKS_Z, FACE_CAP)
    slab_ids = y_ids * BRICKS_Z + z_ids
    solid_ids = slab_ids * (TILES * TILE) + first_ids * (TILE_DEV * TILE) + jnp.maximum(targets, 0)
    solid_ids = jnp.where(targets >= 0, solid_ids, solid_total).astype(jnp.int32)
    arriving = jnp.transpose(outgoing, (1, 0, 2, 3, 4))
    gathered = jnp.zeros((solid_total + 1,), jnp.float32).at[solid_ids].add(arriving)[:solid_total]
    right_side = solid_diag * solid_old + gathered.reshape(SLABS, TILES, TILE)
    solid_temp = lax.map(solve_slab, (right_side, blocks, pattern, solid_diag))
    solid_flat = jnp.concatenate([solid_temp.reshape(-1), jnp.zeros((1,), jnp.float32)])
    returned = jnp.transpose(solid_flat[solid_ids], (1, 0, 2, 3, 4))
    wall_sum = jnp.zeros((fluid_cells + 1,), jnp.float32).at[global_ids].add(returned - outgoing)[:fluid_cells]
    wall_sum = wall_sum.reshape(NX, NY, NZ)
    laplacian = -6.0 * fluid_temp
    for dimension in range(3):
        laplacian = laplacian + jnp.roll(fluid_temp, 1, dimension) + jnp.roll(fluid_temp, -1, dimension)
    liquid_share = liquid.astype(jnp.float32)
    fluid_new = fluid_temp + DIFFUSION * laplacian - EVAPORATION * liquid_share * jnp.maximum(fluid_temp - SATURATION, 0.0) + WALL_COUPLING * wall_sum
    return fluid_new, solid_temp
```

```python
import functools

import jax
import jax.numpy as jnp
from jax import lax
from jax.experimental import pallas as pl
from jax.experimental.pallas import tpu as pltpu
from jax.sharding import PartitionSpec as P

F32 = jnp.float32
BF16 = jnp.bfloat16
I32 = jnp.int32
RUNS = 32
WIDTH = 128
ROWS = 1024
TILES = 8
NB = 5
WIN = 24

DIFFUSION = 0.12
EVAPORATION = 0.5
SATURATION = 0.25
WALL_COUPLING = 0.2

VMEM = pl.BlockSpec(memory_space=pltpu.VMEM)


def params(mib):
    return pltpu.CompilerParams(vmem_limit_bytes=mib << 20)


def two_parts(values):
    high = values.astype(BF16)
    return high, (values - high.astype(F32)).astype(BF16)


def lanes(rows):
    return jnp.concatenate(rows, axis=1)


def row_hots(row, count):
    width = row.shape[1]
    part = min(count, 256)
    level = lax.broadcasted_iota(I32, (part, width), 0).astype(F32).astype(BF16)
    one, zero = jnp.ones((), BF16), jnp.zeros((), BF16)
    parts = []
    for index in range(count // part):
        here = jnp.where((row >= index * part) & (row < (index + 1) * part), row - index * part, -1)
        parts.append(jnp.where(level == here.astype(F32).astype(BF16), one, zero))
    return parts[0] if len(parts) == 1 else jnp.concatenate(parts, axis=0)


def placed_parts(column, count, values):
    width = column.shape[1]
    mask = lax.broadcasted_iota(I32, (count, width), 0) == column
    high = values.astype(BF16).astype(F32)
    low = values - high
    both = [jnp.where(mask, part, 0.0) for part in (high, low)]
    return jnp.concatenate(both, axis=0).astype(BF16)


CONTRACT_LAST = (((1,), (1,)), ((), ()))


def pick_kernel(fluid, src, dst, old, diag, pattern, sent, outgoing, on_chip, across, y_faces, z_faces, table):
    parity = lax.rem(lax.axis_index("gx"), 2)
    for block in range(8):
        turned = fluid[128 * block : 128 * block + 128, :].T
        z_faces[0, block : block + 1, :] = turned[0:1, :]
        z_faces[1, block : block + 1, :] = turned[127:128, :]
        high, low = two_parts(turned)
        table[0:128, 128 * block : 128 * block + 128] = high
        table[128:256, 128 * block : 128 * block + 128] = low
    for slab in range(16):
        y_faces[0, slab : slab + 1, :] = fluid[64 * slab : 64 * slab + 1, :]
        y_faces[1, slab : slab + 1, :] = fluid[64 * slab + 63 : 64 * slab + 64, :]
    first, last = fluid[0:64, :], fluid[960:1024, :]
    for packed, face in ((on_chip, jnp.where(parity == 0, last, first)), (across, jnp.where(parity == 0, first, last))):
        packed[0:32, :] = dst[...].astype(F32)
        packed[32:40, :] = old[...]
        packed[40:48, :] = diag[...]
        packed[48:56, :] = jnp.zeros((8, WIDTH), F32)
        packed[48:56, 0:NB] = pattern[...].astype(F32)
        packed[56:120, :] = face
    group = 4
    for start in range(0, RUNS, group):
        ids = lanes([src[r : r + 1, :] for r in range(start, start + group)])
        picked = jnp.dot(table[...], row_hots(ids >> 7, ROWS), preferred_element_type=F32)
        both = picked[0:128] + picked[128:256]
        mask = lax.broadcasted_iota(I32, (WIDTH, group * WIDTH), 0) == (ids & 127)
        value = jnp.sum(jnp.where(mask, both, 0.0), axis=0, keepdims=True)
        for r in range(start, start + group):
            mine = value[:, (r - start) * WIDTH : (r - start + 1) * WIDTH]
            outgoing[r : r + 1, :] = mine
            sent[r, :, 0:128] = mine
            sent[r ^ 1, :, 128:256] = mine
            beside = (r + 1) % RUNS if r % 2 else (r - 1) % RUNS
            sent[beside, :, 256:384] = mine


def spread_run(ids_of, values_of):
    group = 8
    total = None
    for start in range(0, RUNS, group):
        cell = lanes([ids_of(r) for r in range(start, start + group)])
        value = lanes([values_of(r) for r in range(start, start + group)])
        row = jnp.where(cell >= 0, ((cell >> 5) & 3) * 8 + (cell >> 7), -1)
        hots = row_hots(row, 32)
        placed = placed_parts(cell & 31, 32, value)
        added = lax.dot_general(hots, placed, CONTRACT_LAST, preferred_element_type=F32)
        total = added if total is None else total + added
    total = total[:, 0:32] + total[:, 32:64]
    return lanes([total[8 * u : 8 * u + 8, :] for u in range(4)])


def window(parity, own, partner, beside):
    pad = jnp.zeros((4, WIDTH), F32)
    low = jnp.concatenate([beside[4:8], own, partner, pad], axis=0)
    high = jnp.concatenate([partner, own, beside[0:4], pad], axis=0)
    return jnp.where(parity == 0, low, high)


def neighbours(iterate, pats, first, count, shifted):
    for offset in range(NB):
        values = iterate[first - 2 + offset : first - 2 + offset + count, :]
        shifted[offset, first : first + count, :] = values * pats[offset, first : first + count, :]


def apply_tile(blocks, tile, shifted, place, coupled):
    total = None
    for offset in range(NB):
        term = blocks[tile, offset] * shifted[offset, pl.ds(place, 1), :]
        total = term if total is None else total + term
    coupled[pl.ds(place, 1), :] = jnp.sum(total.T, axis=0, keepdims=True)


RHO = [0.5]
for _ in range(3):
    RHO.append(1.0 / (4.0 - RHO[-1]))


def wall_first_kernel(
    arrived, dst, old, diag, pattern, on_chip, across, own_blocks, partner_blocks, beside_blocks,
    state, pats, swap, iterate, shifted, coupled,
):
    me = lax.axis_index("gx")
    parity = lax.rem(me, 2)
    at_edge = (me == 0) | (me == RUNS - 1)
    keep = jnp.where(at_edge, 0.0, 1.0)
    added = [
        spread_run(lambda r: dst[r : r + 1, :], lambda r: arrived[r, :, 0:128]),
        spread_run(lambda r: on_chip[r : r + 1, :].astype(I32), lambda r: arrived[r, :, 128:256]),
        spread_run(lambda r: across[r : r + 1, :].astype(I32), lambda r: arrived[r, :, 256:384]),
    ]
    diagonals = [diag[...], on_chip[40:48, :], across[40:48, :]]
    olds = [old[...], on_chip[32:40, :], across[32:40, :]]
    rights = [d * o + a for d, o, a in zip(diagonals, olds, added)]
    inverses = [1.0 / d for d in diagonals]
    rights[2], inverses[2] = rights[2] * keep, inverses[2] * keep
    own_pattern = jnp.concatenate([pattern[...].astype(F32), jnp.zeros((TILES, WIDTH - NB), F32)], axis=1)
    present = window(parity, own_pattern, on_chip[48:56, :], across[48:56, :])
    for offset in range(NB):
        pats[offset] = jnp.broadcast_to(present[:, offset : offset + 1], (WIN, WIDTH))
    right = window(parity, *rights)
    inverse = window(parity, *inverses)
    diagonal = window(parity, *diagonals)
    value = inverse * right
    iterate[...] = value
    shifted[...] = jnp.zeros((NB, WIN, WIDTH), F32)
    coupled[...] = jnp.zeros((WIN, WIDTH), F32)
    own_at, partner_at, beside_at = 4 + 4 * parity, 12 - 12 * parity, 2 + 14 * parity

    neighbours(iterate, pats, 2, 16, shifted)
    for tile in range(TILES):
        apply_tile(own_blocks, tile, shifted, own_at + tile, coupled)
    for tile in range(6):
        apply_tile(partner_blocks, tile + 2 * parity, shifted, partner_at + tile + 2 * parity, coupled)
    for tile in range(2):
        apply_tile(beside_blocks, tile, shifted, beside_at + tile, coupled)
    update = inverse * (right - (diagonal * value + coupled[...]))
    value = value + update
    iterate[...] = value

    neighbours(iterate, pats, 4, 12, shifted)
    for tile in range(TILES):
        apply_tile(own_blocks, tile, shifted, own_at + tile, coupled)
    for tile in range(4):
        apply_tile(partner_blocks, tile + 4 * parity, shifted, partner_at + tile + 4 * parity, coupled)
    update = RHO[1] * RHO[0] * update + 4.0 * RHO[1] * inverse * (right - (diagonal * value + coupled[...]))
    value = value + update
    state[0], state[1], state[2], state[3], state[4] = value, update, right, inverse, diagonal
    swap[0:4, :] = jnp.where(parity == 0, value[4:8], value[12:16])
    swap[4:8, :] = jnp.where(parity == 0, update[4:8], update[12:16])


def wall_second_kernel(
    state, pats, swapped, dst, own_blocks, partner_blocks, beside_blocks,
    solid, returned, iterate, shifted, coupled,
):
    me = lax.axis_index("gx")
    parity = lax.rem(me, 2)
    at_edge = (me == 0) | (me == RUNS - 1)
    keep = jnp.where(at_edge, 0.0, 1.0)
    value, update, right, inverse, diagonal = (state[i] for i in range(5))

    def with_swapped(inside, outside):
        low = jnp.concatenate([outside, inside[4:24]], axis=0)
        high = jnp.concatenate([inside[0:16], outside, inside[20:24]], axis=0)
        return jnp.where(parity == 0, low, high)

    value = with_swapped(value, swapped[0:4, :] * keep)
    update = with_swapped(update, swapped[4:8, :] * keep)
    own_at, partner_at, beside_at = 4 + 4 * parity, 12 - 12 * parity, 2 + 14 * parity
    iterate[...] = value
    shifted[...] = jnp.zeros((NB, WIN, WIDTH), F32)
    coupled[...] = jnp.zeros((WIN, WIDTH), F32)

    neighbours(iterate, pats, 2, 16, shifted)
    for tile in range(TILES):
        apply_tile(own_blocks, tile, shifted, own_at + tile, coupled)
    for tile in range(2):
        apply_tile(partner_blocks, tile + 6 * parity, shifted, partner_at + tile + 6 * parity, coupled)
    for tile in range(2):
        apply_tile(beside_blocks, tile, shifted, beside_at + tile, coupled)
    update = RHO[2] * RHO[1] * update + 4.0 * RHO[2] * inverse * (right - (diagonal * value + coupled[...]))
    value = value + update
    iterate[...] = value

    neighbours(iterate, pats, 4, 12, shifted)
    for tile in range(TILES):
        apply_tile(own_blocks, tile, shifted, own_at + tile, coupled)
    update = RHO[3] * RHO[2] * update + 4.0 * RHO[3] * inverse * (right - (diagonal * value + coupled[...]))
    value = value + update
    mine = jnp.where(parity == 0, value[4:12], value[8:16])
    solid[...] = mine
    for block in range(4):
        cell = dst[8 * block : 8 * block + 8, :]
        tile, lane = cell >> 7, cell & 127
        found = jnp.zeros((8, WIDTH), F32)
        for index in range(TILES):
            row = jnp.broadcast_to(mine[index : index + 1, :], (8, WIDTH))
            found = jnp.where(tile == index, jnp.take_along_axis(row, lane, axis=1, mode="promise_in_bounds"), found)
        for r in range(8):
            returned[8 * block + r] = found[r : r + 1, :]


def stencil_kernel(fluid, liquid, on_chip, across, y_before, y_after, z_before, z_after, base):
    parity = lax.rem(lax.axis_index("gx"), 2)
    near, far = on_chip[56:120, :], across[56:120, :]
    x_before = jnp.where(parity == 0, far, near)
    x_after = jnp.where(parity == 0, near, far)
    row = lax.broadcasted_iota(I32, (64, WIDTH), 0)
    lane = lax.broadcasted_iota(I32, (64, WIDTH), 1)
    for slab in range(16):
        start = 64 * slab
        here = fluid[start : start + 64, :]
        total = (fluid[start - 64 : start, :] if slab else x_before) + (
            fluid[start + 64 : start + 128, :] if slab < 15 else x_after
        )
        total = total + jnp.where(row == 0, y_before[slab : slab + 1, :], pltpu.roll(here, 1, 0))
        total = total + jnp.where(row == 63, y_after[slab : slab + 1, :], pltpu.roll(here, 63, 0))
        half = 64 * (slab % 2)
        left = jnp.broadcast_to(z_before[slab // 2 : slab // 2 + 1, :], (WIDTH, WIDTH)).T[half : half + 64, :]
        right = jnp.broadcast_to(z_after[slab // 2 : slab // 2 + 1, :], (WIDTH, WIDTH)).T[half : half + 64, :]
        total = total + jnp.where(lane == 0, left, pltpu.roll(here, 1, 1))
        total = total + jnp.where(lane == 127, right, pltpu.roll(here, 127, 1))
        total = total - 6.0 * here
        share = liquid[start : start + 64, :].astype(F32)
        base[start : start + 64, :] = (
            here + DIFFUSION * total - EVAPORATION * share * jnp.maximum(here - SATURATION, 0.0)
        )


def final_kernel(base, src, outgoing, returned, fluid_new):
    group = 4
    total = None
    for start in range(0, RUNS, group):
        rows = range(start, start + group)
        ids = lanes([src[r : r + 1, :] for r in rows])
        value = lanes([returned[r] - outgoing[r : r + 1, :] for r in rows])
        placed = placed_parts(ids & 127, WIDTH, value)
        added = lax.dot_general(row_hots(ids >> 7, ROWS), placed, CONTRACT_LAST, preferred_element_type=F32)
        total = added if total is None else total + added
    fluid_new[...] = base[...] + WALL_COUPLING * (total[:, 0:128] + total[:, 128:256])


def shape(*dims):
    return jax.ShapeDtypeStruct(dims, F32)


def call(kernel, outs, scratch, mib, flops, moved):
    return pl.pallas_call(
        kernel,
        out_shape=outs,
        scratch_shapes=scratch,
        compiler_params=params(mib),
        cost_estimate=pl.CostEstimate(flops=flops, bytes_accessed=moved, transcendentals=0),
    )


def per_device(fluid_temp, liquid, face_src, face_dst, solid_old, solid_diag, blocks, pattern):
    parity = lax.rem(lax.axis_index("gx"), 2)
    inside = [(i, i ^ 1) for i in range(RUNS)]
    outside = [(i, (i - 1) % RUNS if i % 2 == 0 else (i + 1) % RUNS) for i in range(RUNS)]
    up = [(i, (i + 1) % 4) for i in range(4)]
    down = [(i, (i - 1) % 4) for i in range(4)]
    fluid = fluid_temp.reshape(ROWS, WIDTH)
    src = face_src.reshape(RUNS, WIDTH)
    dst = face_dst.reshape(RUNS, WIDTH)
    old, diag, own_blocks, present = solid_old[0], solid_diag[0], blocks[0], pattern[0]

    sent, outgoing, on_chip, across, y_faces, z_faces = call(
        pick_kernel,
        (shape(RUNS, 1, 384), shape(RUNS, WIDTH), shape(120, WIDTH), shape(120, WIDTH), shape(2, 16, WIDTH), shape(2, 8, WIDTH)),
        [pltpu.VMEM((256, ROWS), BF16)],
        24, 2 * 256 * 1024 * 4096, 1 << 20,
    )(fluid, src, dst, old, diag, present)

    arrived = lax.all_to_all(sent, "gx", split_axis=0, concat_axis=0, tiled=True)
    partner_blocks = lax.ppermute(own_blocks, "gx", inside)
    edge_blocks = lax.dynamic_slice_in_dim(own_blocks, 6 * parity, 2, axis=0)
    beside_blocks = lax.ppermute(edge_blocks, "gx", outside)
    on_chip = lax.ppermute(on_chip, "gx", inside)
    across = lax.ppermute(across, "gx", outside)

    scratch = [pltpu.VMEM((WIN, WIDTH), F32), pltpu.VMEM((NB, WIN, WIDTH), F32), pltpu.VMEM((WIN, WIDTH), F32)]
    state, pats, swap = call(
        wall_first_kernel,
        (shape(5, WIN, WIDTH), shape(NB, WIN, WIDTH), shape(8, WIDTH)),
        scratch, 24, 1 << 24, 6 << 20,
    )(arrived, dst, old, diag, present, on_chip, across, own_blocks, partner_blocks, beside_blocks)
    swapped = lax.ppermute(swap, "gx", outside)
    solid, sent_back = call(
        wall_second_kernel,
        (shape(TILES, WIDTH), shape(RUNS, 1, WIDTH)),
        scratch, 24, 1 << 24, 6 << 20,
    )(state, pats, swapped, dst, own_blocks, partner_blocks, beside_blocks)
    returned = lax.all_to_all(sent_back, "gx", split_axis=0, concat_axis=0, tiled=True)

    y_before = lax.ppermute(y_faces[1], "gy", up)
    y_after = lax.ppermute(y_faces[0], "gy", down)
    z_before = lax.ppermute(z_faces[1], "gz", up)
    z_after = lax.ppermute(z_faces[0], "gz", down)
    base = call(stencil_kernel, shape(ROWS, WIDTH), [], 24, 1 << 22, 1 << 21)(
        fluid, liquid.reshape(ROWS, WIDTH), on_chip, across, y_before, y_after, z_before, z_after
    )
    fluid_new = call(final_kernel, shape(ROWS, WIDTH), [], 24, 2 * 256 * 1024 * 4096, 1 << 20)(
        base, src, outgoing, returned
    )
    return fluid_new.reshape(fluid_temp.shape), solid[None]


def solution(mesh):
    return jax.shard_map(
        per_device,
        mesh=mesh,
        in_specs=(
            P("gx", "gy", "gz"),
            P("gx", "gy", "gz"),
            P("gx", "gy", "gz", None),
            P("gx", "gy", "gz", None),
            P(("gy", "gz"), "gx", None),
            P(("gy", "gz"), "gx", None),
            P(("gy", "gz"), "gx", None, None, None),
            P(("gy", "gz"), "gx", None),
        ),
        out_specs=(P("gx", "gy", "gz"), P(("gy", "gz"), "gx", None)),
        check_vma=False,
    )
```

```python
import jax
import jax.numpy as jnp
from jax import lax
from jax.experimental import pallas as pl
from jax.experimental.pallas import tpu as pltpu
from jax.sharding import PartitionSpec as P

F32 = jnp.float32
BF16 = jnp.bfloat16
I32 = jnp.int32
RUNS = 32
WIDTH = 128
ROWS = 1024
TILES = 8
NB = 5
WIN = 24
TILE_ROWS = NB * WIDTH
SMALL = 120

DIFFUSION = 0.12
EVAPORATION = 0.5
SATURATION = 0.25
WALL_COUPLING = 0.2

VMEM = pl.BlockSpec(memory_space=pltpu.VMEM)
HBM = pl.BlockSpec(memory_space=pltpu.HBM)
ANY = pl.BlockSpec(memory_space=pl.ANY)


def params(mib):
    return pltpu.CompilerParams(vmem_limit_bytes=mib << 20)


def two_parts(values):
    high = values.astype(BF16)
    return high, (values - high.astype(F32)).astype(BF16)


def lanes(rows):
    return jnp.concatenate(rows, axis=1)


def row_hots(row, count):
    width = row.shape[1]
    part = min(count, 256)
    level = lax.broadcasted_iota(I32, (part, width), 0).astype(F32).astype(BF16)
    one, zero = jnp.ones((), BF16), jnp.zeros((), BF16)
    parts = []
    for index in range(count // part):
        here = jnp.where((row >= index * part) & (row < (index + 1) * part), row - index * part, -1)
        parts.append(jnp.where(level == here.astype(F32).astype(BF16), one, zero))
    return parts[0] if len(parts) == 1 else jnp.concatenate(parts, axis=0)


def placed_parts(column, count, values):
    width = column.shape[1]
    mask = lax.broadcasted_iota(I32, (count, width), 0) == column
    high = values.astype(BF16).astype(F32)
    low = values - high
    both = [jnp.where(mask, part, 0.0) for part in (high, low)]
    return jnp.concatenate(both, axis=0).astype(BF16)


CONTRACT_LAST = (((1,), (1,)), ((), ()))


def pick_kernel(
    fluid_hbm, src_hbm, dst_hbm, old_hbm, diag_hbm, pattern_hbm, blocks_hbm,
    sent, outgoing, own, y_faces, z_faces, on_chip_hbm, across_hbm,
    fluid, src, dst, pattern, table, packed, sems,
):
    me = lax.axis_index("gx")
    parity = lax.rem(me, 2)

    def copy(source, target, index):
        started = pltpu.make_async_copy(source, target, sems.at[index])
        started.start()
        return started

    loads = [copy(fluid_hbm.at[128 * i : 128 * i + 128], fluid.at[128 * i : 128 * i + 128], i) for i in range(8)]
    load_src = copy(src_hbm, src, 8)
    small = [
        copy(dst_hbm, dst, 9),
        copy(old_hbm, own.at[32:40], 10),
        copy(diag_hbm, own.at[40:48], 11),
        copy(pattern_hbm, pattern, 16),
    ]
    inside = copy(blocks_hbm.at[pl.ds((1 - parity) * 2 * TILE_ROWS, 6 * TILE_ROWS)], on_chip_hbm.at[0 : 6 * TILE_ROWS], 12)
    outside = copy(blocks_hbm.at[pl.ds(parity * 6 * TILE_ROWS, 2 * TILE_ROWS)], across_hbm.at[0 : 2 * TILE_ROWS], 13)
    for block in range(8):
        loads[block].wait()
        turned = fluid[128 * block : 128 * block + 128, :].T
        high, low = two_parts(turned)
        table[0:128, 128 * block : 128 * block + 128] = high
        table[128:256, 128 * block : 128 * block + 128] = low
        z_faces[0, block : block + 1, :] = turned[0:1, :]
        z_faces[1, block : block + 1, :] = turned[127:128, :]
    load_src.wait()
    group = 4
    for start in range(0, RUNS, group):
        ids = lanes([src[r : r + 1, :] for r in range(start, start + group)])
        picked = jnp.dot(table[...], row_hots(ids >> 7, ROWS), preferred_element_type=F32)
        both = picked[0:128] + picked[128:256]
        mask = lax.broadcasted_iota(I32, (WIDTH, group * WIDTH), 0) == (ids & 127)
        value = jnp.sum(jnp.where(mask, both, 0.0), axis=0, keepdims=True)
        for r in range(start, start + group):
            mine = value[:, (r - start) * WIDTH : (r - start + 1) * WIDTH]
            outgoing[r : r + 1, :] = mine
            sent[r, :, 0:128] = mine
            sent[r ^ 1, :, 128:256] = mine
            beside = (r + 1) % RUNS if r % 2 else (r - 1) % RUNS
            sent[beside, :, 256:384] = mine
    for slab in range(16):
        y_faces[0, slab : slab + 1, :] = fluid[64 * slab : 64 * slab + 1, :]
        y_faces[1, slab : slab + 1, :] = fluid[64 * slab + 63 : 64 * slab + 64, :]
    for each in small:
        each.wait()
    own[0:32, :] = dst[...].astype(F32)
    own[48:56, :] = jnp.zeros((8, WIDTH), F32)
    for offset in range(NB):
        own[48 + offset : 49 + offset, 0:TILES] = pattern[offset].astype(F32)
    first, last = fluid[0:64, :], fluid[960:1024, :]
    for index, face in ((0, jnp.where(parity == 0, last, first)), (1, jnp.where(parity == 0, first, last))):
        packed[index, 0:56, :] = own[...]
        packed[index, 56:120, :] = face
    tail_in = copy(packed.at[0], on_chip_hbm.at[6 * TILE_ROWS : 6 * TILE_ROWS + SMALL], 14)
    tail_out = copy(packed.at[1], across_hbm.at[2 * TILE_ROWS : 2 * TILE_ROWS + SMALL], 15)
    for each in (inside, outside, tail_in, tail_out):
        each.wait()


def spread_run(ids_of, values_of):
    group = 8
    total = None
    for start in range(0, RUNS, group):
        cell = lanes([ids_of(r) for r in range(start, start + group)])
        value = lanes([values_of(r) for r in range(start, start + group)])
        row = jnp.where(cell >= 0, ((cell >> 5) & 3) * 8 + (cell >> 7), -1)
        hots = row_hots(row, 32)
        placed = placed_parts(cell & 31, 32, value)
        added = lax.dot_general(hots, placed, CONTRACT_LAST, preferred_element_type=F32)
        total = added if total is None else total + added
    total = total[:, 0:32] + total[:, 32:64]
    return lanes([total[8 * u : 8 * u + 8, :] for u in range(4)])


def window(parity, own, partner, beside):
    pad = jnp.zeros((4, own.shape[1]), F32)
    low = jnp.concatenate([beside[4:8], own, partner, pad], axis=0)
    high = jnp.concatenate([partner, own, beside[0:4], pad], axis=0)
    return jnp.where(parity == 0, low, high)


def neighbours(iterate, pats, first, count, shifted):
    for offset in range(NB):
        values = iterate[first - 2 + offset : first - 2 + offset + count, :]
        shifted[offset, first : first + count, :] = values * pats[offset, first : first + count, :]


def apply_tile(blocks, tile, shifted, place, coupled):
    total = None
    for offset in range(NB):
        start = pl.multiple_of(tile * TILE_ROWS + offset * WIDTH, WIDTH)
        term = blocks[pl.ds(start, WIDTH), :] * shifted[offset, pl.ds(place, 1), :]
        total = term if total is None else total + term
    coupled[pl.ds(place, 1), :] = jnp.sum(total.T, axis=0, keepdims=True)


RHO = [0.5]
for _ in range(3):
    RHO.append(1.0 / (4.0 - RHO[-1]))


def stepped(sweep, value, update, right, inverse, diagonal, coupled):
    residual = right - (diagonal * value + coupled)
    if sweep == 0:
        update = inverse * residual
    else:
        update = RHO[sweep] * RHO[sweep - 1] * update + 4.0 * RHO[sweep] * inverse * residual
    return value + update, update


def own_run_kernel(arrived, own, added):
    added[...] = spread_run(lambda r: own[r : r + 1, :].astype(I32), lambda r: arrived[r, :, 0:128])


def beside_run_kernel(arrived, across_hbm, added_own, added, small, sem):
    load = pltpu.make_async_copy(across_hbm.at[2 * TILE_ROWS : 2 * TILE_ROWS + SMALL], small, sem)
    load.start()
    added[0:TILES, :] = added_own[...]
    load.wait()
    added[TILES : 2 * TILES, :] = spread_run(
        lambda r: small[r : r + 1, :].astype(I32), lambda r: arrived[r, :, 256:384]
    )


def wall_first_kernel(
    arrived, added_before, beside_small, own, own_blocks, on_chip_hbm, across_hbm, y_before, y_after,
    state, pats, swap, faces, y_faces,
    inner, outer, iterate, shifted, coupled, sems,
):
    me = lax.axis_index("gx")
    parity = lax.rem(me, 2)
    keep = jnp.where((me == 0) | (me == RUNS - 1), 0.0, 1.0)
    loads = []
    at_in = 6 * TILE_ROWS
    for index, (source, target, low, high) in enumerate((
        (on_chip_hbm, inner, at_in, at_in + SMALL),
        (on_chip_hbm, inner, 0, at_in),
        (across_hbm, outer, 0, 2 * TILE_ROWS),
    )):
        loads.append(pltpu.make_async_copy(source.at[low:high], target.at[low:high], sems.at[index]))
        loads[-1].start()
    loads[0].wait()
    partner, beside = inner[at_in : at_in + SMALL, :], beside_small[...]
    added = [
        added_before[0:TILES, :],
        spread_run(lambda r: inner[at_in + r : at_in + r + 1, :].astype(I32), lambda r: arrived[r, :, 128:256]),
        added_before[TILES : 2 * TILES, :],
    ]
    holders = [own[...], partner, beside]
    diagonals = [each[40:48] for each in holders]
    rights = [d * each[32:40] + a for d, each, a in zip(diagonals, holders, added)]
    inverses = [1.0 / d for d in diagonals]
    rights[2], inverses[2] = rights[2] * keep, inverses[2] * keep
    present = window(parity, *[each[48:56].T[0:TILES] for each in holders])
    for offset in range(NB):
        pats[offset] = jnp.broadcast_to(present[:, offset : offset + 1], (WIN, WIDTH))
    right = window(parity, *rights)
    inverse = window(parity, *inverses)
    diagonal = window(parity, *diagonals)
    y_faces[0], y_faces[1] = y_before[...], y_after[...]
    faces[0] = jnp.where(parity == 0, beside[56:120], partner[56:120])
    faces[1] = jnp.where(parity == 0, partner[56:120], beside[56:120])
    value = inverse * right
    iterate[...] = value
    shifted[...] = jnp.zeros((NB, WIN, WIDTH), F32)
    coupled[...] = jnp.zeros((WIN, WIDTH), F32)
    own_at = 4 + 4 * parity

    neighbours(iterate, pats, 2, 16, shifted)
    for tile in range(TILES):
        apply_tile(own_blocks, tile, shifted, own_at + tile, coupled)
    loads[1].wait()
    loads[2].wait()
    for tile in range(6):
        apply_tile(inner, tile, shifted, 12 - 10 * parity + tile, coupled)
    for tile in range(2):
        apply_tile(outer, tile, shifted, 2 + 14 * parity + tile, coupled)
    value, update = stepped(0, value, None, right, inverse, diagonal, coupled[...])
    iterate[...] = value

    neighbours(iterate, pats, 4, 12, shifted)
    for tile in range(TILES):
        apply_tile(own_blocks, tile, shifted, own_at + tile, coupled)
    for tile in range(4):
        apply_tile(inner, tile + 2 * parity, shifted, 12 - 8 * parity + tile, coupled)
    value, update = stepped(1, value, update, right, inverse, diagonal, coupled[...])
    state[0], state[1], state[2], state[3], state[4] = value, update, right, inverse, diagonal
    swap[0:4, :] = jnp.where(parity == 0, value[4:8], value[12:16])
    swap[4:8, :] = jnp.where(parity == 0, update[4:8], update[12:16])


def wall_inner_kernel(state, pats, own_blocks, on_chip_hbm, inside, inner, iterate, shifted, coupled, sem):
    parity = lax.rem(lax.axis_index("gx"), 2)
    load = pltpu.make_async_copy(on_chip_hbm.at[pl.ds(parity * 4 * TILE_ROWS, 2 * TILE_ROWS)], inner, sem)
    load.start()
    value, update, right, inverse, diagonal = (state[i] for i in range(5))
    iterate[...] = value
    shifted[...] = jnp.zeros((NB, WIN, WIDTH), F32)
    coupled[...] = jnp.zeros((WIN, WIDTH), F32)
    own_at = 4 + 4 * parity
    neighbours(iterate, pats, 6, 8, shifted)
    for index in range(6):
        tile = index + 2 - 2 * parity
        apply_tile(own_blocks, tile, shifted, own_at + tile, coupled)
    load.wait()
    for index in range(2):
        apply_tile(inner, index, shifted, 12 - 6 * parity + index, coupled)
    value, update = stepped(2, value, update, right, inverse, diagonal, coupled[...])
    inside[0], inside[1] = value, update
    iterate[...] = value
    neighbours(iterate, pats, 8, 4, shifted)
    for index in range(4):
        tile = index + 4 - 4 * parity
        apply_tile(own_blocks, tile, shifted, own_at + tile, coupled)
    inside[2] = coupled[...]


def wall_last_kernel(
    state, pats, inside, swapped, own, own_blocks, across_hbm,
    solid, returned, outer, iterate, shifted, coupled, sem,
):
    load = pltpu.make_async_copy(across_hbm.at[0 : 2 * TILE_ROWS], outer, sem)
    load.start()
    me = lax.axis_index("gx")
    parity = lax.rem(me, 2)
    keep = jnp.where((me == 0) | (me == RUNS - 1), 0.0, 1.0)
    value, update, right, inverse, diagonal = (state[i] for i in range(5))

    def with_swapped(inside, outside):
        low = jnp.concatenate([outside, inside[4:24]], axis=0)
        high = jnp.concatenate([inside[0:16], outside, inside[20:24]], axis=0)
        return jnp.where(parity == 0, low, high)

    value = with_swapped(value, swapped[0:4, :] * keep)
    update = with_swapped(update, swapped[4:8, :] * keep)
    place = lax.broadcasted_iota(I32, (WIN, WIDTH), 0)
    own_at = 4 + 4 * parity
    iterate[...] = value
    shifted[...] = jnp.zeros((NB, WIN, WIDTH), F32)
    coupled[...] = jnp.zeros((WIN, WIDTH), F32)
    neighbours(iterate, pats, 2, 16, shifted)
    for index in range(2):
        tile = index + 6 * parity
        apply_tile(own_blocks, tile, shifted, own_at + tile, coupled)
    load.wait()
    for index in range(2):
        apply_tile(outer, index, shifted, 2 + 14 * parity + index, coupled)
    value, update = stepped(2, value, update, right, inverse, diagonal, coupled[...])
    known = (place >= 6) & (place < 14)
    value, update = jnp.where(known, inside[0], value), jnp.where(known, inside[1], update)
    iterate[...] = value
    neighbours(iterate, pats, 4, 12, shifted)
    for index in range(4):
        tile = index + 4 * parity
        apply_tile(own_blocks, tile, shifted, own_at + tile, coupled)
    product = jnp.where((place >= 8) & (place < 12), inside[2], coupled[...])
    value, update = stepped(3, value, update, right, inverse, diagonal, product)
    mine = jnp.where(parity == 0, value[4:12], value[8:16])
    solid[...] = mine
    for block in range(4):
        cell = own[8 * block : 8 * block + 8, :].astype(I32)
        tile, lane = cell >> 7, cell & 127
        found = jnp.zeros((8, WIDTH), F32)
        for index in range(TILES):
            row = jnp.broadcast_to(mine[index : index + 1, :], (8, WIDTH))
            found = jnp.where(tile == index, jnp.take_along_axis(row, lane, axis=1, mode="promise_in_bounds"), found)
        for r in range(8):
            returned[8 * block + r] = found[r : r + 1, :]


def stencil_kernel(fluid_hbm, liquid_hbm, x_faces, y_faces, z_before, z_after, base, fluid, liquid, sems):
    loads = [
        pltpu.make_async_copy(fluid_hbm, fluid, sems.at[0]),
        pltpu.make_async_copy(liquid_hbm, liquid, sems.at[1]),
    ]
    for each in loads:
        each.start()
    row = lax.broadcasted_iota(I32, (64, WIDTH), 0)
    lane = lax.broadcasted_iota(I32, (64, WIDTH), 1)
    for each in loads:
        each.wait()
    for slab in range(16):
        start = 64 * slab
        block = slab // 2
        here = fluid[start : start + 64, :]
        total = (fluid[start - 64 : start, :] if slab else x_faces[0]) + (
            fluid[start + 64 : start + 128, :] if slab < 15 else x_faces[1]
        )
        total = total + jnp.where(row == 0, y_faces[0, slab : slab + 1, :], pltpu.roll(here, 1, 0))
        total = total + jnp.where(row == 63, y_faces[1, slab : slab + 1, :], pltpu.roll(here, 63, 0))
        half = 64 * (slab % 2)
        left = jnp.broadcast_to(z_before[block : block + 1, :], (WIDTH, WIDTH)).T[half : half + 64, :]
        right = jnp.broadcast_to(z_after[block : block + 1, :], (WIDTH, WIDTH)).T[half : half + 64, :]
        total = total + jnp.where(lane == 0, left, pltpu.roll(here, 1, 1))
        total = total + jnp.where(lane == 127, right, pltpu.roll(here, 127, 1))
        total = total - 6.0 * here
        share = liquid[start : start + 64, :].astype(F32)
        base[start : start + 64, :] = (
            here + DIFFUSION * total - EVAPORATION * share * jnp.maximum(here - SATURATION, 0.0)
        )


def final_kernel(base, src, outgoing, returned, fluid_new):
    group = 4
    total = None
    for start in range(0, RUNS, group):
        rows = range(start, start + group)
        ids = lanes([src[r : r + 1, :] for r in rows])
        value = lanes([returned[r] - outgoing[r : r + 1, :] for r in rows])
        placed = placed_parts(ids & 127, WIDTH, value)
        added = lax.dot_general(row_hots(ids >> 7, ROWS), placed, CONTRACT_LAST, preferred_element_type=F32)
        total = added if total is None else total + added
    fluid_new[...] = base[...] + WALL_COUPLING * (total[:, 0:128] + total[:, 128:256])


def shape(*dims):
    return jax.ShapeDtypeStruct(dims, F32)


def call(kernel, mib, ins, outs, out_specs, scratch, flops, moved):
    return pl.pallas_call(
        kernel,
        in_specs=ins,
        out_shape=outs,
        out_specs=out_specs,
        scratch_shapes=scratch,
        compiler_params=params(mib),
        cost_estimate=pl.CostEstimate(flops=flops, bytes_accessed=moved, transcendentals=0),
    )


def vmem(*dims, kind=F32):
    return pltpu.VMEM(dims, kind)


def dma(*dims):
    return pltpu.SemaphoreType.DMA(dims) if dims else pltpu.SemaphoreType.DMA


def per_device(fluid_temp, liquid, face_src, face_dst, solid_old, solid_diag, blocks, pattern):
    inside_pairs = [(i, i ^ 1) for i in range(RUNS)]
    outside_pairs = [(i, (i - 1) % RUNS if i % 2 == 0 else (i + 1) % RUNS) for i in range(RUNS)]
    fluid = fluid_temp.reshape(ROWS, WIDTH)
    src = face_src.reshape(RUNS, WIDTH)
    dst = face_dst.reshape(RUNS, WIDTH)
    own_blocks = blocks.reshape(TILES * TILE_ROWS, WIDTH)
    in_rows, out_rows = 6 * TILE_ROWS + SMALL, 2 * TILE_ROWS + SMALL

    sent, outgoing, own, y_faces, z_faces, on_chip, across = call(
        pick_kernel, 60,
        [HBM] * 7,
        (
            shape(RUNS, 1, 384), shape(RUNS, WIDTH), shape(56, WIDTH), shape(2, 16, WIDTH), shape(2, 8, WIDTH),
            shape(in_rows, WIDTH), shape(out_rows, WIDTH),
        ),
        (VMEM, VMEM, VMEM, VMEM, VMEM, HBM, HBM),
        [
            vmem(ROWS, WIDTH), vmem(RUNS, WIDTH, kind=I32), vmem(RUNS, WIDTH, kind=I32), vmem(NB, 1, TILES, kind=I32),
            vmem(256, ROWS, kind=BF16), vmem(2, SMALL, WIDTH), dma(17),
        ],
        2 * 256 * 1024 * 4096, 1 << 22,
    )(fluid, src, dst, solid_old[0], solid_diag[0], jnp.transpose(pattern, (2, 0, 1)), own_blocks)

    arrived = lax.all_to_all(sent, "gx", split_axis=0, concat_axis=0, tiled=True)
    on_chip = lax.ppermute(on_chip, "gx", inside_pairs)
    across = lax.ppermute(across, "gx", outside_pairs)
    up = [(i, (i + 1) % 4) for i in range(4)]
    down = [(i, (i - 1) % 4) for i in range(4)]
    y_before = lax.ppermute(y_faces[1], "gy", up)
    y_after = lax.ppermute(y_faces[0], "gy", down)

    work = [vmem(WIN, WIDTH), vmem(NB, WIN, WIDTH), vmem(WIN, WIDTH)]
    added_own = call(
        own_run_kernel, 12, [VMEM, VMEM], shape(TILES, WIDTH), VMEM, [], 65 * 10**8, 1 << 16
    )(arrived, own)
    added_before, beside_small = call(
        beside_run_kernel, 12, [VMEM, ANY, VMEM], (shape(2 * TILES, WIDTH), shape(SMALL, WIDTH)), (VMEM, VMEM), [dma()],
        14 * 10**9, 1 << 16,
    )(arrived, across, added_own)
    state, pats, swap, x_faces, y_faces = call(
        wall_first_kernel, 16,
        [VMEM, VMEM, VMEM, VMEM, VMEM, ANY, ANY, VMEM, VMEM],
        (shape(5, WIN, WIDTH), shape(NB, WIN, WIDTH), shape(8, WIDTH), shape(2, 64, WIDTH), shape(2, 16, WIDTH)),
        (VMEM,) * 5,
        [vmem(in_rows, WIDTH), vmem(2 * TILE_ROWS, WIDTH)] + work + [dma(3)],
        1 << 24, 6 << 20,
    )(arrived, added_before, beside_small, own, own_blocks, on_chip, across, y_before, y_after)
    swapped = lax.ppermute(swap, "gx", outside_pairs)
    inside = call(
        wall_inner_kernel, 12,
        [VMEM, VMEM, VMEM, ANY],
        shape(3, WIN, WIDTH), VMEM,
        [vmem(2 * TILE_ROWS, WIDTH)] + work + [dma()],
        1 << 22, 3 << 20,
    )(state, pats, own_blocks, on_chip)
    solid, sent_back = call(
        wall_last_kernel, 12,
        [VMEM] * 6 + [ANY],
        (shape(TILES, WIDTH), shape(RUNS, 1, WIDTH)), (VMEM, VMEM),
        [vmem(2 * TILE_ROWS, WIDTH)] + work + [dma()],
        1 << 23, 3 << 20,
    )(state, pats, inside, swapped, own, own_blocks, across)
    sent_back, z_faces = lax.optimization_barrier((sent_back, z_faces))
    z_before = lax.ppermute(z_faces[1], "gz", up)
    z_after = lax.ppermute(z_faces[0], "gz", down)
    returned = lax.all_to_all(sent_back, "gx", split_axis=0, concat_axis=0, tiled=True)

    base = call(
        stencil_kernel, 12,
        [HBM, HBM, VMEM, VMEM, VMEM, VMEM],
        shape(ROWS, WIDTH), VMEM,
        [vmem(ROWS, WIDTH), vmem(ROWS, WIDTH, kind=I32), dma(2)],
        1 << 22, 1 << 21,
    )(fluid, liquid.reshape(ROWS, WIDTH), x_faces, y_faces, z_before, z_after)
    fluid_new = call(
        final_kernel, 16, [VMEM] * 4, shape(ROWS, WIDTH), VMEM, [], 2 * 256 * 1024 * 4096, 1 << 20
    )(base, src, outgoing, returned)
    return fluid_new.reshape(fluid_temp.shape), solid[None]


def solution(mesh):
    return jax.shard_map(
        per_device,
        mesh=mesh,
        in_specs=(
            P("gx", "gy", "gz"),
            P("gx", "gy", "gz"),
            P("gx", "gy", "gz", None),
            P("gx", "gy", "gz", None),
            P(("gy", "gz"), "gx", None),
            P(("gy", "gz"), "gx", None),
            P(("gy", "gz"), "gx", None, None, None),
            P(("gy", "gz"), "gx", None),
        ),
        out_specs=(P("gx", "gy", "gz"), P(("gy", "gz"), "gx", None)),
        check_vma=False,
    )
```

```python
import jax
import jax.numpy as jnp
from jax import lax
from jax.experimental import pallas as pl
from jax.experimental.pallas import tpu as pltpu
from jax.sharding import PartitionSpec as P

F32 = jnp.float32
BF16 = jnp.bfloat16
I32 = jnp.int32
RUNS = 32
WIDTH = 128
ROWS = 1024
TILES = 8
NB = 5
WIN = 24
TILE_ROWS = NB * WIDTH
SMALL = 120

DIFFUSION = 0.12
EVAPORATION = 0.5
SATURATION = 0.25
WALL_COUPLING = 0.2

VMEM = pl.BlockSpec(memory_space=pltpu.VMEM)
HBM = pl.BlockSpec(memory_space=pltpu.HBM)
ANY = pl.BlockSpec(memory_space=pl.ANY)


def params(mib):
    return pltpu.CompilerParams(vmem_limit_bytes=mib << 20)


def two_parts(values):
    high = values.astype(BF16)
    return high, (values - high.astype(F32)).astype(BF16)


def lanes(rows):
    return jnp.concatenate(rows, axis=1)


def row_hots(row, count):
    width = row.shape[1]
    part = min(count, 256)
    level = lax.broadcasted_iota(I32, (part, width), 0).astype(F32).astype(BF16)
    one, zero = jnp.ones((), BF16), jnp.zeros((), BF16)
    parts = []
    for index in range(count // part):
        here = jnp.where((row >= index * part) & (row < (index + 1) * part), row - index * part, -1)
        parts.append(jnp.where(level == here.astype(F32).astype(BF16), one, zero))
    return parts[0] if len(parts) == 1 else jnp.concatenate(parts, axis=0)


def placed_parts(column, count, values):
    width = column.shape[1]
    mask = lax.broadcasted_iota(I32, (count, width), 0) == column
    high = values.astype(BF16).astype(F32)
    low = values - high
    both = [jnp.where(mask, part, 0.0) for part in (high, low)]
    return jnp.concatenate(both, axis=0).astype(BF16)


CONTRACT_LAST = (((1,), (1,)), ((), ()))


def pick_kernel(
    fluid_hbm, src_hbm, dst_hbm, old_hbm, diag_hbm, pattern_hbm, blocks_hbm,
    sent, outgoing, own, y_faces, z_faces, on_chip_hbm, across_hbm,
    fluid, src, dst, pattern, table, packed, staged_in, staged_out, sems,
):
    me = lax.axis_index("gx")
    parity = lax.rem(me, 2)

    def copy(source, target, index):
        started = pltpu.make_async_copy(source, target, sems.at[index])
        started.start()
        return started

    loads = [copy(fluid_hbm.at[128 * i : 128 * i + 128], fluid.at[128 * i : 128 * i + 128], i) for i in range(8)]
    load_src = copy(src_hbm, src, 8)
    small = [
        copy(dst_hbm, dst, 9),
        copy(old_hbm, own.at[32:40], 10),
        copy(diag_hbm, own.at[40:48], 11),
        copy(pattern_hbm, pattern, 16),
    ]
    inside = copy(blocks_hbm.at[pl.ds((1 - parity) * 2 * TILE_ROWS, 6 * TILE_ROWS)], staged_in, 12)
    outside = copy(blocks_hbm.at[pl.ds(parity * 6 * TILE_ROWS, 2 * TILE_ROWS)], staged_out, 13)
    for block in range(8):
        loads[block].wait()
        turned = fluid[128 * block : 128 * block + 128, :].T
        high, low = two_parts(turned)
        table[0:128, 128 * block : 128 * block + 128] = high
        table[128:256, 128 * block : 128 * block + 128] = low
        z_faces[0, block : block + 1, :] = turned[0:1, :]
        z_faces[1, block : block + 1, :] = turned[127:128, :]
    load_src.wait()
    group = 4
    for start in range(0, RUNS, group):
        if start == RUNS // 2:
            inside.wait()
            outside.wait()
            inside = copy(staged_in, on_chip_hbm.at[0 : 6 * TILE_ROWS], 17)
            outside = copy(staged_out, across_hbm.at[0 : 2 * TILE_ROWS], 18)
        ids = lanes([src[r : r + 1, :] for r in range(start, start + group)])
        picked = jnp.dot(table[...], row_hots(ids >> 7, ROWS), preferred_element_type=F32)
        both = picked[0:128] + picked[128:256]
        mask = lax.broadcasted_iota(I32, (WIDTH, group * WIDTH), 0) == (ids & 127)
        value = jnp.sum(jnp.where(mask, both, 0.0), axis=0, keepdims=True)
        for r in range(start, start + group):
            mine = value[:, (r - start) * WIDTH : (r - start + 1) * WIDTH]
            outgoing[r : r + 1, :] = mine
            sent[r, :, 0:128] = mine
            sent[r ^ 1, :, 128:256] = mine
            beside = (r + 1) % RUNS if r % 2 else (r - 1) % RUNS
            sent[beside, :, 256:384] = mine
    for slab in range(16):
        y_faces[0, slab : slab + 1, :] = fluid[64 * slab : 64 * slab + 1, :]
        y_faces[1, slab : slab + 1, :] = fluid[64 * slab + 63 : 64 * slab + 64, :]
    for each in small:
        each.wait()
    own[0:32, :] = dst[...].astype(F32)
    own[48:56, :] = jnp.zeros((8, WIDTH), F32)
    for offset in range(NB):
        own[48 + offset : 49 + offset, 0:TILES] = pattern[offset].astype(F32)
    first, last = fluid[0:64, :], fluid[960:1024, :]
    for index, face in ((0, jnp.where(parity == 0, last, first)), (1, jnp.where(parity == 0, first, last))):
        packed[index, 0:56, :] = own[...]
        packed[index, 56:120, :] = face
    tail_in = copy(packed.at[0], on_chip_hbm.at[6 * TILE_ROWS : 6 * TILE_ROWS + SMALL], 14)
    tail_out = copy(packed.at[1], across_hbm.at[2 * TILE_ROWS : 2 * TILE_ROWS + SMALL], 15)
    for each in (inside, outside, tail_in, tail_out):
        each.wait()


def spread_run(ids_of, values_of):
    group = 8
    total = None
    for start in range(0, RUNS, group):
        cell = lanes([ids_of(r) for r in range(start, start + group)])
        value = lanes([values_of(r) for r in range(start, start + group)])
        row = jnp.where(cell >= 0, ((cell >> 5) & 3) * 8 + (cell >> 7), -1)
        hots = row_hots(row, 32)
        placed = placed_parts(cell & 31, 32, value)
        added = lax.dot_general(hots, placed, CONTRACT_LAST, preferred_element_type=F32)
        total = added if total is None else total + added
    total = total[:, 0:32] + total[:, 32:64]
    return lanes([total[8 * u : 8 * u + 8, :] for u in range(4)])


def window(parity, own, partner, beside):
    pad = jnp.zeros((4, own.shape[1]), F32)
    low = jnp.concatenate([beside[4:8], own, partner, pad], axis=0)
    high = jnp.concatenate([partner, own, beside[0:4], pad], axis=0)
    return jnp.where(parity == 0, low, high)


def neighbours(iterate, pats, first, count, shifted):
    for offset in range(NB):
        values = iterate[first - 2 + offset : first - 2 + offset + count, :]
        shifted[offset, first : first + count, :] = values * pats[offset, first : first + count, :]


def apply_tile(blocks, tile, shifted, place, coupled):
    total = None
    for offset in range(NB):
        start = pl.multiple_of(tile * TILE_ROWS + offset * WIDTH, WIDTH)
        term = blocks[pl.ds(start, WIDTH), :] * shifted[offset, pl.ds(place, 1), :]
        total = term if total is None else total + term
    coupled[pl.ds(place, 1), :] = jnp.sum(total.T, axis=0, keepdims=True)


RHO = [0.5]
for _ in range(3):
    RHO.append(1.0 / (4.0 - RHO[-1]))


def stepped(sweep, value, update, right, inverse, diagonal, coupled):
    residual = right - (diagonal * value + coupled)
    if sweep == 0:
        update = inverse * residual
    else:
        update = RHO[sweep] * RHO[sweep - 1] * update + 4.0 * RHO[sweep] * inverse * residual
    return value + update, update


def own_run_kernel(arrived, own, added):
    added[...] = spread_run(lambda r: own[r : r + 1, :].astype(I32), lambda r: arrived[r, :, 0:128])


def beside_run_kernel(arrived, across_hbm, added_own, added, small, sem):
    load = pltpu.make_async_copy(across_hbm.at[2 * TILE_ROWS : 2 * TILE_ROWS + SMALL], small, sem)
    load.start()
    added[0:TILES, :] = added_own[...]
    load.wait()
    added[TILES : 2 * TILES, :] = spread_run(
        lambda r: small[r : r + 1, :].astype(I32), lambda r: arrived[r, :, 256:384]
    )


def wall_first_kernel(
    arrived, added_before, beside_small, own, own_blocks, on_chip_hbm, across_hbm, y_before, y_after,
    state, pats, swap, faces, y_faces,
    inner, outer, iterate, shifted, coupled, sems,
):
    me = lax.axis_index("gx")
    parity = lax.rem(me, 2)
    keep = jnp.where((me == 0) | (me == RUNS - 1), 0.0, 1.0)
    loads = []
    at_in = 6 * TILE_ROWS
    for index, (source, target, low, high) in enumerate((
        (on_chip_hbm, inner, at_in, at_in + SMALL),
        (on_chip_hbm, inner, 0, at_in),
        (across_hbm, outer, 0, 2 * TILE_ROWS),
    )):
        loads.append(pltpu.make_async_copy(source.at[low:high], target.at[low:high], sems.at[index]))
        loads[-1].start()
    loads[0].wait()
    partner, beside = inner[at_in : at_in + SMALL, :], beside_small[...]
    added = [
        added_before[0:TILES, :],
        spread_run(lambda r: inner[at_in + r : at_in + r + 1, :].astype(I32), lambda r: arrived[r, :, 128:256]),
        added_before[TILES : 2 * TILES, :],
    ]
    holders = [own[...], partner, beside]
    diagonals = [each[40:48] for each in holders]
    rights = [d * each[32:40] + a for d, each, a in zip(diagonals, holders, added)]
    inverses = [1.0 / d for d in diagonals]
    rights[2], inverses[2] = rights[2] * keep, inverses[2] * keep
    present = window(parity, *[each[48:56].T[0:TILES] for each in holders])
    for offset in range(NB):
        pats[offset] = jnp.broadcast_to(present[:, offset : offset + 1], (WIN, WIDTH))
    right = window(parity, *rights)
    inverse = window(parity, *inverses)
    diagonal = window(parity, *diagonals)
    y_faces[0], y_faces[1] = y_before[...], y_after[...]
    faces[0] = jnp.where(parity == 0, beside[56:120], partner[56:120])
    faces[1] = jnp.where(parity == 0, partner[56:120], beside[56:120])
    value = inverse * right
    iterate[...] = value
    shifted[...] = jnp.zeros((NB, WIN, WIDTH), F32)
    coupled[...] = jnp.zeros((WIN, WIDTH), F32)
    own_at = 4 + 4 * parity

    neighbours(iterate, pats, 2, 16, shifted)
    for tile in range(TILES):
        apply_tile(own_blocks, tile, shifted, own_at + tile, coupled)
    loads[1].wait()
    loads[2].wait()
    for tile in range(6):
        apply_tile(inner, tile, shifted, 12 - 10 * parity + tile, coupled)
    for tile in range(2):
        apply_tile(outer, tile, shifted, 2 + 14 * parity + tile, coupled)
    value, update = stepped(0, value, None, right, inverse, diagonal, coupled[...])
    iterate[...] = value

    neighbours(iterate, pats, 4, 12, shifted)
    for tile in range(TILES):
        apply_tile(own_blocks, tile, shifted, own_at + tile, coupled)
    for tile in range(4):
        apply_tile(inner, tile + 2 * parity, shifted, 12 - 8 * parity + tile, coupled)
    value, update = stepped(1, value, update, right, inverse, diagonal, coupled[...])
    state[0], state[1], state[2], state[3], state[4] = value, update, right, inverse, diagonal
    swap[0:4, :] = jnp.where(parity == 0, value[4:8], value[12:16])
    swap[4:8, :] = jnp.where(parity == 0, update[4:8], update[12:16])


def wall_inner_kernel(state, pats, own_blocks, on_chip_hbm, inside, inner, iterate, shifted, coupled, sem):
    parity = lax.rem(lax.axis_index("gx"), 2)
    load = pltpu.make_async_copy(on_chip_hbm.at[pl.ds(parity * 4 * TILE_ROWS, 2 * TILE_ROWS)], inner, sem)
    load.start()
    value, update, right, inverse, diagonal = (state[i] for i in range(5))
    iterate[...] = value
    shifted[...] = jnp.zeros((NB, WIN, WIDTH), F32)
    coupled[...] = jnp.zeros((WIN, WIDTH), F32)
    own_at = 4 + 4 * parity
    neighbours(iterate, pats, 6, 8, shifted)
    for index in range(6):
        tile = index + 2 - 2 * parity
        apply_tile(own_blocks, tile, shifted, own_at + tile, coupled)
    load.wait()
    for index in range(2):
        apply_tile(inner, index, shifted, 12 - 6 * parity + index, coupled)
    value, update = stepped(2, value, update, right, inverse, diagonal, coupled[...])
    inside[0], inside[1] = value, update
    iterate[...] = value
    neighbours(iterate, pats, 8, 4, shifted)
    for index in range(4):
        tile = index + 4 - 4 * parity
        apply_tile(own_blocks, tile, shifted, own_at + tile, coupled)
    inside[2] = coupled[...]


def wall_last_kernel(
    state, pats, inside, swapped, own, own_blocks, across_hbm,
    solid, returned, outer, iterate, shifted, coupled, sem,
):
    load = pltpu.make_async_copy(across_hbm.at[0 : 2 * TILE_ROWS], outer, sem)
    load.start()
    me = lax.axis_index("gx")
    parity = lax.rem(me, 2)
    keep = jnp.where((me == 0) | (me == RUNS - 1), 0.0, 1.0)
    value, update, right, inverse, diagonal = (state[i] for i in range(5))

    def with_swapped(inside, outside):
        low = jnp.concatenate([outside, inside[4:24]], axis=0)
        high = jnp.concatenate([inside[0:16], outside, inside[20:24]], axis=0)
        return jnp.where(parity == 0, low, high)

    value = with_swapped(value, swapped[0:4, :] * keep)
    update = with_swapped(update, swapped[4:8, :] * keep)
    place = lax.broadcasted_iota(I32, (WIN, WIDTH), 0)
    own_at = 4 + 4 * parity
    iterate[...] = value
    shifted[...] = jnp.zeros((NB, WIN, WIDTH), F32)
    coupled[...] = jnp.zeros((WIN, WIDTH), F32)
    neighbours(iterate, pats, 2, 16, shifted)
    for index in range(2):
        tile = index + 6 * parity
        apply_tile(own_blocks, tile, shifted, own_at + tile, coupled)
    load.wait()
    for index in range(2):
        apply_tile(outer, index, shifted, 2 + 14 * parity + index, coupled)
    value, update = stepped(2, value, update, right, inverse, diagonal, coupled[...])
    known = (place >= 6) & (place < 14)
    value, update = jnp.where(known, inside[0], value), jnp.where(known, inside[1], update)
    iterate[...] = value
    neighbours(iterate, pats, 4, 12, shifted)
    for index in range(4):
        tile = index + 4 * parity
        apply_tile(own_blocks, tile, shifted, own_at + tile, coupled)
    product = jnp.where((place >= 8) & (place < 12), inside[2], coupled[...])
    value, update = stepped(3, value, update, right, inverse, diagonal, product)
    mine = jnp.where(parity == 0, value[4:12], value[8:16])
    solid[...] = mine
    for block in range(4):
        cell = own[8 * block : 8 * block + 8, :].astype(I32)
        tile, lane = cell >> 7, cell & 127
        found = jnp.zeros((8, WIDTH), F32)
        for index in range(TILES):
            row = jnp.broadcast_to(mine[index : index + 1, :], (8, WIDTH))
            found = jnp.where(tile == index, jnp.take_along_axis(row, lane, axis=1, mode="promise_in_bounds"), found)
        for r in range(8):
            returned[8 * block + r] = found[r : r + 1, :]


def stencil_kernel(fluid_hbm, liquid_hbm, x_faces, y_faces, z_before, z_after, base, fluid, liquid, sems):
    loads = [
        pltpu.make_async_copy(fluid_hbm, fluid, sems.at[0]),
        pltpu.make_async_copy(liquid_hbm, liquid, sems.at[1]),
    ]
    for each in loads:
        each.start()
    row = lax.broadcasted_iota(I32, (64, WIDTH), 0)
    lane = lax.broadcasted_iota(I32, (64, WIDTH), 1)
    for each in loads:
        each.wait()
    for slab in range(16):
        start = 64 * slab
        block = slab // 2
        here = fluid[start : start + 64, :]
        total = (fluid[start - 64 : start, :] if slab else x_faces[0]) + (
            fluid[start + 64 : start + 128, :] if slab < 15 else x_faces[1]
        )
        total = total + jnp.where(row == 0, y_faces[0, slab : slab + 1, :], pltpu.roll(here, 1, 0))
        total = total + jnp.where(row == 63, y_faces[1, slab : slab + 1, :], pltpu.roll(here, 63, 0))
        half = 64 * (slab % 2)
        left = jnp.broadcast_to(z_before[block : block + 1, :], (WIDTH, WIDTH)).T[half : half + 64, :]
        right = jnp.broadcast_to(z_after[block : block + 1, :], (WIDTH, WIDTH)).T[half : half + 64, :]
        total = total + jnp.where(lane == 0, left, pltpu.roll(here, 1, 1))
        total = total + jnp.where(lane == 127, right, pltpu.roll(here, 127, 1))
        total = total - 6.0 * here
        share = liquid[start : start + 64, :].astype(F32)
        base[start : start + 64, :] = (
            here + DIFFUSION * total - EVAPORATION * share * jnp.maximum(here - SATURATION, 0.0)
        )


def final_kernel(base, src, outgoing, returned, fluid_new):
    group = 4
    total = None
    for start in range(0, RUNS, group):
        rows = range(start, start + group)
        ids = lanes([src[r : r + 1, :] for r in rows])
        value = lanes([returned[r] - outgoing[r : r + 1, :] for r in rows])
        placed = placed_parts(ids & 127, WIDTH, value)
        added = lax.dot_general(row_hots(ids >> 7, ROWS), placed, CONTRACT_LAST, preferred_element_type=F32)
        total = added if total is None else total + added
    fluid_new[...] = base[...] + WALL_COUPLING * (total[:, 0:128] + total[:, 128:256])


def shape(*dims):
    return jax.ShapeDtypeStruct(dims, F32)


def call(kernel, mib, ins, outs, out_specs, scratch, flops, moved):
    return pl.pallas_call(
        kernel,
        in_specs=ins,
        out_shape=outs,
        out_specs=out_specs,
        scratch_shapes=scratch,
        compiler_params=params(mib),
        cost_estimate=pl.CostEstimate(flops=flops, bytes_accessed=moved, transcendentals=0),
    )


def vmem(*dims, kind=F32):
    return pltpu.VMEM(dims, kind)


def dma(*dims):
    return pltpu.SemaphoreType.DMA(dims) if dims else pltpu.SemaphoreType.DMA


def per_device(fluid_temp, liquid, face_src, face_dst, solid_old, solid_diag, blocks, pattern):
    inside_pairs = [(i, i ^ 1) for i in range(RUNS)]
    outside_pairs = [(i, (i - 1) % RUNS if i % 2 == 0 else (i + 1) % RUNS) for i in range(RUNS)]
    fluid = fluid_temp.reshape(ROWS, WIDTH)
    src = face_src.reshape(RUNS, WIDTH)
    dst = face_dst.reshape(RUNS, WIDTH)
    own_blocks = blocks.reshape(TILES * TILE_ROWS, WIDTH)
    in_rows, out_rows = 6 * TILE_ROWS + SMALL, 2 * TILE_ROWS + SMALL

    sent, outgoing, own, y_faces, z_faces, on_chip, across = call(
        pick_kernel, 60,
        [HBM] * 7,
        (
            shape(RUNS, 1, 384), shape(RUNS, WIDTH), shape(56, WIDTH), shape(2, 16, WIDTH), shape(2, 8, WIDTH),
            shape(in_rows, WIDTH), shape(out_rows, WIDTH),
        ),
        (VMEM, VMEM, VMEM, VMEM, VMEM, HBM, HBM),
        [
            vmem(ROWS, WIDTH), vmem(RUNS, WIDTH, kind=I32), vmem(RUNS, WIDTH, kind=I32), vmem(NB, 1, TILES, kind=I32),
            vmem(256, ROWS, kind=BF16), vmem(2, SMALL, WIDTH), vmem(6 * TILE_ROWS, WIDTH), vmem(2 * TILE_ROWS, WIDTH), dma(19),
        ],
        2 * 256 * 1024 * 4096, 1 << 22,
    )(fluid, src, dst, solid_old[0], solid_diag[0], jnp.transpose(pattern, (2, 0, 1)), own_blocks)

    arrived = lax.all_to_all(sent, "gx", split_axis=0, concat_axis=0, tiled=True)
    on_chip = lax.ppermute(on_chip, "gx", inside_pairs)
    across = lax.ppermute(across, "gx", outside_pairs)
    up = [(i, (i + 1) % 4) for i in range(4)]
    down = [(i, (i - 1) % 4) for i in range(4)]
    y_before = lax.ppermute(y_faces[1], "gy", up)
    y_after = lax.ppermute(y_faces[0], "gy", down)

    work = [vmem(WIN, WIDTH), vmem(NB, WIN, WIDTH), vmem(WIN, WIDTH)]
    added_own = call(
        own_run_kernel, 12, [VMEM, VMEM], shape(TILES, WIDTH), VMEM, [], 65 * 10**8, 1 << 16
    )(arrived, own)
    added_before, beside_small = call(
        beside_run_kernel, 12, [VMEM, ANY, VMEM], (shape(2 * TILES, WIDTH), shape(SMALL, WIDTH)), (VMEM, VMEM), [dma()],
        14 * 10**9, 1 << 16,
    )(arrived, across, added_own)
    state, pats, swap, x_faces, y_faces = call(
        wall_first_kernel, 16,
        [VMEM, VMEM, VMEM, VMEM, VMEM, ANY, ANY, VMEM, VMEM],
        (shape(5, WIN, WIDTH), shape(NB, WIN, WIDTH), shape(8, WIDTH), shape(2, 64, WIDTH), shape(2, 16, WIDTH)),
        (VMEM,) * 5,
        [vmem(in_rows, WIDTH), vmem(2 * TILE_ROWS, WIDTH)] + work + [dma(3)],
        1 << 24, 6 << 20,
    )(arrived, added_before, beside_small, own, own_blocks, on_chip, across, y_before, y_after)
    swapped = lax.ppermute(swap, "gx", outside_pairs)
    inside = call(
        wall_inner_kernel, 12,
        [VMEM, VMEM, VMEM, ANY],
        shape(3, WIN, WIDTH), VMEM,
        [vmem(2 * TILE_ROWS, WIDTH)] + work + [dma()],
        1 << 22, 3 << 20,
    )(state, pats, own_blocks, on_chip)
    solid, sent_back = call(
        wall_last_kernel, 12,
        [VMEM] * 6 + [ANY],
        (shape(TILES, WIDTH), shape(RUNS, 1, WIDTH)), (VMEM, VMEM),
        [vmem(2 * TILE_ROWS, WIDTH)] + work + [dma()],
        1 << 23, 3 << 20,
    )(state, pats, inside, swapped, own, own_blocks, across)
    sent_back, z_faces = lax.optimization_barrier((sent_back, z_faces))
    z_before = lax.ppermute(z_faces[1], "gz", up)
    z_after = lax.ppermute(z_faces[0], "gz", down)
    returned = lax.all_to_all(sent_back, "gx", split_axis=0, concat_axis=0, tiled=True)

    base = call(
        stencil_kernel, 12,
        [HBM, HBM, VMEM, VMEM, VMEM, VMEM],
        shape(ROWS, WIDTH), VMEM,
        [vmem(ROWS, WIDTH), vmem(ROWS, WIDTH, kind=I32), dma(2)],
        1 << 22, 1 << 21,
    )(fluid, liquid.reshape(ROWS, WIDTH), x_faces, y_faces, z_before, z_after)
    fluid_new = call(
        final_kernel, 16, [VMEM] * 4, shape(ROWS, WIDTH), VMEM, [], 2 * 256 * 1024 * 4096, 1 << 20
    )(base, src, outgoing, returned)
    return fluid_new.reshape(fluid_temp.shape), solid[None]


def solution(mesh):
    return jax.shard_map(
        per_device,
        mesh=mesh,
        in_specs=(
            P("gx", "gy", "gz"),
            P("gx", "gy", "gz"),
            P("gx", "gy", "gz", None),
            P("gx", "gy", "gz", None),
            P(("gy", "gz"), "gx", None),
            P(("gy", "gz"), "gx", None),
            P(("gy", "gz"), "gx", None, None, None),
            P(("gy", "gz"), "gx", None),
        ),
        out_specs=(P("gx", "gy", "gz"), P(("gy", "gz"), "gx", None)),
        check_vma=False,
    )
```

```python
import jax
import jax.numpy as jnp
from jax import lax
from jax.experimental import pallas as pl
from jax.experimental.pallas import tpu as pltpu
from jax.sharding import PartitionSpec as P

F32 = jnp.float32
BF16 = jnp.bfloat16
I32 = jnp.int32
RUNS = 32
WIDTH = 128
ROWS = 1024
TILES = 8
NB = 5
WIN = 24
TILE_ROWS = NB * WIDTH
SMALL = 120
FACE_ROWS = 128

DIFFUSION = 0.12
EVAPORATION = 0.5
SATURATION = 0.25
WALL_COUPLING = 0.2

VMEM = pl.BlockSpec(memory_space=pltpu.VMEM)
HBM = pl.BlockSpec(memory_space=pltpu.HBM)
ANY = pl.BlockSpec(memory_space=pl.ANY)


def params(mib):
    return pltpu.CompilerParams(vmem_limit_bytes=mib << 20)


def two_parts(values):
    high = values.astype(BF16)
    return high, (values - high.astype(F32)).astype(BF16)


def lanes(rows):
    return jnp.concatenate(rows, axis=1)


def row_hots(row, count):
    width = row.shape[1]
    part = min(count, 256)
    level = lax.broadcasted_iota(I32, (part, width), 0).astype(F32).astype(BF16)
    one, zero = jnp.ones((), BF16), jnp.zeros((), BF16)
    parts = []
    for index in range(count // part):
        here = jnp.where((row >= index * part) & (row < (index + 1) * part), row - index * part, -1)
        parts.append(jnp.where(level == here.astype(F32).astype(BF16), one, zero))
    return parts[0] if len(parts) == 1 else jnp.concatenate(parts, axis=0)


def placed_parts(column, count, values):
    width = column.shape[1]
    mask = lax.broadcasted_iota(I32, (count, width), 0) == column
    high = values.astype(BF16).astype(F32)
    low = values - high
    both = [jnp.where(mask, part, 0.0) for part in (high, low)]
    return jnp.concatenate(both, axis=0).astype(BF16)


CONTRACT_LAST = (((1,), (1,)), ((), ()))


def pick_kernel(
    fluid_hbm, src_hbm, dst_hbm, old_hbm, diag_hbm, pattern_hbm, blocks_hbm,
    sent, outgoing, own, faces_hbm, on_chip_hbm, across_hbm,
    fluid, src, dst, pattern, table, packed, staged_in, staged_out, faces, sems,
):
    me = lax.axis_index("gx")
    parity = lax.rem(me, 2)

    def copy(source, target, index):
        started = pltpu.make_async_copy(source, target, sems.at[index])
        started.start()
        return started

    loads = [copy(fluid_hbm.at[128 * i : 128 * i + 128], fluid.at[128 * i : 128 * i + 128], i) for i in range(8)]
    load_src = copy(src_hbm, src, 8)
    small = [
        copy(dst_hbm, dst, 9),
        copy(old_hbm, own.at[32:40], 10),
        copy(diag_hbm, own.at[40:48], 11),
        copy(pattern_hbm, pattern, 12),
    ]
    pieces = []
    for count, first, staged, target in (
        (2, parity * 6, staged_out, across_hbm),
        (6, (1 - parity) * 2, staged_in, on_chip_hbm),
    ):
        for tile in range(count):
            at = slice(tile * TILE_ROWS, (tile + 1) * TILE_ROWS)
            load = copy(blocks_hbm.at[pl.ds((first + tile) * TILE_ROWS, TILE_ROWS)], staged.at[at], 16 + len(pieces))
            pieces.append((load, staged.at[at], target.at[at]))
    for block in range(8):
        loads[block].wait()
        turned = fluid[128 * block : 128 * block + 128, :].T
        high, low = two_parts(turned)
        table[0:128, 128 * block : 128 * block + 128] = high
        table[128:256, 128 * block : 128 * block + 128] = low
        faces[32 + block : 33 + block, :] = turned[0:1, :]
        faces[40 + block : 41 + block, :] = turned[127:128, :]
    for slab in range(16):
        faces[slab : slab + 1, :] = fluid[64 * slab : 64 * slab + 1, :]
        faces[16 + slab : 17 + slab, :] = fluid[64 * slab + 63 : 64 * slab + 64, :]
    save_faces = copy(faces, faces_hbm.at[0:48], 13)
    load_src.wait()
    group = 4
    for start in range(0, RUNS, group):
        ids = lanes([src[r : r + 1, :] for r in range(start, start + group)])
        picked = jnp.dot(table[...], row_hots(ids >> 7, ROWS), preferred_element_type=F32)
        both = picked[0:128] + picked[128:256]
        mask = lax.broadcasted_iota(I32, (WIDTH, group * WIDTH), 0) == (ids & 127)
        value = jnp.sum(jnp.where(mask, both, 0.0), axis=0, keepdims=True)
        for r in range(start, start + group):
            mine = value[:, (r - start) * WIDTH : (r - start + 1) * WIDTH]
            outgoing[r : r + 1, :] = mine
            sent[r, :, 0:128] = mine
            sent[r ^ 1, :, 128:256] = mine
            beside = (r + 1) % RUNS if r % 2 else (r - 1) % RUNS
            sent[beside, :, 256:384] = mine
        index = start // group
        load, staged, target = pieces[index]
        load.wait()
        pieces[index] = copy(staged, target, 24 + index)
    for each in small:
        each.wait()
    own[0:32, :] = dst[...].astype(F32)
    own[48:56, :] = jnp.zeros((8, WIDTH), F32)
    for offset in range(NB):
        own[48 + offset : 49 + offset, 0:TILES] = pattern[offset].astype(F32)
    first, last = fluid[0:64, :], fluid[960:1024, :]
    for index, face in ((0, jnp.where(parity == 0, last, first)), (1, jnp.where(parity == 0, first, last))):
        packed[index, 0:56, :] = own[...]
        packed[index, 56:120, :] = face
    tail_in = copy(packed.at[0], on_chip_hbm.at[6 * TILE_ROWS : 6 * TILE_ROWS + SMALL], 14)
    tail_out = copy(packed.at[1], across_hbm.at[2 * TILE_ROWS : 2 * TILE_ROWS + SMALL], 15)
    for each in (*pieces, tail_in, tail_out, save_faces):
        each.wait()


def spread_run(ids_of, values_of):
    group = 8
    total = None
    for start in range(0, RUNS, group):
        cell = lanes([ids_of(r) for r in range(start, start + group)])
        value = lanes([values_of(r) for r in range(start, start + group)])
        row = jnp.where(cell >= 0, ((cell >> 5) & 3) * 8 + (cell >> 7), -1)
        hots = row_hots(row, 32)
        placed = placed_parts(cell & 31, 32, value)
        added = lax.dot_general(hots, placed, CONTRACT_LAST, preferred_element_type=F32)
        total = added if total is None else total + added
    total = total[:, 0:32] + total[:, 32:64]
    return lanes([total[8 * u : 8 * u + 8, :] for u in range(4)])


def window(parity, own, partner, beside):
    pad = jnp.zeros((4, own.shape[1]), F32)
    low = jnp.concatenate([beside[4:8], own, partner, pad], axis=0)
    high = jnp.concatenate([partner, own, beside[0:4], pad], axis=0)
    return jnp.where(parity == 0, low, high)


def neighbours(iterate, pats, first, count, shifted):
    for offset in range(NB):
        values = iterate[first - 2 + offset : first - 2 + offset + count, :]
        shifted[offset, first : first + count, :] = values * pats[offset, first : first + count, :]


def apply_tile(blocks, tile, shifted, place, coupled):
    total = None
    for offset in range(NB):
        start = pl.multiple_of(tile * TILE_ROWS + offset * WIDTH, WIDTH)
        term = blocks[pl.ds(start, WIDTH), :] * shifted[offset, pl.ds(place, 1), :]
        total = term if total is None else total + term
    coupled[pl.ds(place, 1), :] = jnp.sum(total.T, axis=0, keepdims=True)


RHO = [0.5]
for _ in range(3):
    RHO.append(1.0 / (4.0 - RHO[-1]))


def stepped(sweep, value, update, right, inverse, diagonal, coupled):
    residual = right - (diagonal * value + coupled)
    if sweep == 0:
        update = inverse * residual
    else:
        update = RHO[sweep] * RHO[sweep - 1] * update + 4.0 * RHO[sweep] * inverse * residual
    return value + update, update


def own_run_kernel(arrived, own, added):
    added[...] = spread_run(lambda r: own[r : r + 1, :].astype(I32), lambda r: arrived[r, :, 0:128])


def beside_run_kernel(arrived, across_hbm, added_own, added, small, sem):
    load = pltpu.make_async_copy(across_hbm.at[2 * TILE_ROWS : 2 * TILE_ROWS + SMALL], small, sem)
    load.start()
    added[0:TILES, :] = added_own[...]
    load.wait()
    added[TILES : 2 * TILES, :] = spread_run(
        lambda r: small[r : r + 1, :].astype(I32), lambda r: arrived[r, :, 256:384]
    )


def wall_first_kernel(
    arrived, added_before, beside_small, own, own_blocks, on_chip_hbm, across_hbm,
    state, pats, swap, faces,
    inner, outer, iterate, shifted, coupled, sems,
):
    me = lax.axis_index("gx")
    parity = lax.rem(me, 2)
    keep = jnp.where((me == 0) | (me == RUNS - 1), 0.0, 1.0)
    loads = []
    at_in = 6 * TILE_ROWS
    for index, (source, target, low, high) in enumerate((
        (on_chip_hbm, inner, at_in, at_in + SMALL),
        (on_chip_hbm, inner, 0, at_in),
        (across_hbm, outer, 0, 2 * TILE_ROWS),
    )):
        loads.append(pltpu.make_async_copy(source.at[low:high], target.at[low:high], sems.at[index]))
        loads[-1].start()
    loads[0].wait()
    partner, beside = inner[at_in : at_in + SMALL, :], beside_small[...]
    added = [
        added_before[0:TILES, :],
        spread_run(lambda r: inner[at_in + r : at_in + r + 1, :].astype(I32), lambda r: arrived[r, :, 128:256]),
        added_before[TILES : 2 * TILES, :],
    ]
    holders = [own[...], partner, beside]
    diagonals = [each[40:48] for each in holders]
    rights = [d * each[32:40] + a for d, each, a in zip(diagonals, holders, added)]
    inverses = [1.0 / d for d in diagonals]
    rights[2], inverses[2] = rights[2] * keep, inverses[2] * keep
    present = window(parity, *[each[48:56].T[0:TILES] for each in holders])
    for offset in range(NB):
        pats[offset] = jnp.broadcast_to(present[:, offset : offset + 1], (WIN, WIDTH))
    right = window(parity, *rights)
    inverse = window(parity, *inverses)
    diagonal = window(parity, *diagonals)
    faces[0] = jnp.where(parity == 0, beside[56:120], partner[56:120])
    faces[1] = jnp.where(parity == 0, partner[56:120], beside[56:120])
    value = inverse * right
    iterate[...] = value
    shifted[...] = jnp.zeros((NB, WIN, WIDTH), F32)
    coupled[...] = jnp.zeros((WIN, WIDTH), F32)
    own_at = 4 + 4 * parity

    neighbours(iterate, pats, 2, 16, shifted)
    for tile in range(TILES):
        apply_tile(own_blocks, tile, shifted, own_at + tile, coupled)
    loads[1].wait()
    loads[2].wait()
    for tile in range(6):
        apply_tile(inner, tile, shifted, 12 - 10 * parity + tile, coupled)
    for tile in range(2):
        apply_tile(outer, tile, shifted, 2 + 14 * parity + tile, coupled)
    value, update = stepped(0, value, None, right, inverse, diagonal, coupled[...])
    iterate[...] = value

    neighbours(iterate, pats, 4, 12, shifted)
    for tile in range(TILES):
        apply_tile(own_blocks, tile, shifted, own_at + tile, coupled)
    for tile in range(4):
        apply_tile(inner, tile + 2 * parity, shifted, 12 - 8 * parity + tile, coupled)
    value, update = stepped(1, value, update, right, inverse, diagonal, coupled[...])
    state[0], state[1], state[2], state[3], state[4] = value, update, right, inverse, diagonal
    swap[0:4, :] = jnp.where(parity == 0, value[4:8], value[12:16])
    swap[4:8, :] = jnp.where(parity == 0, update[4:8], update[12:16])


def wall_inner_kernel(state, pats, own_blocks, on_chip_hbm, inside, inner, iterate, shifted, coupled, sem):
    parity = lax.rem(lax.axis_index("gx"), 2)
    load = pltpu.make_async_copy(on_chip_hbm.at[pl.ds(parity * 4 * TILE_ROWS, 2 * TILE_ROWS)], inner, sem)
    load.start()
    value, update, right, inverse, diagonal = (state[i] for i in range(5))
    iterate[...] = value
    shifted[...] = jnp.zeros((NB, WIN, WIDTH), F32)
    coupled[...] = jnp.zeros((WIN, WIDTH), F32)
    own_at = 4 + 4 * parity
    neighbours(iterate, pats, 6, 8, shifted)
    for index in range(6):
        tile = index + 2 - 2 * parity
        apply_tile(own_blocks, tile, shifted, own_at + tile, coupled)
    load.wait()
    for index in range(2):
        apply_tile(inner, index, shifted, 12 - 6 * parity + index, coupled)
    value, update = stepped(2, value, update, right, inverse, diagonal, coupled[...])
    inside[0], inside[1] = value, update
    iterate[...] = value
    neighbours(iterate, pats, 8, 4, shifted)
    for index in range(4):
        tile = index + 4 - 4 * parity
        apply_tile(own_blocks, tile, shifted, own_at + tile, coupled)
    inside[2] = coupled[...]


def wall_last_kernel(
    state, pats, inside, swapped, own, own_blocks, across_hbm,
    solid, returned, outer, iterate, shifted, coupled, sem,
):
    load = pltpu.make_async_copy(across_hbm.at[0 : 2 * TILE_ROWS], outer, sem)
    load.start()
    me = lax.axis_index("gx")
    parity = lax.rem(me, 2)
    keep = jnp.where((me == 0) | (me == RUNS - 1), 0.0, 1.0)
    value, update, right, inverse, diagonal = (state[i] for i in range(5))

    def with_swapped(inside, outside):
        low = jnp.concatenate([outside, inside[4:24]], axis=0)
        high = jnp.concatenate([inside[0:16], outside, inside[20:24]], axis=0)
        return jnp.where(parity == 0, low, high)

    value = with_swapped(value, swapped[0:4, :] * keep)
    update = with_swapped(update, swapped[4:8, :] * keep)
    place = lax.broadcasted_iota(I32, (WIN, WIDTH), 0)
    own_at = 4 + 4 * parity
    iterate[...] = value
    shifted[...] = jnp.zeros((NB, WIN, WIDTH), F32)
    coupled[...] = jnp.zeros((WIN, WIDTH), F32)
    neighbours(iterate, pats, 2, 16, shifted)
    for index in range(2):
        tile = index + 6 * parity
        apply_tile(own_blocks, tile, shifted, own_at + tile, coupled)
    load.wait()
    for index in range(2):
        apply_tile(outer, index, shifted, 2 + 14 * parity + index, coupled)
    value, update = stepped(2, value, update, right, inverse, diagonal, coupled[...])
    known = (place >= 6) & (place < 14)
    value, update = jnp.where(known, inside[0], value), jnp.where(known, inside[1], update)
    iterate[...] = value
    neighbours(iterate, pats, 4, 12, shifted)
    for index in range(4):
        tile = index + 4 * parity
        apply_tile(own_blocks, tile, shifted, own_at + tile, coupled)
    product = jnp.where((place >= 8) & (place < 12), inside[2], coupled[...])
    value, update = stepped(3, value, update, right, inverse, diagonal, product)
    mine = jnp.where(parity == 0, value[4:12], value[8:16])
    solid[...] = mine
    for block in range(4):
        cell = own[8 * block : 8 * block + 8, :].astype(I32)
        tile, lane = cell >> 7, cell & 127
        found = jnp.zeros((8, WIDTH), F32)
        for index in range(TILES):
            row = jnp.broadcast_to(mine[index : index + 1, :], (8, WIDTH))
            found = jnp.where(tile == index, jnp.take_along_axis(row, lane, axis=1, mode="promise_in_bounds"), found)
        for r in range(8):
            returned[8 * block + r] = found[r : r + 1, :]


def stencil_kernel(fluid_hbm, liquid_hbm, x_faces, faces_hbm, base, fluid, liquid, faces, sems):
    loads = [
        pltpu.make_async_copy(fluid_hbm, fluid, sems.at[0]),
        pltpu.make_async_copy(liquid_hbm, liquid, sems.at[1]),
    ]
    y, z = lax.axis_index("gy"), lax.axis_index("gz")
    before_y, after_y = lax.rem(y + 3, 4) * 4 + z, lax.rem(y + 1, 4) * 4 + z
    before_z, after_z = y * 4 + lax.rem(z + 3, 4), y * 4 + lax.rem(z + 1, 4)
    for index, (holder, first, count) in enumerate((
        (before_y, 16, 16), (after_y, 0, 16), (before_z, 40, 8), (after_z, 32, 8),
    )):
        target = faces.at[16 * index : 16 * index + count]
        loads.append(pltpu.make_async_copy(faces_hbm.at[holder, first : first + count], target, sems.at[2 + index]))
    for each in loads:
        each.start()
    row = lax.broadcasted_iota(I32, (64, WIDTH), 0)
    lane = lax.broadcasted_iota(I32, (64, WIDTH), 1)
    for each in loads:
        each.wait()
    for slab in range(16):
        start = 64 * slab
        block = slab // 2
        here = fluid[start : start + 64, :]
        total = (fluid[start - 64 : start, :] if slab else x_faces[0]) + (
            fluid[start + 64 : start + 128, :] if slab < 15 else x_faces[1]
        )
        total = total + jnp.where(row == 0, faces[slab : slab + 1, :], pltpu.roll(here, 1, 0))
        total = total + jnp.where(row == 63, faces[16 + slab : 17 + slab, :], pltpu.roll(here, 63, 0))
        half = 64 * (slab % 2)
        left = jnp.broadcast_to(faces[32 + block : 33 + block, :], (WIDTH, WIDTH)).T[half : half + 64, :]
        right = jnp.broadcast_to(faces[48 + block : 49 + block, :], (WIDTH, WIDTH)).T[half : half + 64, :]
        total = total + jnp.where(lane == 0, left, pltpu.roll(here, 1, 1))
        total = total + jnp.where(lane == 127, right, pltpu.roll(here, 127, 1))
        total = total - 6.0 * here
        share = liquid[start : start + 64, :].astype(F32)
        base[start : start + 64, :] = (
            here + DIFFUSION * total - EVAPORATION * share * jnp.maximum(here - SATURATION, 0.0)
        )


def final_kernel(base, src, outgoing, returned, fluid_new):
    group = 4
    total = None
    for start in range(0, RUNS, group):
        rows = range(start, start + group)
        ids = lanes([src[r : r + 1, :] for r in rows])
        value = lanes([returned[r] - outgoing[r : r + 1, :] for r in rows])
        placed = placed_parts(ids & 127, WIDTH, value)
        added = lax.dot_general(row_hots(ids >> 7, ROWS), placed, CONTRACT_LAST, preferred_element_type=F32)
        total = added if total is None else total + added
    fluid_new[...] = base[...] + WALL_COUPLING * (total[:, 0:128] + total[:, 128:256])


def shape(*dims):
    return jax.ShapeDtypeStruct(dims, F32)


def call(kernel, mib, ins, outs, out_specs, scratch, flops, moved):
    return pl.pallas_call(
        kernel,
        in_specs=ins,
        out_shape=outs,
        out_specs=out_specs,
        scratch_shapes=scratch,
        compiler_params=params(mib),
        cost_estimate=pl.CostEstimate(flops=flops, bytes_accessed=moved, transcendentals=0),
    )


def vmem(*dims, kind=F32):
    return pltpu.VMEM(dims, kind)


def dma(*dims):
    return pltpu.SemaphoreType.DMA(dims) if dims else pltpu.SemaphoreType.DMA


def per_device(fluid_temp, liquid, face_src, face_dst, solid_old, solid_diag, blocks, pattern):
    inside_pairs = [(i, i ^ 1) for i in range(RUNS)]
    outside_pairs = [(i, (i - 1) % RUNS if i % 2 == 0 else (i + 1) % RUNS) for i in range(RUNS)]
    fluid = fluid_temp.reshape(ROWS, WIDTH)
    src = face_src.reshape(RUNS, WIDTH)
    dst = face_dst.reshape(RUNS, WIDTH)
    own_blocks = blocks.reshape(TILES * TILE_ROWS, WIDTH)
    in_rows, out_rows = 6 * TILE_ROWS + SMALL, 2 * TILE_ROWS + SMALL

    sent, outgoing, own, faces, on_chip, across = call(
        pick_kernel, 60,
        [HBM] * 7,
        (
            shape(RUNS, 1, 384), shape(RUNS, WIDTH), shape(56, WIDTH), shape(FACE_ROWS, WIDTH),
            shape(in_rows, WIDTH), shape(out_rows, WIDTH),
        ),
        (VMEM, VMEM, VMEM, HBM, HBM, HBM),
        [
            vmem(ROWS, WIDTH), vmem(RUNS, WIDTH, kind=I32), vmem(RUNS, WIDTH, kind=I32), vmem(NB, 1, TILES, kind=I32),
            vmem(256, ROWS, kind=BF16), vmem(2, SMALL, WIDTH), vmem(6 * TILE_ROWS, WIDTH), vmem(2 * TILE_ROWS, WIDTH), vmem(48, WIDTH), dma(32),
        ],
        2 * 256 * 1024 * 4096, 1 << 22,
    )(fluid, src, dst, solid_old[0], solid_diag[0], jnp.transpose(pattern, (2, 0, 1)), own_blocks)

    arrived = lax.all_to_all(sent, "gx", split_axis=0, concat_axis=0, tiled=True)
    on_chip = lax.ppermute(on_chip, "gx", inside_pairs)
    across = lax.ppermute(across, "gx", outside_pairs)
    faces = lax.all_gather(faces, ("gy", "gz"), axis=0, tiled=False)

    work = [vmem(WIN, WIDTH), vmem(NB, WIN, WIDTH), vmem(WIN, WIDTH)]
    added_own = call(
        own_run_kernel, 12, [VMEM, VMEM], shape(TILES, WIDTH), VMEM, [], 65 * 10**8, 1 << 16
    )(arrived, own)
    added_before, beside_small = call(
        beside_run_kernel, 12, [VMEM, ANY, VMEM], (shape(2 * TILES, WIDTH), shape(SMALL, WIDTH)), (VMEM, VMEM), [dma()],
        14 * 10**9, 1 << 16,
    )(arrived, across, added_own)
    state, pats, swap, x_faces = call(
        wall_first_kernel, 16,
        [VMEM, VMEM, VMEM, VMEM, VMEM, ANY, ANY],
        (shape(5, WIN, WIDTH), shape(NB, WIN, WIDTH), shape(8, WIDTH), shape(2, 64, WIDTH)),
        (VMEM,) * 4,
        [vmem(in_rows, WIDTH), vmem(2 * TILE_ROWS, WIDTH)] + work + [dma(3)],
        1 << 24, 6 << 20,
    )(arrived, added_before, beside_small, own, own_blocks, on_chip, across)
    swapped = lax.ppermute(swap, "gx", outside_pairs)
    inside = call(
        wall_inner_kernel, 12,
        [VMEM, VMEM, VMEM, ANY],
        shape(3, WIN, WIDTH), VMEM,
        [vmem(2 * TILE_ROWS, WIDTH)] + work + [dma()],
        1 << 22, 3 << 20,
    )(state, pats, own_blocks, on_chip)
    solid, sent_back = call(
        wall_last_kernel, 12,
        [VMEM] * 6 + [ANY],
        (shape(TILES, WIDTH), shape(RUNS, 1, WIDTH)), (VMEM, VMEM),
        [vmem(2 * TILE_ROWS, WIDTH)] + work + [dma()],
        1 << 23, 3 << 20,
    )(state, pats, inside, swapped, own, own_blocks, across)
    returned = lax.all_to_all(sent_back, "gx", split_axis=0, concat_axis=0, tiled=True)

    base = call(
        stencil_kernel, 12,
        [HBM, HBM, VMEM, ANY],
        shape(ROWS, WIDTH), VMEM,
        [vmem(ROWS, WIDTH), vmem(ROWS, WIDTH, kind=I32), vmem(64, WIDTH), dma(6)],
        1 << 22, 1 << 21,
    )(fluid, liquid.reshape(ROWS, WIDTH), x_faces, faces)
    fluid_new = call(
        final_kernel, 16, [VMEM] * 4, shape(ROWS, WIDTH), VMEM, [], 2 * 256 * 1024 * 4096, 1 << 20
    )(base, src, outgoing, returned)
    return fluid_new.reshape(fluid_temp.shape), solid[None]


def solution(mesh):
    return jax.shard_map(
        per_device,
        mesh=mesh,
        in_specs=(
            P("gx", "gy", "gz"),
            P("gx", "gy", "gz"),
            P("gx", "gy", "gz", None),
            P("gx", "gy", "gz", None),
            P(("gy", "gz"), "gx", None),
            P(("gy", "gz"), "gx", None),
            P(("gy", "gz"), "gx", None, None, None),
            P(("gy", "gz"), "gx", None),
        ),
        out_specs=(P("gx", "gy", "gz"), P(("gy", "gz"), "gx", None)),
        check_vma=False,
    )
```

```python
import jax
import jax.numpy as jnp
from jax import lax
from jax.experimental import pallas as pl
from jax.experimental.pallas import tpu as pltpu
from jax.sharding import PartitionSpec as P

F32 = jnp.float32
BF16 = jnp.bfloat16
I32 = jnp.int32
RUNS = 32
WIDTH = 128
ROWS = 1024
TILES = 8
NB = 5
WIN = 24
TILE_ROWS = NB * WIDTH
SMALL = 120

DIFFUSION = 0.12
EVAPORATION = 0.5
SATURATION = 0.25
WALL_COUPLING = 0.2

VMEM = pl.BlockSpec(memory_space=pltpu.VMEM)
HBM = pl.BlockSpec(memory_space=pltpu.HBM)
ANY = pl.BlockSpec(memory_space=pl.ANY)


def params(mib):
    return pltpu.CompilerParams(vmem_limit_bytes=mib << 20)


def two_parts(values):
    high = values.astype(BF16)
    return high, (values - high.astype(F32)).astype(BF16)


def lanes(rows):
    return jnp.concatenate(rows, axis=1)


def row_hots(row, count):
    width = row.shape[1]
    part = min(count, 256)
    level = lax.broadcasted_iota(I32, (part, width), 0).astype(F32).astype(BF16)
    one, zero = jnp.ones((), BF16), jnp.zeros((), BF16)
    parts = []
    for index in range(count // part):
        here = jnp.where((row >= index * part) & (row < (index + 1) * part), row - index * part, -1)
        parts.append(jnp.where(level == here.astype(F32).astype(BF16), one, zero))
    return parts[0] if len(parts) == 1 else jnp.concatenate(parts, axis=0)


def placed_parts(column, count, values):
    width = column.shape[1]
    mask = lax.broadcasted_iota(I32, (count, width), 0) == column
    high = values.astype(BF16).astype(F32)
    low = values - high
    both = [jnp.where(mask, part, 0.0) for part in (high, low)]
    return jnp.concatenate(both, axis=0).astype(BF16)


CONTRACT_LAST = (((1,), (1,)), ((), ()))


def pick_kernel(
    fluid_hbm, src_hbm, dst_hbm, old_hbm, diag_hbm, pattern_hbm, blocks_hbm,
    sent, outgoing, own, faces, on_chip_hbm, across_hbm,
    fluid, src, dst, pattern, table, packed, staged_in, staged_out, sems,
):
    me = lax.axis_index("gx")
    parity = lax.rem(me, 2)

    def copy(source, target, index):
        started = pltpu.make_async_copy(source, target, sems.at[index])
        started.start()
        return started

    loads = [copy(fluid_hbm.at[128 * i : 128 * i + 128], fluid.at[128 * i : 128 * i + 128], i) for i in range(8)]
    load_src = copy(src_hbm, src, 8)
    small = [
        copy(dst_hbm, dst, 9),
        copy(old_hbm, own.at[32:40], 10),
        copy(diag_hbm, own.at[40:48], 11),
        copy(pattern_hbm, pattern, 16),
    ]
    inside = copy(blocks_hbm.at[pl.ds((1 - parity) * 2 * TILE_ROWS, 6 * TILE_ROWS)], staged_in, 12)
    outside = copy(blocks_hbm.at[pl.ds(parity * 6 * TILE_ROWS, 2 * TILE_ROWS)], staged_out, 13)
    before_z = lax.axis_index("gy") * 4 + lax.rem(lax.axis_index("gz") + 3, 4)
    after_z = lax.axis_index("gy") * 4 + lax.rem(lax.axis_index("gz") + 1, 4)
    for block in range(8):
        loads[block].wait()
        turned = fluid[128 * block : 128 * block + 128, :].T
        high, low = two_parts(turned)
        table[0:128, 128 * block : 128 * block + 128] = high
        table[128:256, 128 * block : 128 * block + 128] = low
        at = slice(128 * block, 128 * block + 128)
        faces[before_z, :, at] = turned[0:1, :]
        faces[after_z, :, at] = turned[127:128, :]
    for each in small:
        each.wait()
    own[0:32, :] = dst[...].astype(F32)
    own[48:56, :] = jnp.zeros((8, WIDTH), F32)
    for offset in range(NB):
        own[48 + offset : 49 + offset, 0:TILES] = pattern[offset].astype(F32)
    first, last = fluid[0:64, :], fluid[960:1024, :]
    for index, face in ((0, jnp.where(parity == 0, last, first)), (1, jnp.where(parity == 0, first, last))):
        packed[index, 0:56, :] = own[...]
        packed[index, 56:120, :] = face
    tail_in = copy(packed.at[0], on_chip_hbm.at[6 * TILE_ROWS : 6 * TILE_ROWS + SMALL], 14)
    tail_out = copy(packed.at[1], across_hbm.at[2 * TILE_ROWS : 2 * TILE_ROWS + SMALL], 15)
    y, z = lax.axis_index("gy"), lax.axis_index("gz")
    after_y, before_y = lax.rem(y + 1, 4) * 4 + z, lax.rem(y + 3, 4) * 4 + z
    for slab in range(16):
        at = slice(128 * slab, 128 * slab + 128)
        faces[before_y, :, at] = fluid[64 * slab : 64 * slab + 1, :]
        faces[after_y, :, at] = fluid[64 * slab + 63 : 64 * slab + 64, :]
    load_src.wait()
    group = 4
    for start in range(0, RUNS, group):
        if start == RUNS // 2:
            inside.wait()
            outside.wait()
            inside = copy(staged_in, on_chip_hbm.at[0 : 6 * TILE_ROWS], 17)
            outside = copy(staged_out, across_hbm.at[0 : 2 * TILE_ROWS], 18)
        ids = lanes([src[r : r + 1, :] for r in range(start, start + group)])
        picked = jnp.dot(table[...], row_hots(ids >> 7, ROWS), preferred_element_type=F32)
        both = picked[0:128] + picked[128:256]
        mask = lax.broadcasted_iota(I32, (WIDTH, group * WIDTH), 0) == (ids & 127)
        value = jnp.sum(jnp.where(mask, both, 0.0), axis=0, keepdims=True)
        for r in range(start, start + group):
            mine = value[:, (r - start) * WIDTH : (r - start + 1) * WIDTH]
            outgoing[r : r + 1, :] = mine
            sent[r, :, 0:128] = mine
            sent[r ^ 1, :, 128:256] = mine
            beside = (r + 1) % RUNS if r % 2 else (r - 1) % RUNS
            sent[beside, :, 256:384] = mine
    for each in (inside, outside, tail_in, tail_out):
        each.wait()


def spread_run(ids_of, values_of):
    group = 8
    total = None
    for start in range(0, RUNS, group):
        cell = lanes([ids_of(r) for r in range(start, start + group)])
        value = lanes([values_of(r) for r in range(start, start + group)])
        row = jnp.where(cell >= 0, ((cell >> 5) & 3) * 8 + (cell >> 7), -1)
        hots = row_hots(row, 32)
        placed = placed_parts(cell & 31, 32, value)
        added = lax.dot_general(hots, placed, CONTRACT_LAST, preferred_element_type=F32)
        total = added if total is None else total + added
    total = total[:, 0:32] + total[:, 32:64]
    return lanes([total[8 * u : 8 * u + 8, :] for u in range(4)])


def window(parity, own, partner, beside):
    pad = jnp.zeros((4, own.shape[1]), F32)
    low = jnp.concatenate([beside[4:8], own, partner, pad], axis=0)
    high = jnp.concatenate([partner, own, beside[0:4], pad], axis=0)
    return jnp.where(parity == 0, low, high)


def neighbours(iterate, pats, first, count, shifted):
    for offset in range(NB):
        values = iterate[first - 2 + offset : first - 2 + offset + count, :]
        shifted[offset, first : first + count, :] = values * pats[offset, first : first + count, :]


def apply_tile(blocks, tile, shifted, place, coupled):
    total = None
    for offset in range(NB):
        start = pl.multiple_of(tile * TILE_ROWS + offset * WIDTH, WIDTH)
        term = blocks[pl.ds(start, WIDTH), :] * shifted[offset, pl.ds(place, 1), :]
        total = term if total is None else total + term
    coupled[pl.ds(place, 1), :] = jnp.sum(total.T, axis=0, keepdims=True)


RHO = [0.5]
for _ in range(3):
    RHO.append(1.0 / (4.0 - RHO[-1]))


def stepped(sweep, value, update, right, inverse, diagonal, coupled):
    residual = right - (diagonal * value + coupled)
    if sweep == 0:
        update = inverse * residual
    else:
        update = RHO[sweep] * RHO[sweep - 1] * update + 4.0 * RHO[sweep] * inverse * residual
    return value + update, update


def own_run_kernel(arrived, dst, added):
    added[...] = spread_run(lambda r: dst[r : r + 1, :], lambda r: arrived[r, :, 0:128])


def beside_run_kernel(arrived, across_hbm, added_own, added, small, sem):
    load = pltpu.make_async_copy(across_hbm.at[2 * TILE_ROWS : 2 * TILE_ROWS + SMALL], small, sem)
    load.start()
    added[0:TILES, :] = added_own[...]
    load.wait()
    added[TILES : 2 * TILES, :] = spread_run(
        lambda r: small[r : r + 1, :].astype(I32), lambda r: arrived[r, :, 256:384]
    )


def wall_first_kernel(
    arrived, added_before, beside_small, own, own_blocks, on_chip_hbm, across_hbm,
    state, pats, swap, faces,
    inner, outer, iterate, shifted, coupled, sems,
):
    me = lax.axis_index("gx")
    parity = lax.rem(me, 2)
    keep = jnp.where((me == 0) | (me == RUNS - 1), 0.0, 1.0)
    loads = []
    at_in = 6 * TILE_ROWS
    for index, (source, target, low, high) in enumerate((
        (on_chip_hbm, inner, at_in, at_in + SMALL),
        (on_chip_hbm, inner, 0, at_in),
        (across_hbm, outer, 0, 2 * TILE_ROWS),
    )):
        loads.append(pltpu.make_async_copy(source.at[low:high], target.at[low:high], sems.at[index]))
        loads[-1].start()
    loads[0].wait()
    partner, beside = inner[at_in : at_in + SMALL, :], beside_small[...]
    added = [
        added_before[0:TILES, :],
        spread_run(lambda r: inner[at_in + r : at_in + r + 1, :].astype(I32), lambda r: arrived[r, :, 128:256]),
        added_before[TILES : 2 * TILES, :],
    ]
    holders = [own[...], partner, beside]
    diagonals = [each[40:48] for each in holders]
    rights = [d * each[32:40] + a for d, each, a in zip(diagonals, holders, added)]
    inverses = [1.0 / d for d in diagonals]
    rights[2], inverses[2] = rights[2] * keep, inverses[2] * keep
    present = window(parity, *[each[48:56].T[0:TILES] for each in holders])
    for offset in range(NB):
        pats[offset] = jnp.broadcast_to(present[:, offset : offset + 1], (WIN, WIDTH))
    right = window(parity, *rights)
    inverse = window(parity, *inverses)
    diagonal = window(parity, *diagonals)
    faces[0] = jnp.where(parity == 0, beside[56:120], partner[56:120])
    faces[1] = jnp.where(parity == 0, partner[56:120], beside[56:120])
    value = inverse * right
    iterate[...] = value
    shifted[...] = jnp.zeros((NB, WIN, WIDTH), F32)
    coupled[...] = jnp.zeros((WIN, WIDTH), F32)
    own_at = 4 + 4 * parity

    neighbours(iterate, pats, 2, 16, shifted)
    for tile in range(TILES):
        apply_tile(own_blocks, tile, shifted, own_at + tile, coupled)
    loads[1].wait()
    loads[2].wait()
    for tile in range(6):
        apply_tile(inner, tile, shifted, 12 - 10 * parity + tile, coupled)
    for tile in range(2):
        apply_tile(outer, tile, shifted, 2 + 14 * parity + tile, coupled)
    value, update = stepped(0, value, None, right, inverse, diagonal, coupled[...])
    iterate[...] = value

    neighbours(iterate, pats, 4, 12, shifted)
    for tile in range(TILES):
        apply_tile(own_blocks, tile, shifted, own_at + tile, coupled)
    for tile in range(4):
        apply_tile(inner, tile + 2 * parity, shifted, 12 - 8 * parity + tile, coupled)
    value, update = stepped(1, value, update, right, inverse, diagonal, coupled[...])
    state[0], state[1], state[2], state[3], state[4] = value, update, right, inverse, diagonal
    swap[0:4, :] = jnp.where(parity == 0, value[4:8], value[12:16])
    swap[4:8, :] = jnp.where(parity == 0, update[4:8], update[12:16])


def wall_inner_kernel(state, pats, own_blocks, on_chip_hbm, inside, inner, iterate, shifted, coupled, sem):
    parity = lax.rem(lax.axis_index("gx"), 2)
    load = pltpu.make_async_copy(on_chip_hbm.at[pl.ds(parity * 4 * TILE_ROWS, 2 * TILE_ROWS)], inner, sem)
    load.start()
    value, update, right, inverse, diagonal = (state[i] for i in range(5))
    iterate[...] = value
    shifted[...] = jnp.zeros((NB, WIN, WIDTH), F32)
    coupled[...] = jnp.zeros((WIN, WIDTH), F32)
    own_at = 4 + 4 * parity
    neighbours(iterate, pats, 6, 8, shifted)
    for index in range(6):
        tile = index + 2 - 2 * parity
        apply_tile(own_blocks, tile, shifted, own_at + tile, coupled)
    load.wait()
    for index in range(2):
        apply_tile(inner, index, shifted, 12 - 6 * parity + index, coupled)
    value, update = stepped(2, value, update, right, inverse, diagonal, coupled[...])
    inside[0], inside[1] = value, update
    iterate[...] = value
    neighbours(iterate, pats, 8, 4, shifted)
    for index in range(4):
        tile = index + 4 - 4 * parity
        apply_tile(own_blocks, tile, shifted, own_at + tile, coupled)
    inside[2] = coupled[...]


def wall_last_kernel(
    state, pats, inside, swapped, own, own_blocks, across_hbm,
    solid, returned, outer, iterate, shifted, coupled, sem,
):
    load = pltpu.make_async_copy(across_hbm.at[0 : 2 * TILE_ROWS], outer, sem)
    load.start()
    me = lax.axis_index("gx")
    parity = lax.rem(me, 2)
    keep = jnp.where((me == 0) | (me == RUNS - 1), 0.0, 1.0)
    value, update, right, inverse, diagonal = (state[i] for i in range(5))

    def with_swapped(inside, outside):
        low = jnp.concatenate([outside, inside[4:24]], axis=0)
        high = jnp.concatenate([inside[0:16], outside, inside[20:24]], axis=0)
        return jnp.where(parity == 0, low, high)

    value = with_swapped(value, swapped[0:4, :] * keep)
    update = with_swapped(update, swapped[4:8, :] * keep)
    place = lax.broadcasted_iota(I32, (WIN, WIDTH), 0)
    own_at = 4 + 4 * parity
    iterate[...] = value
    shifted[...] = jnp.zeros((NB, WIN, WIDTH), F32)
    coupled[...] = jnp.zeros((WIN, WIDTH), F32)
    neighbours(iterate, pats, 2, 16, shifted)
    for index in range(2):
        tile = index + 6 * parity
        apply_tile(own_blocks, tile, shifted, own_at + tile, coupled)
    load.wait()
    for index in range(2):
        apply_tile(outer, index, shifted, 2 + 14 * parity + index, coupled)
    value, update = stepped(2, value, update, right, inverse, diagonal, coupled[...])
    known = (place >= 6) & (place < 14)
    value, update = jnp.where(known, inside[0], value), jnp.where(known, inside[1], update)
    iterate[...] = value
    neighbours(iterate, pats, 4, 12, shifted)
    for index in range(4):
        tile = index + 4 * parity
        apply_tile(own_blocks, tile, shifted, own_at + tile, coupled)
    product = jnp.where((place >= 8) & (place < 12), inside[2], coupled[...])
    value, update = stepped(3, value, update, right, inverse, diagonal, product)
    mine = jnp.where(parity == 0, value[4:12], value[8:16])
    solid[...] = mine
    for block in range(4):
        cell = own[8 * block : 8 * block + 8, :].astype(I32)
        tile, lane = cell >> 7, cell & 127
        found = jnp.zeros((8, WIDTH), F32)
        for index in range(TILES):
            row = jnp.broadcast_to(mine[index : index + 1, :], (8, WIDTH))
            found = jnp.where(tile == index, jnp.take_along_axis(row, lane, axis=1, mode="promise_in_bounds"), found)
        for r in range(8):
            returned[8 * block + r] = found[r : r + 1, :]


def final_kernel(fluid, liquid, x_faces, faces, src, outgoing, returned, fluid_new):
    group = 4
    total = None
    for start in range(0, RUNS, group):
        rows = range(start, start + group)
        ids = lanes([src[r : r + 1, :] for r in rows])
        value = lanes([returned[r] - outgoing[r : r + 1, :] for r in rows])
        placed = placed_parts(ids & 127, WIDTH, value)
        added = lax.dot_general(row_hots(ids >> 7, ROWS), placed, CONTRACT_LAST, preferred_element_type=F32)
        total = added if total is None else total + added
    wall = total[:, 0:128] + total[:, 128:256]
    y, z = lax.axis_index("gy"), lax.axis_index("gz")
    after_y, before_y = lax.rem(y + 1, 4) * 4 + z, lax.rem(y + 3, 4) * 4 + z
    after_z, before_z = y * 4 + lax.rem(z + 1, 4), y * 4 + lax.rem(z + 3, 4)
    row = lax.broadcasted_iota(I32, (64, WIDTH), 0)
    lane = lax.broadcasted_iota(I32, (64, WIDTH), 1)
    for slab in range(16):
        start = 64 * slab
        at, at_z = slice(128 * slab, 128 * slab + 128), slice(128 * (slab // 2), 128 * (slab // 2) + 128)
        here = fluid[start : start + 64, :]
        total = (fluid[start - 64 : start, :] if slab else x_faces[0]) + (
            fluid[start + 64 : start + 128, :] if slab < 15 else x_faces[1]
        )
        total = total + jnp.where(row == 0, faces[before_y, :, at], pltpu.roll(here, 1, 0))
        total = total + jnp.where(row == 63, faces[after_y, :, at], pltpu.roll(here, 63, 0))
        half = 64 * (slab % 2)
        left = jnp.broadcast_to(faces[before_z, :, at_z], (WIDTH, WIDTH)).T[half : half + 64, :]
        right = jnp.broadcast_to(faces[after_z, :, at_z], (WIDTH, WIDTH)).T[half : half + 64, :]
        total = total + jnp.where(lane == 0, left, pltpu.roll(here, 1, 1))
        total = total + jnp.where(lane == 127, right, pltpu.roll(here, 127, 1))
        total = total - 6.0 * here
        share = liquid[start : start + 64, :].astype(F32)
        fluid_new[start : start + 64, :] = (
            here
            + DIFFUSION * total
            - EVAPORATION * share * jnp.maximum(here - SATURATION, 0.0)
            + WALL_COUPLING * wall[start : start + 64, :]
        )


def shape(*dims):
    return jax.ShapeDtypeStruct(dims, F32)


def call(kernel, mib, ins, outs, out_specs, scratch, flops, moved):
    return pl.pallas_call(
        kernel,
        in_specs=ins,
        out_shape=outs,
        out_specs=out_specs,
        scratch_shapes=scratch,
        compiler_params=params(mib),
        cost_estimate=pl.CostEstimate(flops=flops, bytes_accessed=moved, transcendentals=0),
    )


def vmem(*dims, kind=F32):
    return pltpu.VMEM(dims, kind)


def dma(*dims):
    return pltpu.SemaphoreType.DMA(dims) if dims else pltpu.SemaphoreType.DMA


def per_device(fluid_temp, liquid, face_src, face_dst, solid_old, solid_diag, blocks, pattern):
    inside_pairs = [(i, i ^ 1) for i in range(RUNS)]
    outside_pairs = [(i, (i - 1) % RUNS if i % 2 == 0 else (i + 1) % RUNS) for i in range(RUNS)]
    fluid = fluid_temp.reshape(ROWS, WIDTH)
    src = face_src.reshape(RUNS, WIDTH)
    dst = face_dst.reshape(RUNS, WIDTH)
    own_blocks = blocks.reshape(TILES * TILE_ROWS, WIDTH)
    in_rows, out_rows = 6 * TILE_ROWS + SMALL, 2 * TILE_ROWS + SMALL

    sent, outgoing, own, faces, on_chip, across = call(
        pick_kernel, 60,
        [HBM] * 7,
        (
            shape(RUNS, 1, 384), shape(RUNS, WIDTH), shape(56, WIDTH), shape(16, 1, 2048),
            shape(in_rows, WIDTH), shape(out_rows, WIDTH),
        ),
        (VMEM, VMEM, VMEM, VMEM, HBM, HBM),
        [
            vmem(ROWS, WIDTH), vmem(RUNS, WIDTH, kind=I32), vmem(RUNS, WIDTH, kind=I32), vmem(NB, 1, TILES, kind=I32),
            vmem(256, ROWS, kind=BF16), vmem(2, SMALL, WIDTH), vmem(6 * TILE_ROWS, WIDTH), vmem(2 * TILE_ROWS, WIDTH), dma(19),
        ],
        2 * 256 * 1024 * 4096, 1 << 22,
    )(fluid, src, dst, solid_old[0], solid_diag[0], jnp.transpose(pattern, (2, 0, 1)), own_blocks)

    arrived = lax.all_to_all(sent, "gx", split_axis=0, concat_axis=0, tiled=True)
    on_chip = lax.ppermute(on_chip, "gx", inside_pairs)
    across = lax.ppermute(across, "gx", outside_pairs)
    faces = lax.all_to_all(faces, ("gy", "gz"), split_axis=0, concat_axis=0, tiled=True)

    work = [vmem(WIN, WIDTH), vmem(NB, WIN, WIDTH), vmem(WIN, WIDTH)]
    added_own = call(
        own_run_kernel, 12, [VMEM, VMEM], shape(TILES, WIDTH), VMEM, [], 65 * 10**8, 1 << 16
    )(arrived, dst)
    added_before, beside_small = call(
        beside_run_kernel, 12, [VMEM, ANY, VMEM], (shape(2 * TILES, WIDTH), shape(SMALL, WIDTH)), (VMEM, VMEM), [dma()],
        14 * 10**9, 1 << 16,
    )(arrived, across, added_own)
    state, pats, swap, x_faces = call(
        wall_first_kernel, 16,
        [VMEM, VMEM, VMEM, VMEM, VMEM, ANY, ANY],
        (shape(5, WIN, WIDTH), shape(NB, WIN, WIDTH), shape(8, WIDTH), shape(2, 64, WIDTH)),
        (VMEM,) * 4,
        [vmem(in_rows, WIDTH), vmem(2 * TILE_ROWS, WIDTH)] + work + [dma(3)],
        1 << 24, 6 << 20,
    )(arrived, added_before, beside_small, own, own_blocks, on_chip, across)
    swapped = lax.ppermute(swap, "gx", outside_pairs)
    inside = call(
        wall_inner_kernel, 12,
        [VMEM, VMEM, VMEM, ANY],
        shape(3, WIN, WIDTH), VMEM,
        [vmem(2 * TILE_ROWS, WIDTH)] + work + [dma()],
        1 << 22, 3 << 20,
    )(state, pats, own_blocks, on_chip)
    solid, sent_back = call(
        wall_last_kernel, 12,
        [VMEM] * 6 + [ANY],
        (shape(TILES, WIDTH), shape(RUNS, 1, WIDTH)), (VMEM, VMEM),
        [vmem(2 * TILE_ROWS, WIDTH)] + work + [dma()],
        1 << 23, 3 << 20,
    )(state, pats, inside, swapped, own, own_blocks, across)
    returned = lax.all_to_all(sent_back, "gx", split_axis=0, concat_axis=0, tiled=True)

    fluid_new = call(
        final_kernel, 16, [VMEM] * 7, shape(ROWS, WIDTH), VMEM, [], 2 * 256 * 1024 * 4096, 1 << 20
    )(fluid, liquid.reshape(ROWS, WIDTH), x_faces, faces, src, outgoing, returned)
    return fluid_new.reshape(fluid_temp.shape), solid[None]


def solution(mesh):
    return jax.shard_map(
        per_device,
        mesh=mesh,
        in_specs=(
            P("gx", "gy", "gz"),
            P("gx", "gy", "gz"),
            P("gx", "gy", "gz", None),
            P("gx", "gy", "gz", None),
            P(("gy", "gz"), "gx", None),
            P(("gy", "gz"), "gx", None),
            P(("gy", "gz"), "gx", None, None, None),
            P(("gy", "gz"), "gx", None),
        ),
        out_specs=(P("gx", "gy", "gz"), P(("gy", "gz"), "gx", None)),
        check_vma=False,
    )
```

```python
import jax
import jax.numpy as jnp
from jax import lax
from jax.experimental import pallas as pl
from jax.experimental.pallas import tpu as pltpu
from jax.sharding import PartitionSpec as P

F32 = jnp.float32
BF16 = jnp.bfloat16
I32 = jnp.int32
RUNS = 32
WIDTH = 128
ROWS = 1024
TILES = 8
NB = 5
WIN = 24
TILE_ROWS = NB * WIDTH
SMALL = 120

DIFFUSION = 0.12
EVAPORATION = 0.5
SATURATION = 0.25
WALL_COUPLING = 0.2

VMEM = pl.BlockSpec(memory_space=pltpu.VMEM)
HBM = pl.BlockSpec(memory_space=pltpu.HBM)
ANY = pl.BlockSpec(memory_space=pl.ANY)


def params(mib):
    return pltpu.CompilerParams(vmem_limit_bytes=mib << 20)


def two_parts(values):
    high = values.astype(BF16)
    return high, (values - high.astype(F32)).astype(BF16)


def lanes(rows):
    return jnp.concatenate(rows, axis=1)


def row_hots(row, count):
    width = row.shape[1]
    part = min(count, 256)
    level = lax.broadcasted_iota(I32, (part, width), 0).astype(F32).astype(BF16)
    one, zero = jnp.ones((), BF16), jnp.zeros((), BF16)
    parts = []
    for index in range(count // part):
        here = jnp.where((row >= index * part) & (row < (index + 1) * part), row - index * part, -1)
        parts.append(jnp.where(level == here.astype(F32).astype(BF16), one, zero))
    return parts[0] if len(parts) == 1 else jnp.concatenate(parts, axis=0)


def placed_parts(column, count, values):
    width = column.shape[1]
    mask = lax.broadcasted_iota(I32, (count, width), 0) == column
    high = values.astype(BF16).astype(F32)
    low = values - high
    both = [jnp.where(mask, part, 0.0) for part in (high, low)]
    return jnp.concatenate(both, axis=0).astype(BF16)


CONTRACT_LAST = (((1,), (1,)), ((), ()))


def pick_kernel(
    fluid_hbm, src_hbm, dst_hbm, old_hbm, diag_hbm, pattern_hbm, blocks_hbm,
    sent, outgoing, own, faces, on_chip_hbm, across_hbm,
    fluid, src, dst, pattern, table, packed, staged_in, staged_out, sems,
):
    me = lax.axis_index("gx")
    parity = lax.rem(me, 2)

    def copy(source, target, index):
        started = pltpu.make_async_copy(source, target, sems.at[index])
        started.start()
        return started

    loads = [copy(fluid_hbm.at[128 * i : 128 * i + 128], fluid.at[128 * i : 128 * i + 128], i) for i in range(8)]
    load_src = copy(src_hbm, src, 8)
    small = [
        copy(dst_hbm, dst, 9),
        copy(old_hbm, own.at[32:40], 10),
        copy(diag_hbm, own.at[40:48], 11),
        copy(pattern_hbm, pattern, 16),
    ]
    inside = copy(blocks_hbm.at[pl.ds((1 - parity) * 2 * TILE_ROWS, 6 * TILE_ROWS)], staged_in, 12)
    outside = copy(blocks_hbm.at[pl.ds(parity * 6 * TILE_ROWS, 2 * TILE_ROWS)], staged_out, 13)
    before_z = lax.axis_index("gy") * 4 + lax.rem(lax.axis_index("gz") + 3, 4)
    after_z = lax.axis_index("gy") * 4 + lax.rem(lax.axis_index("gz") + 1, 4)
    for block in range(8):
        loads[block].wait()
        turned = fluid[128 * block : 128 * block + 128, :].T
        high, low = two_parts(turned)
        table[0:128, 128 * block : 128 * block + 128] = high
        table[128:256, 128 * block : 128 * block + 128] = low
        at = slice(128 * block, 128 * block + 128)
        faces[before_z, :, at] = turned[0:1, :]
        faces[after_z, :, at] = turned[127:128, :]
    for each in small:
        each.wait()
    own[0:32, :] = dst[...].astype(F32)
    own[48:56, :] = jnp.zeros((8, WIDTH), F32)
    for offset in range(NB):
        own[48 + offset : 49 + offset, 0:TILES] = pattern[offset].astype(F32)
    first, last = fluid[0:64, :], fluid[960:1024, :]
    for index, face in ((0, jnp.where(parity == 0, last, first)), (1, jnp.where(parity == 0, first, last))):
        packed[index, 0:56, :] = own[...]
        packed[index, 56:120, :] = face
    tail_in = copy(packed.at[0], on_chip_hbm.at[6 * TILE_ROWS : 6 * TILE_ROWS + SMALL], 14)
    tail_out = copy(packed.at[1], across_hbm.at[2 * TILE_ROWS : 2 * TILE_ROWS + SMALL], 15)
    y, z = lax.axis_index("gy"), lax.axis_index("gz")
    after_y, before_y = lax.rem(y + 1, 4) * 4 + z, lax.rem(y + 3, 4) * 4 + z
    for slab in range(16):
        at = slice(128 * slab, 128 * slab + 128)
        faces[before_y, :, at] = fluid[64 * slab : 64 * slab + 1, :]
        faces[after_y, :, at] = fluid[64 * slab + 63 : 64 * slab + 64, :]
    load_src.wait()
    group = 4
    for start in range(0, RUNS, group):
        if start == RUNS // 2:
            inside.wait()
            outside.wait()
            inside = copy(staged_in, on_chip_hbm.at[0 : 6 * TILE_ROWS], 17)
            outside = copy(staged_out, across_hbm.at[0 : 2 * TILE_ROWS], 18)
        ids = lanes([src[r : r + 1, :] for r in range(start, start + group)])
        picked = jnp.dot(table[...], row_hots(ids >> 7, ROWS), preferred_element_type=F32)
        both = picked[0:128] + picked[128:256]
        mask = lax.broadcasted_iota(I32, (WIDTH, group * WIDTH), 0) == (ids & 127)
        value = jnp.sum(jnp.where(mask, both, 0.0), axis=0, keepdims=True)
        for r in range(start, start + group):
            mine = value[:, (r - start) * WIDTH : (r - start + 1) * WIDTH]
            outgoing[r : r + 1, :] = mine
            sent[r, :, 0:128] = mine
            sent[r ^ 1, :, 128:256] = mine
            beside = (r + 1) % RUNS if r % 2 else (r - 1) % RUNS
            sent[beside, :, 256:384] = mine
    for each in (inside, outside, tail_in, tail_out):
        each.wait()


def spread_run(ids_of, values_of):
    group = 8
    total = None
    for start in range(0, RUNS, group):
        cell = lanes([ids_of(r) for r in range(start, start + group)])
        value = lanes([values_of(r) for r in range(start, start + group)])
        row = jnp.where(cell >= 0, ((cell >> 5) & 3) * 8 + (cell >> 7), -1)
        hots = row_hots(row, 32)
        placed = placed_parts(cell & 31, 32, value)
        added = lax.dot_general(hots, placed, CONTRACT_LAST, preferred_element_type=F32)
        total = added if total is None else total + added
    total = total[:, 0:32] + total[:, 32:64]
    return lanes([total[8 * u : 8 * u + 8, :] for u in range(4)])


def window(parity, own, partner, beside):
    pad = jnp.zeros((4, own.shape[1]), F32)
    low = jnp.concatenate([beside[4:8], own, partner, pad], axis=0)
    high = jnp.concatenate([partner, own, beside[0:4], pad], axis=0)
    return jnp.where(parity == 0, low, high)


def neighbours(iterate, pats, first, count, shifted):
    for offset in range(NB):
        values = iterate[first - 2 + offset : first - 2 + offset + count, :]
        shifted[offset, first : first + count, :] = values * pats[offset, first : first + count, :]


def apply_tile(blocks, tile, shifted, place, coupled):
    total = None
    for offset in range(NB):
        start = pl.multiple_of(tile * TILE_ROWS + offset * WIDTH, WIDTH)
        term = blocks[pl.ds(start, WIDTH), :] * shifted[offset, pl.ds(place, 1), :]
        total = term if total is None else total + term
    coupled[pl.ds(place, 1), :] = jnp.sum(total.T, axis=0, keepdims=True)


RHO = [0.5]
for _ in range(3):
    RHO.append(1.0 / (4.0 - RHO[-1]))


def stepped(sweep, value, update, right, inverse, diagonal, coupled):
    residual = right - (diagonal * value + coupled)
    if sweep == 0:
        update = inverse * residual
    else:
        update = RHO[sweep] * RHO[sweep - 1] * update + 4.0 * RHO[sweep] * inverse * residual
    return value + update, update


def own_run_kernel(arrived, dst, added):
    added[...] = spread_run(lambda r: dst[r : r + 1, :], lambda r: arrived[r, :, 0:128])


def beside_run_kernel(arrived, across_hbm, added_own, added, small, sem):
    load = pltpu.make_async_copy(across_hbm.at[2 * TILE_ROWS : 2 * TILE_ROWS + SMALL], small, sem)
    load.start()
    added[0:TILES, :] = added_own[...]
    load.wait()
    added[TILES : 2 * TILES, :] = spread_run(
        lambda r: small[r : r + 1, :].astype(I32), lambda r: arrived[r, :, 256:384]
    )


def windows(parity, keep, own, partner, beside, added):
    holders = [own, partner, beside]
    diagonals = [each[40:48] for each in holders]
    rights = [d * each[32:40] + a for d, each, a in zip(diagonals, holders, added)]
    inverses = [1.0 / d for d in diagonals]
    rights[2], inverses[2] = rights[2] * keep, inverses[2] * keep
    present = window(parity, *[each[48:56].T[0:TILES] for each in holders])
    return window(parity, *rights), window(parity, *inverses), window(parity, *diagonals), present


def wall_edge_kernel(
    added_before, beside_small, own, own_blocks, across_hbm,
    products, swap,
    outer, pats, iterate, shifted, coupled, sem,
):
    load = pltpu.make_async_copy(across_hbm.at[0 : 2 * TILE_ROWS], outer, sem)
    load.start()
    me = lax.axis_index("gx")
    parity = lax.rem(me, 2)
    keep = jnp.where((me == 0) | (me == RUNS - 1), 0.0, 1.0)
    mine = own[...]
    added = [added_before[0:TILES, :], jnp.zeros((TILES, WIDTH), F32), added_before[TILES : 2 * TILES, :]]
    right, inverse, diagonal, present = windows(parity, keep, mine, mine, beside_small[...], added)
    for offset in range(NB):
        pats[offset] = jnp.broadcast_to(present[:, offset : offset + 1], (WIN, WIDTH))
    value = inverse * right
    iterate[...] = value
    shifted[...] = jnp.zeros((NB, WIN, WIDTH), F32)
    coupled[...] = jnp.zeros((WIN, WIDTH), F32)
    own_at = 4 + 4 * parity
    neighbours(iterate, pats, 2, 16, shifted)
    for index in range(6):
        tile = index + 2 * parity
        apply_tile(own_blocks, tile, shifted, own_at + tile, coupled)
    load.wait()
    for index in range(2):
        apply_tile(outer, index, shifted, 2 + 14 * parity + index, coupled)
    products[0] = coupled[...]
    value, update = stepped(0, value, None, right, inverse, diagonal, coupled[...])
    iterate[...] = value
    neighbours(iterate, pats, 4, 12, shifted)
    for index in range(4):
        tile = index + 4 * parity
        apply_tile(own_blocks, tile, shifted, own_at + tile, coupled)
    products[1] = coupled[...]
    value, update = stepped(1, value, update, right, inverse, diagonal, coupled[...])
    swap[0:4, :] = jnp.where(parity == 0, value[4:8], value[12:16])
    swap[4:8, :] = jnp.where(parity == 0, update[4:8], update[12:16])


def wall_inner_kernel(
    arrived, added_before, beside_small, own, products, own_blocks, on_chip_hbm,
    state, pats, inside, faces,
    inner, iterate, shifted, coupled, sems,
):
    at_in = 6 * TILE_ROWS
    loads = [
        pltpu.make_async_copy(on_chip_hbm.at[low:high], inner.at[low:high], sems.at[index])
        for index, (low, high) in enumerate(((at_in, at_in + SMALL), (0, at_in)))
    ]
    for each in loads:
        each.start()
    me = lax.axis_index("gx")
    parity = lax.rem(me, 2)
    keep = jnp.where((me == 0) | (me == RUNS - 1), 0.0, 1.0)
    loads[0].wait()
    partner, beside = inner[at_in : at_in + SMALL, :], beside_small[...]
    added = [
        added_before[0:TILES, :],
        spread_run(lambda r: inner[at_in + r : at_in + r + 1, :].astype(I32), lambda r: arrived[r, :, 128:256]),
        added_before[TILES : 2 * TILES, :],
    ]
    right, inverse, diagonal, present = windows(parity, keep, own[...], partner, beside, added)
    for offset in range(NB):
        pats[offset] = jnp.broadcast_to(present[:, offset : offset + 1], (WIN, WIDTH))
    faces[0] = jnp.where(parity == 0, beside[56:120], partner[56:120])
    faces[1] = jnp.where(parity == 0, partner[56:120], beside[56:120])
    place = lax.broadcasted_iota(I32, (WIN, WIDTH), 0)
    value = inverse * right
    iterate[...] = value
    shifted[...] = jnp.zeros((NB, WIN, WIDTH), F32)
    coupled[...] = jnp.zeros((WIN, WIDTH), F32)
    own_at = 4 + 4 * parity

    neighbours(iterate, pats, 2, 16, shifted)
    for index in range(2):
        tile = index + 6 - 6 * parity
        apply_tile(own_blocks, tile, shifted, own_at + tile, coupled)
    loads[1].wait()
    for index in range(6):
        apply_tile(inner, index, shifted, 12 - 10 * parity + index, coupled)
    low = 2 + 8 * parity
    product = jnp.where((place >= low) & (place < low + 8), products[0], coupled[...])
    value, update = stepped(0, value, None, right, inverse, diagonal, product)
    iterate[...] = value

    neighbours(iterate, pats, 4, 12, shifted)
    for index in range(4):
        tile = index + 4 - 4 * parity
        apply_tile(own_blocks, tile, shifted, own_at + tile, coupled)
    for index in range(4):
        apply_tile(inner, index + 2 * parity, shifted, 12 - 8 * parity + index, coupled)
    low = 4 + 8 * parity
    product = jnp.where((place >= low) & (place < low + 4), products[1], coupled[...])
    value, update = stepped(1, value, update, right, inverse, diagonal, product)
    state[0], state[1], state[2], state[3], state[4] = value, update, right, inverse, diagonal
    iterate[...] = value

    neighbours(iterate, pats, 6, 8, shifted)
    for index in range(6):
        tile = index + 2 - 2 * parity
        apply_tile(own_blocks, tile, shifted, own_at + tile, coupled)
    for index in range(2):
        apply_tile(inner, index + 4 * parity, shifted, 12 - 6 * parity + index, coupled)
    value, update = stepped(2, value, update, right, inverse, diagonal, coupled[...])
    inside[0], inside[1] = value, update
    iterate[...] = value
    neighbours(iterate, pats, 8, 4, shifted)
    for index in range(4):
        tile = index + 4 - 4 * parity
        apply_tile(own_blocks, tile, shifted, own_at + tile, coupled)
    inside[2] = coupled[...]


def wall_last_kernel(
    state, pats, inside, swapped, own, own_blocks, across_hbm,
    solid, returned, outer, iterate, shifted, coupled, sem,
):
    load = pltpu.make_async_copy(across_hbm.at[0 : 2 * TILE_ROWS], outer, sem)
    load.start()
    me = lax.axis_index("gx")
    parity = lax.rem(me, 2)
    keep = jnp.where((me == 0) | (me == RUNS - 1), 0.0, 1.0)
    value, update, right, inverse, diagonal = (state[i] for i in range(5))

    def with_swapped(inside, outside):
        low = jnp.concatenate([outside, inside[4:24]], axis=0)
        high = jnp.concatenate([inside[0:16], outside, inside[20:24]], axis=0)
        return jnp.where(parity == 0, low, high)

    value = with_swapped(value, swapped[0:4, :] * keep)
    update = with_swapped(update, swapped[4:8, :] * keep)
    place = lax.broadcasted_iota(I32, (WIN, WIDTH), 0)
    own_at = 4 + 4 * parity
    iterate[...] = value
    shifted[...] = jnp.zeros((NB, WIN, WIDTH), F32)
    coupled[...] = jnp.zeros((WIN, WIDTH), F32)
    neighbours(iterate, pats, 2, 16, shifted)
    for index in range(2):
        tile = index + 6 * parity
        apply_tile(own_blocks, tile, shifted, own_at + tile, coupled)
    load.wait()
    for index in range(2):
        apply_tile(outer, index, shifted, 2 + 14 * parity + index, coupled)
    value, update = stepped(2, value, update, right, inverse, diagonal, coupled[...])
    known = (place >= 6) & (place < 14)
    value, update = jnp.where(known, inside[0], value), jnp.where(known, inside[1], update)
    iterate[...] = value
    neighbours(iterate, pats, 4, 12, shifted)
    for index in range(4):
        tile = index + 4 * parity
        apply_tile(own_blocks, tile, shifted, own_at + tile, coupled)
    product = jnp.where((place >= 8) & (place < 12), inside[2], coupled[...])
    value, update = stepped(3, value, update, right, inverse, diagonal, product)
    mine = jnp.where(parity == 0, value[4:12], value[8:16])
    solid[...] = mine
    for block in range(4):
        cell = own[8 * block : 8 * block + 8, :].astype(I32)
        tile, lane = cell >> 7, cell & 127
        found = jnp.zeros((8, WIDTH), F32)
        for index in range(TILES):
            row = jnp.broadcast_to(mine[index : index + 1, :], (8, WIDTH))
            found = jnp.where(tile == index, jnp.take_along_axis(row, lane, axis=1, mode="promise_in_bounds"), found)
        for r in range(8):
            returned[8 * block + r] = found[r : r + 1, :]


def final_kernel(fluid, liquid, x_faces, faces, src, outgoing, returned, fluid_new):
    group = 4
    total = None
    for start in range(0, RUNS, group):
        rows = range(start, start + group)
        ids = lanes([src[r : r + 1, :] for r in rows])
        value = lanes([returned[r] - outgoing[r : r + 1, :] for r in rows])
        placed = placed_parts(ids & 127, WIDTH, value)
        added = lax.dot_general(row_hots(ids >> 7, ROWS), placed, CONTRACT_LAST, preferred_element_type=F32)
        total = added if total is None else total + added
    wall = total[:, 0:128] + total[:, 128:256]
    y, z = lax.axis_index("gy"), lax.axis_index("gz")
    after_y, before_y = lax.rem(y + 1, 4) * 4 + z, lax.rem(y + 3, 4) * 4 + z
    after_z, before_z = y * 4 + lax.rem(z + 1, 4), y * 4 + lax.rem(z + 3, 4)
    row = lax.broadcasted_iota(I32, (64, WIDTH), 0)
    lane = lax.broadcasted_iota(I32, (64, WIDTH), 1)
    for slab in range(16):
        start = 64 * slab
        at, at_z = slice(128 * slab, 128 * slab + 128), slice(128 * (slab // 2), 128 * (slab // 2) + 128)
        here = fluid[start : start + 64, :]
        total = (fluid[start - 64 : start, :] if slab else x_faces[0]) + (
            fluid[start + 64 : start + 128, :] if slab < 15 else x_faces[1]
        )
        total = total + jnp.where(row == 0, faces[before_y, :, at], pltpu.roll(here, 1, 0))
        total = total + jnp.where(row == 63, faces[after_y, :, at], pltpu.roll(here, 63, 0))
        half = 64 * (slab % 2)
        left = jnp.broadcast_to(faces[before_z, :, at_z], (WIDTH, WIDTH)).T[half : half + 64, :]
        right = jnp.broadcast_to(faces[after_z, :, at_z], (WIDTH, WIDTH)).T[half : half + 64, :]
        total = total + jnp.where(lane == 0, left, pltpu.roll(here, 1, 1))
        total = total + jnp.where(lane == 127, right, pltpu.roll(here, 127, 1))
        total = total - 6.0 * here
        share = liquid[start : start + 64, :].astype(F32)
        fluid_new[start : start + 64, :] = (
            here
            + DIFFUSION * total
            - EVAPORATION * share * jnp.maximum(here - SATURATION, 0.0)
            + WALL_COUPLING * wall[start : start + 64, :]
        )


def shape(*dims):
    return jax.ShapeDtypeStruct(dims, F32)


def call(kernel, mib, ins, outs, out_specs, scratch, flops, moved):
    return pl.pallas_call(
        kernel,
        in_specs=ins,
        out_shape=outs,
        out_specs=out_specs,
        scratch_shapes=scratch,
        compiler_params=params(mib),
        cost_estimate=pl.CostEstimate(flops=flops, bytes_accessed=moved, transcendentals=0),
    )


def vmem(*dims, kind=F32):
    return pltpu.VMEM(dims, kind)


def dma(*dims):
    return pltpu.SemaphoreType.DMA(dims) if dims else pltpu.SemaphoreType.DMA


def per_device(fluid_temp, liquid, face_src, face_dst, solid_old, solid_diag, blocks, pattern):
    inside_pairs = [(i, i ^ 1) for i in range(RUNS)]
    outside_pairs = [(i, (i - 1) % RUNS if i % 2 == 0 else (i + 1) % RUNS) for i in range(RUNS)]
    fluid = fluid_temp.reshape(ROWS, WIDTH)
    src = face_src.reshape(RUNS, WIDTH)
    dst = face_dst.reshape(RUNS, WIDTH)
    own_blocks = blocks.reshape(TILES * TILE_ROWS, WIDTH)
    in_rows, out_rows = 6 * TILE_ROWS + SMALL, 2 * TILE_ROWS + SMALL

    sent, outgoing, own, faces, on_chip, across = call(
        pick_kernel, 60,
        [HBM] * 7,
        (
            shape(RUNS, 1, 384), shape(RUNS, WIDTH), shape(56, WIDTH), shape(16, 1, 2048),
            shape(in_rows, WIDTH), shape(out_rows, WIDTH),
        ),
        (VMEM, VMEM, VMEM, VMEM, HBM, HBM),
        [
            vmem(ROWS, WIDTH), vmem(RUNS, WIDTH, kind=I32), vmem(RUNS, WIDTH, kind=I32), vmem(NB, 1, TILES, kind=I32),
            vmem(256, ROWS, kind=BF16), vmem(2, SMALL, WIDTH), vmem(6 * TILE_ROWS, WIDTH), vmem(2 * TILE_ROWS, WIDTH), dma(19),
        ],
        2 * 256 * 1024 * 4096, 1 << 22,
    )(fluid, src, dst, solid_old[0], solid_diag[0], jnp.transpose(pattern, (2, 0, 1)), own_blocks)

    arrived = lax.all_to_all(sent, "gx", split_axis=0, concat_axis=0, tiled=True)
    on_chip = lax.ppermute(on_chip, "gx", inside_pairs)
    across = lax.ppermute(across, "gx", outside_pairs)
    faces = lax.all_to_all(faces, ("gy", "gz"), split_axis=0, concat_axis=0, tiled=True)

    work = [vmem(WIN, WIDTH), vmem(NB, WIN, WIDTH), vmem(WIN, WIDTH)]
    added_own = call(
        own_run_kernel, 12, [VMEM, VMEM], shape(TILES, WIDTH), VMEM, [], 65 * 10**8, 1 << 16
    )(arrived, dst)
    added_before, beside_small = call(
        beside_run_kernel, 12, [VMEM, ANY, VMEM], (shape(2 * TILES, WIDTH), shape(SMALL, WIDTH)), (VMEM, VMEM), [dma()],
        14 * 10**9, 1 << 16,
    )(arrived, across, added_own)
    products, swap = call(
        wall_edge_kernel, 12,
        [VMEM] * 4 + [ANY],
        (shape(2, WIN, WIDTH), shape(8, WIDTH)), (VMEM, VMEM),
        [vmem(2 * TILE_ROWS, WIDTH), vmem(NB, WIN, WIDTH)] + work + [dma()],
        1 << 23, 4 << 20,
    )(added_before, beside_small, own, own_blocks, across)
    swapped = lax.ppermute(swap, "gx", outside_pairs)
    state, pats, inside, x_faces = call(
        wall_inner_kernel, 16,
        [VMEM] * 6 + [ANY],
        (shape(5, WIN, WIDTH), shape(NB, WIN, WIDTH), shape(3, WIN, WIDTH), shape(2, 64, WIDTH)), (VMEM,) * 4,
        [vmem(in_rows, WIDTH)] + work + [dma(2)],
        1 << 24, 6 << 20,
    )(arrived, added_before, beside_small, own, products, own_blocks, on_chip)
    solid, sent_back = call(
        wall_last_kernel, 12,
        [VMEM] * 6 + [ANY],
        (shape(TILES, WIDTH), shape(RUNS, 1, WIDTH)), (VMEM, VMEM),
        [vmem(2 * TILE_ROWS, WIDTH)] + work + [dma()],
        1 << 23, 3 << 20,
    )(state, pats, inside, swapped, own, own_blocks, across)
    returned = lax.all_to_all(sent_back, "gx", split_axis=0, concat_axis=0, tiled=True)

    fluid_new = call(
        final_kernel, 16, [VMEM] * 7, shape(ROWS, WIDTH), VMEM, [], 2 * 256 * 1024 * 4096, 1 << 20
    )(fluid, liquid.reshape(ROWS, WIDTH), x_faces, faces, src, outgoing, returned)
    return fluid_new.reshape(fluid_temp.shape), solid[None]


def solution(mesh):
    return jax.shard_map(
        per_device,
        mesh=mesh,
        in_specs=(
            P("gx", "gy", "gz"),
            P("gx", "gy", "gz"),
            P("gx", "gy", "gz", None),
            P("gx", "gy", "gz", None),
            P(("gy", "gz"), "gx", None),
            P(("gy", "gz"), "gx", None),
            P(("gy", "gz"), "gx", None, None, None),
            P(("gy", "gz"), "gx", None),
        ),
        out_specs=(P("gx", "gy", "gz"), P(("gy", "gz"), "gx", None)),
        check_vma=False,
    )
```

```python
import jax
import jax.numpy as jnp
from jax import lax
from jax.experimental import pallas as pl
from jax.experimental.pallas import tpu as pltpu
from jax.sharding import PartitionSpec as P

F32 = jnp.float32
BF16 = jnp.bfloat16
I32 = jnp.int32
RUNS = 32
WIDTH = 128
ROWS = 1024
TILES = 8
NB = 5
WIN = 24
TILE_ROWS = NB * WIDTH
SMALL = 120

DIFFUSION = 0.12
EVAPORATION = 0.5
SATURATION = 0.25
WALL_COUPLING = 0.2

VMEM = pl.BlockSpec(memory_space=pltpu.VMEM)
HBM = pl.BlockSpec(memory_space=pltpu.HBM)
ANY = pl.BlockSpec(memory_space=pl.ANY)


def params(mib):
    return pltpu.CompilerParams(vmem_limit_bytes=mib << 20)


def two_parts(values):
    high = values.astype(BF16)
    return high, (values - high.astype(F32)).astype(BF16)


def lanes(rows):
    return jnp.concatenate(rows, axis=1)


def row_hots(row, count):
    width = row.shape[1]
    part = min(count, 256)
    level = lax.broadcasted_iota(I32, (part, width), 0).astype(F32).astype(BF16)
    one, zero = jnp.ones((), BF16), jnp.zeros((), BF16)
    parts = []
    for index in range(count // part):
        here = jnp.where((row >= index * part) & (row < (index + 1) * part), row - index * part, -1)
        parts.append(jnp.where(level == here.astype(F32).astype(BF16), one, zero))
    return parts[0] if len(parts) == 1 else jnp.concatenate(parts, axis=0)


def placed_parts(column, count, values):
    width = column.shape[1]
    mask = lax.broadcasted_iota(I32, (count, width), 0) == column
    high = values.astype(BF16).astype(F32)
    low = values - high
    both = [jnp.where(mask, part, 0.0) for part in (high, low)]
    return jnp.concatenate(both, axis=0).astype(BF16)


CONTRACT_LAST = (((1,), (1,)), ((), ()))


def pick_kernel(
    fluid_hbm, src_hbm, dst_hbm, old_hbm, diag_hbm, pattern_hbm, blocks_hbm,
    sent, outgoing, own, faces, on_chip_hbm, across_hbm,
    fluid, src, dst, pattern, table, staged_in, staged_out, sems,
):
    me = lax.axis_index("gx")
    parity = lax.rem(me, 2)

    def copy(source, target, index):
        started = pltpu.make_async_copy(source, target, sems.at[index])
        started.start()
        return started

    load_fluid = copy(fluid_hbm, fluid, 0)
    load_src = copy(src_hbm, src, 8)
    small = [
        copy(dst_hbm, dst, 9),
        copy(old_hbm, own.at[32:40], 10),
        copy(diag_hbm, own.at[40:48], 11),
        copy(pattern_hbm, pattern, 16),
    ]
    inside = copy(blocks_hbm.at[pl.ds((1 - parity) * 2 * TILE_ROWS, 6 * TILE_ROWS)], staged_in.at[0 : 6 * TILE_ROWS], 12)
    outside = copy(blocks_hbm.at[pl.ds(parity * 6 * TILE_ROWS, 2 * TILE_ROWS)], staged_out.at[0 : 2 * TILE_ROWS], 13)
    before_z = lax.axis_index("gy") * 4 + lax.rem(lax.axis_index("gz") + 3, 4)
    after_z = lax.axis_index("gy") * 4 + lax.rem(lax.axis_index("gz") + 1, 4)
    load_fluid.wait()
    for block in range(8):
        turned = fluid[128 * block : 128 * block + 128, :].T
        high, low = two_parts(turned)
        table[0:128, 128 * block : 128 * block + 128] = high
        table[128:256, 128 * block : 128 * block + 128] = low
        at = slice(128 * block, 128 * block + 128)
        faces[before_z, :, at] = turned[0:1, :]
        faces[after_z, :, at] = turned[127:128, :]
    for each in small:
        each.wait()
    own[0:32, :] = dst[...].astype(F32)
    own[48:56, :] = jnp.zeros((8, WIDTH), F32)
    for offset in range(NB):
        own[48 + offset : 49 + offset, 0:TILES] = pattern[offset].astype(F32)
    first, last = fluid[0:64, :], fluid[960:1024, :]
    for packed, start, face in (
        (staged_in, 6 * TILE_ROWS, jnp.where(parity == 0, last, first)),
        (staged_out, 2 * TILE_ROWS, jnp.where(parity == 0, first, last)),
    ):
        packed[start : start + 56, :] = own[...]
        packed[start + 56 : start + SMALL, :] = face
    y, z = lax.axis_index("gy"), lax.axis_index("gz")
    after_y, before_y = lax.rem(y + 1, 4) * 4 + z, lax.rem(y + 3, 4) * 4 + z
    for slab in range(16):
        at = slice(128 * slab, 128 * slab + 128)
        faces[before_y, :, at] = fluid[64 * slab : 64 * slab + 1, :]
        faces[after_y, :, at] = fluid[64 * slab + 63 : 64 * slab + 64, :]
    load_src.wait()
    group = 4
    for start in range(0, RUNS, group):
        if start == RUNS // 2:
            inside.wait()
            outside.wait()
            inside = copy(staged_in, on_chip_hbm, 17)
            outside = copy(staged_out, across_hbm, 18)
        ids = lanes([src[r : r + 1, :] for r in range(start, start + group)])
        picked = jnp.dot(table[...], row_hots(ids >> 7, ROWS), preferred_element_type=F32)
        both = picked[0:128] + picked[128:256]
        mask = lax.broadcasted_iota(I32, (WIDTH, group * WIDTH), 0) == (ids & 127)
        value = jnp.sum(jnp.where(mask, both, 0.0), axis=0, keepdims=True)
        for r in range(start, start + group):
            mine = value[:, (r - start) * WIDTH : (r - start + 1) * WIDTH]
            outgoing[r : r + 1, :] = mine
            sent[r, :, 0:128] = mine
            sent[r ^ 1, :, 128:256] = mine
            beside = (r + 1) % RUNS if r % 2 else (r - 1) % RUNS
            sent[beside, :, 256:384] = mine
    for each in (inside, outside):
        each.wait()


def spread_run(ids_of, values_of):
    group = 8
    total = None
    for start in range(0, RUNS, group):
        cell = lanes([ids_of(r) for r in range(start, start + group)])
        value = lanes([values_of(r) for r in range(start, start + group)])
        row = jnp.where(cell >= 0, ((cell >> 5) & 3) * 8 + (cell >> 7), -1)
        hots = row_hots(row, 32)
        placed = placed_parts(cell & 31, 32, value)
        added = lax.dot_general(hots, placed, CONTRACT_LAST, preferred_element_type=F32)
        total = added if total is None else total + added
    total = total[:, 0:32] + total[:, 32:64]
    return lanes([total[8 * u : 8 * u + 8, :] for u in range(4)])


def window(parity, own, partner, beside):
    pad = jnp.zeros((4, own.shape[1]), F32)
    low = jnp.concatenate([beside[4:8], own, partner, pad], axis=0)
    high = jnp.concatenate([partner, own, beside[0:4], pad], axis=0)
    return jnp.where(parity == 0, low, high)


def neighbours(iterate, pats, first, count, shifted):
    for offset in range(NB):
        values = iterate[first - 2 + offset : first - 2 + offset + count, :]
        shifted[offset, first : first + count, :] = values * pats[offset, first : first + count, :]


def apply_tile(blocks, tile, shifted, place, coupled):
    total = None
    for offset in range(NB):
        start = pl.multiple_of(tile * TILE_ROWS + offset * WIDTH, WIDTH)
        term = blocks[pl.ds(start, WIDTH), :] * shifted[offset, pl.ds(place, 1), :]
        total = term if total is None else total + term
    coupled[pl.ds(place, 1), :] = jnp.sum(total.T, axis=0, keepdims=True)


RHO = [0.5]
for _ in range(3):
    RHO.append(1.0 / (4.0 - RHO[-1]))


def stepped(sweep, value, update, right, inverse, diagonal, coupled):
    residual = right - (diagonal * value + coupled)
    if sweep == 0:
        update = inverse * residual
    else:
        update = RHO[sweep] * RHO[sweep - 1] * update + 4.0 * RHO[sweep] * inverse * residual
    return value + update, update


def own_run_kernel(arrived, dst, added):
    added[...] = spread_run(lambda r: dst[r : r + 1, :], lambda r: arrived[r, :, 0:128])


def beside_run_kernel(arrived, across_hbm, added_own, added, small, sem):
    load = pltpu.make_async_copy(across_hbm.at[2 * TILE_ROWS : 2 * TILE_ROWS + SMALL], small, sem)
    load.start()
    added[0:TILES, :] = added_own[...]
    load.wait()
    added[TILES : 2 * TILES, :] = spread_run(
        lambda r: small[r : r + 1, :].astype(I32), lambda r: arrived[r, :, 256:384]
    )


def load_kernel(after, blocks_hbm, blocks, sem):
    load = pltpu.make_async_copy(blocks_hbm, blocks, sem)
    load.start()
    load.wait()


def windows(parity, keep, own, partner, beside, added):
    holders = [own, partner, beside]
    diagonals = [each[40:48] for each in holders]
    rights = [d * each[32:40] + a for d, each, a in zip(diagonals, holders, added)]
    inverses = [1.0 / d for d in diagonals]
    rights[2], inverses[2] = rights[2] * keep, inverses[2] * keep
    present = window(parity, *[each[48:56].T[0:TILES] for each in holders])
    return window(parity, *rights), window(parity, *inverses), window(parity, *diagonals), present


def wall_edge_kernel(
    added_before, beside_small, own, own_blocks, across_hbm,
    products, swap,
    outer, pats, iterate, shifted, coupled, sem,
):
    load = pltpu.make_async_copy(across_hbm.at[0 : 2 * TILE_ROWS], outer, sem)
    load.start()
    me = lax.axis_index("gx")
    parity = lax.rem(me, 2)
    keep = jnp.where((me == 0) | (me == RUNS - 1), 0.0, 1.0)
    mine = own[...]
    added = [added_before[0:TILES, :], jnp.zeros((TILES, WIDTH), F32), added_before[TILES : 2 * TILES, :]]
    right, inverse, diagonal, present = windows(parity, keep, mine, mine, beside_small[...], added)
    for offset in range(NB):
        pats[offset] = jnp.broadcast_to(present[:, offset : offset + 1], (WIN, WIDTH))
    value = inverse * right
    iterate[...] = value
    shifted[...] = jnp.zeros((NB, WIN, WIDTH), F32)
    coupled[...] = jnp.zeros((WIN, WIDTH), F32)
    own_at = 4 + 4 * parity
    neighbours(iterate, pats, 2, 16, shifted)
    for index in range(6):
        tile = index + 2 * parity
        apply_tile(own_blocks, tile, shifted, own_at + tile, coupled)
    load.wait()
    for index in range(2):
        apply_tile(outer, index, shifted, 2 + 14 * parity + index, coupled)
    products[0] = coupled[...]
    value, update = stepped(0, value, None, right, inverse, diagonal, coupled[...])
    iterate[...] = value
    neighbours(iterate, pats, 4, 12, shifted)
    for index in range(4):
        tile = index + 4 * parity
        apply_tile(own_blocks, tile, shifted, own_at + tile, coupled)
    products[1] = coupled[...]
    value, update = stepped(1, value, update, right, inverse, diagonal, coupled[...])
    swap[0:4, :] = jnp.where(parity == 0, value[4:8], value[12:16])
    swap[4:8, :] = jnp.where(parity == 0, update[4:8], update[12:16])


def wall_inner_kernel(
    arrived, added_before, beside_small, own, products, own_blocks, on_chip_hbm,
    state, pats, inside, faces,
    inner, iterate, shifted, coupled, sems,
):
    at_in = 6 * TILE_ROWS
    loads = [
        pltpu.make_async_copy(on_chip_hbm.at[low:high], inner.at[low:high], sems.at[index])
        for index, (low, high) in enumerate(((at_in, at_in + SMALL), (0, at_in)))
    ]
    for each in loads:
        each.start()
    me = lax.axis_index("gx")
    parity = lax.rem(me, 2)
    keep = jnp.where((me == 0) | (me == RUNS - 1), 0.0, 1.0)
    loads[0].wait()
    partner, beside = inner[at_in : at_in + SMALL, :], beside_small[...]
    added = [
        added_before[0:TILES, :],
        spread_run(lambda r: inner[at_in + r : at_in + r + 1, :].astype(I32), lambda r: arrived[r, :, 128:256]),
        added_before[TILES : 2 * TILES, :],
    ]
    right, inverse, diagonal, present = windows(parity, keep, own[...], partner, beside, added)
    for offset in range(NB):
        pats[offset] = jnp.broadcast_to(present[:, offset : offset + 1], (WIN, WIDTH))
    faces[0] = jnp.where(parity == 0, beside[56:120], partner[56:120])
    faces[1] = jnp.where(parity == 0, partner[56:120], beside[56:120])
    place = lax.broadcasted_iota(I32, (WIN, WIDTH), 0)
    value = inverse * right
    iterate[...] = value
    shifted[...] = jnp.zeros((NB, WIN, WIDTH), F32)
    coupled[...] = jnp.zeros((WIN, WIDTH), F32)
    own_at = 4 + 4 * parity

    neighbours(iterate, pats, 2, 16, shifted)
    for index in range(2):
        tile = index + 6 - 6 * parity
        apply_tile(own_blocks, tile, shifted, own_at + tile, coupled)
    loads[1].wait()
    for index in range(6):
        apply_tile(inner, index, shifted, 12 - 10 * parity + index, coupled)
    low = 2 + 8 * parity
    product = jnp.where((place >= low) & (place < low + 8), products[0], coupled[...])
    value, update = stepped(0, value, None, right, inverse, diagonal, product)
    iterate[...] = value

    neighbours(iterate, pats, 4, 12, shifted)
    for index in range(4):
        tile = index + 4 - 4 * parity
        apply_tile(own_blocks, tile, shifted, own_at + tile, coupled)
    for index in range(4):
        apply_tile(inner, index + 2 * parity, shifted, 12 - 8 * parity + index, coupled)
    low = 4 + 8 * parity
    product = jnp.where((place >= low) & (place < low + 4), products[1], coupled[...])
    value, update = stepped(1, value, update, right, inverse, diagonal, product)
    state[0], state[1], state[2], state[3], state[4] = value, update, right, inverse, diagonal
    iterate[...] = value

    neighbours(iterate, pats, 6, 8, shifted)
    for index in range(6):
        tile = index + 2 - 2 * parity
        apply_tile(own_blocks, tile, shifted, own_at + tile, coupled)
    for index in range(2):
        apply_tile(inner, index + 4 * parity, shifted, 12 - 6 * parity + index, coupled)
    value, update = stepped(2, value, update, right, inverse, diagonal, coupled[...])
    inside[0], inside[1] = value, update
    iterate[...] = value
    neighbours(iterate, pats, 8, 4, shifted)
    for index in range(4):
        tile = index + 4 - 4 * parity
        apply_tile(own_blocks, tile, shifted, own_at + tile, coupled)
    inside[2] = coupled[...]


def wall_last_kernel(
    state, pats, inside, swapped, own, own_blocks, across_hbm,
    solid, returned, outer, iterate, shifted, coupled, sem,
):
    load = pltpu.make_async_copy(across_hbm.at[0 : 2 * TILE_ROWS], outer, sem)
    load.start()
    me = lax.axis_index("gx")
    parity = lax.rem(me, 2)
    keep = jnp.where((me == 0) | (me == RUNS - 1), 0.0, 1.0)
    value, update, right, inverse, diagonal = (state[i] for i in range(5))

    def with_swapped(inside, outside):
        low = jnp.concatenate([outside, inside[4:24]], axis=0)
        high = jnp.concatenate([inside[0:16], outside, inside[20:24]], axis=0)
        return jnp.where(parity == 0, low, high)

    value = with_swapped(value, swapped[0:4, :] * keep)
    update = with_swapped(update, swapped[4:8, :] * keep)
    place = lax.broadcasted_iota(I32, (WIN, WIDTH), 0)
    own_at = 4 + 4 * parity
    iterate[...] = value
    shifted[...] = jnp.zeros((NB, WIN, WIDTH), F32)
    coupled[...] = jnp.zeros((WIN, WIDTH), F32)
    neighbours(iterate, pats, 2, 16, shifted)
    for index in range(2):
        tile = index + 6 * parity
        apply_tile(own_blocks, tile, shifted, own_at + tile, coupled)
    load.wait()
    for index in range(2):
        apply_tile(outer, index, shifted, 2 + 14 * parity + index, coupled)
    value, update = stepped(2, value, update, right, inverse, diagonal, coupled[...])
    known = (place >= 6) & (place < 14)
    value, update = jnp.where(known, inside[0], value), jnp.where(known, inside[1], update)
    iterate[...] = value
    neighbours(iterate, pats, 4, 12, shifted)
    for index in range(4):
        tile = index + 4 * parity
        apply_tile(own_blocks, tile, shifted, own_at + tile, coupled)
    product = jnp.where((place >= 8) & (place < 12), inside[2], coupled[...])
    value, update = stepped(3, value, update, right, inverse, diagonal, product)
    mine = jnp.where(parity == 0, value[4:12], value[8:16])
    solid[...] = mine
    for block in range(4):
        cell = own[8 * block : 8 * block + 8, :].astype(I32)
        tile, lane = cell >> 7, cell & 127
        found = jnp.zeros((8, WIDTH), F32)
        for index in range(TILES):
            row = jnp.broadcast_to(mine[index : index + 1, :], (8, WIDTH))
            found = jnp.where(tile == index, jnp.take_along_axis(row, lane, axis=1, mode="promise_in_bounds"), found)
        for r in range(8):
            returned[8 * block + r] = found[r : r + 1, :]


def final_kernel(
    fluid_hbm, liquid_hbm, x_faces_hbm, faces, src, outgoing, returned,
    fluid_new,
    fluid, liquid, x_faces, sems,
):
    loads = [
        pltpu.make_async_copy(fluid_hbm, fluid, sems.at[0]),
        pltpu.make_async_copy(liquid_hbm, liquid, sems.at[1]),
        pltpu.make_async_copy(x_faces_hbm, x_faces, sems.at[2]),
    ]
    for each in loads:
        each.start()
    group = 4
    total = None
    for start in range(0, RUNS, group):
        rows = range(start, start + group)
        ids = lanes([src[r : r + 1, :] for r in rows])
        value = lanes([returned[r] - outgoing[r : r + 1, :] for r in rows])
        placed = placed_parts(ids & 127, WIDTH, value)
        added = lax.dot_general(row_hots(ids >> 7, ROWS), placed, CONTRACT_LAST, preferred_element_type=F32)
        total = added if total is None else total + added
    wall = total[:, 0:128] + total[:, 128:256]
    for each in loads:
        each.wait()
    y, z = lax.axis_index("gy"), lax.axis_index("gz")
    after_y, before_y = lax.rem(y + 1, 4) * 4 + z, lax.rem(y + 3, 4) * 4 + z
    after_z, before_z = y * 4 + lax.rem(z + 1, 4), y * 4 + lax.rem(z + 3, 4)
    row = lax.broadcasted_iota(I32, (64, WIDTH), 0)
    lane = lax.broadcasted_iota(I32, (64, WIDTH), 1)
    for slab in range(16):
        start = 64 * slab
        at, at_z = slice(128 * slab, 128 * slab + 128), slice(128 * (slab // 2), 128 * (slab // 2) + 128)
        here = fluid[start : start + 64, :]
        total = (fluid[start - 64 : start, :] if slab else x_faces[0]) + (
            fluid[start + 64 : start + 128, :] if slab < 15 else x_faces[1]
        )
        total = total + jnp.where(row == 0, faces[before_y, :, at], pltpu.roll(here, 1, 0))
        total = total + jnp.where(row == 63, faces[after_y, :, at], pltpu.roll(here, 63, 0))
        half = 64 * (slab % 2)
        left = jnp.broadcast_to(faces[before_z, :, at_z], (WIDTH, WIDTH)).T[half : half + 64, :]
        right = jnp.broadcast_to(faces[after_z, :, at_z], (WIDTH, WIDTH)).T[half : half + 64, :]
        total = total + jnp.where(lane == 0, left, pltpu.roll(here, 1, 1))
        total = total + jnp.where(lane == 127, right, pltpu.roll(here, 127, 1))
        total = total - 6.0 * here
        share = liquid[start : start + 64, :].astype(F32)
        fluid_new[start : start + 64, :] = (
            here
            + DIFFUSION * total
            - EVAPORATION * share * jnp.maximum(here - SATURATION, 0.0)
            + WALL_COUPLING * wall[start : start + 64, :]
        )


def shape(*dims):
    return jax.ShapeDtypeStruct(dims, F32)


def call(kernel, mib, ins, outs, out_specs, scratch, flops, moved):
    return pl.pallas_call(
        kernel,
        in_specs=ins,
        out_shape=outs,
        out_specs=out_specs,
        scratch_shapes=scratch,
        compiler_params=params(mib),
        cost_estimate=pl.CostEstimate(flops=flops, bytes_accessed=moved, transcendentals=0),
    )


def vmem(*dims, kind=F32):
    return pltpu.VMEM(dims, kind)


def dma(*dims):
    return pltpu.SemaphoreType.DMA(dims) if dims else pltpu.SemaphoreType.DMA


def in_hbm(array):
    return pltpu.with_memory_space_constraint(array, pltpu.HBM)


def per_device(fluid_temp, liquid, face_src, face_dst, solid_old, solid_diag, blocks, pattern):
    inside_pairs = [(i, i ^ 1) for i in range(RUNS)]
    outside_pairs = [(i, (i - 1) % RUNS if i % 2 == 0 else (i + 1) % RUNS) for i in range(RUNS)]
    fluid = fluid_temp.reshape(ROWS, WIDTH)
    src = face_src.reshape(RUNS, WIDTH)
    dst = face_dst.reshape(RUNS, WIDTH)
    own_blocks = blocks.reshape(TILES * TILE_ROWS, WIDTH)
    in_rows, out_rows = 6 * TILE_ROWS + SMALL, 2 * TILE_ROWS + SMALL

    sent, outgoing, own, faces, on_chip, across = call(
        pick_kernel, 60,
        [HBM] * 7,
        (
            shape(RUNS, 1, 384), shape(RUNS, WIDTH), shape(56, WIDTH), shape(16, 1, 2048),
            shape(in_rows, WIDTH), shape(out_rows, WIDTH),
        ),
        (VMEM, VMEM, VMEM, VMEM, HBM, HBM),
        [
            vmem(ROWS, WIDTH), vmem(RUNS, WIDTH, kind=I32), vmem(RUNS, WIDTH, kind=I32), vmem(NB, 1, TILES, kind=I32),
            vmem(256, ROWS, kind=BF16), vmem(in_rows, WIDTH), vmem(out_rows, WIDTH), dma(19),
        ],
        2 * 256 * 1024 * 4096, 1 << 22,
    )(fluid, src, dst, solid_old[0], solid_diag[0], jnp.transpose(pattern, (2, 0, 1)), own_blocks)

    arrived = lax.all_to_all(sent, "gx", split_axis=0, concat_axis=0, tiled=True)
    on_chip = lax.ppermute(on_chip, "gx", inside_pairs)
    across = lax.ppermute(across, "gx", outside_pairs)
    faces = lax.all_to_all(faces, ("gy", "gz"), split_axis=0, concat_axis=0, tiled=True)

    work = [vmem(WIN, WIDTH), vmem(NB, WIN, WIDTH), vmem(WIN, WIDTH)]
    added_own = call(
        own_run_kernel, 12, [VMEM, VMEM], shape(TILES, WIDTH), VMEM, [], 65 * 10**8, 1 << 16
    )(arrived, dst)
    added_before, beside_small = call(
        beside_run_kernel, 12, [VMEM, ANY, VMEM], (shape(2 * TILES, WIDTH), shape(SMALL, WIDTH)), (VMEM, VMEM), [dma()],
        14 * 10**9, 1 << 16,
    )(arrived, across, added_own)
    held_blocks = call(
        load_kernel, 12, [ANY, HBM], shape(TILES * TILE_ROWS, WIDTH), VMEM, [dma()], 1 << 10, 6 << 20
    )(own, in_hbm(own_blocks))
    products, swap = call(
        wall_edge_kernel, 12,
        [VMEM] * 4 + [ANY],
        (shape(2, WIN, WIDTH), shape(8, WIDTH)), (VMEM, VMEM),
        [vmem(2 * TILE_ROWS, WIDTH), vmem(NB, WIN, WIDTH)] + work + [dma()],
        1 << 23, 4 << 20,
    )(added_before, beside_small, own, held_blocks, across)
    swapped = lax.ppermute(swap, "gx", outside_pairs)
    state, pats, inside, x_faces = call(
        wall_inner_kernel, 16,
        [VMEM] * 6 + [ANY],
        (shape(5, WIN, WIDTH), shape(NB, WIN, WIDTH), shape(3, WIN, WIDTH), shape(2, 64, WIDTH)), (VMEM,) * 4,
        [vmem(in_rows, WIDTH)] + work + [dma(2)],
        1 << 24, 6 << 20,
    )(arrived, added_before, beside_small, own, products, held_blocks, on_chip)
    solid, sent_back = call(
        wall_last_kernel, 12,
        [VMEM] * 6 + [ANY],
        (shape(TILES, WIDTH), shape(RUNS, 1, WIDTH)), (VMEM, VMEM),
        [vmem(2 * TILE_ROWS, WIDTH)] + work + [dma()],
        1 << 23, 3 << 20,
    )(state, pats, inside, swapped, own, held_blocks, across)
    returned = lax.all_to_all(sent_back, "gx", split_axis=0, concat_axis=0, tiled=True)

    fluid_new = call(
        final_kernel, 16, [HBM] * 3 + [VMEM] * 4, shape(ROWS, WIDTH), VMEM,
        [vmem(ROWS, WIDTH), vmem(ROWS, WIDTH, kind=I32), vmem(2, 64, WIDTH), dma(3)], 2 * 256 * 1024 * 4096, 1 << 20,
    )(in_hbm(fluid), in_hbm(liquid.reshape(ROWS, WIDTH)), in_hbm(x_faces), faces, src, outgoing, returned)
    return fluid_new.reshape(fluid_temp.shape), solid[None]


def solution(mesh):
    return jax.shard_map(
        per_device,
        mesh=mesh,
        in_specs=(
            P("gx", "gy", "gz"),
            P("gx", "gy", "gz"),
            P("gx", "gy", "gz", None),
            P("gx", "gy", "gz", None),
            P(("gy", "gz"), "gx", None),
            P(("gy", "gz"), "gx", None),
            P(("gy", "gz"), "gx", None, None, None),
            P(("gy", "gz"), "gx", None),
        ),
        out_specs=(P("gx", "gy", "gz"), P(("gy", "gz"), "gx", None)),
        check_vma=False,
    )
```

```python
import jax
import jax.numpy as jnp
from jax import lax
from jax.experimental import pallas as pl
from jax.experimental.pallas import tpu as pltpu
from jax.sharding import PartitionSpec as P

F32 = jnp.float32
BF16 = jnp.bfloat16
I32 = jnp.int32
RUNS = 32
WIDTH = 128
ROWS = 1024
TILES = 8
NB = 5
WIN = 24
TILE_ROWS = NB * WIDTH
SMALL = 120

DIFFUSION = 0.12
EVAPORATION = 0.5
SATURATION = 0.25
WALL_COUPLING = 0.2

VMEM = pl.BlockSpec(memory_space=pltpu.VMEM)
HBM = pl.BlockSpec(memory_space=pltpu.HBM)
ANY = pl.BlockSpec(memory_space=pl.ANY)


def params(mib):
    return pltpu.CompilerParams(vmem_limit_bytes=mib << 20)


def two_parts(values):
    high = values.astype(BF16)
    return high, (values - high.astype(F32)).astype(BF16)


def lanes(rows):
    return jnp.concatenate(rows, axis=1)


def row_hots(row, count):
    width = row.shape[1]
    part = min(count, 256)
    level = lax.broadcasted_iota(I32, (part, width), 0).astype(F32).astype(BF16)
    one, zero = jnp.ones((), BF16), jnp.zeros((), BF16)
    parts = []
    for index in range(count // part):
        here = jnp.where((row >= index * part) & (row < (index + 1) * part), row - index * part, -1)
        parts.append(jnp.where(level == here.astype(F32).astype(BF16), one, zero))
    return parts[0] if len(parts) == 1 else jnp.concatenate(parts, axis=0)


def placed_parts(column, count, values):
    width = column.shape[1]
    mask = lax.broadcasted_iota(I32, (count, width), 0) == column
    high = values.astype(BF16).astype(F32)
    low = values - high
    both = [jnp.where(mask, part, 0.0) for part in (high, low)]
    return jnp.concatenate(both, axis=0).astype(BF16)


CONTRACT_LAST = (((1,), (1,)), ((), ()))


def pick_kernel(
    fluid_hbm, src_hbm, dst_hbm, old_hbm, diag_hbm, pattern_hbm, blocks_hbm,
    sent, outgoing, own, faces, on_chip_hbm, across_hbm,
    fluid, src, dst, pattern, table, staged_in, staged_out, sems,
):
    me = lax.axis_index("gx")
    parity = lax.rem(me, 2)

    def copy(source, target, index):
        started = pltpu.make_async_copy(source, target, sems.at[index])
        started.start()
        return started

    load_fluid = copy(fluid_hbm, fluid, 0)
    load_src = copy(src_hbm, src, 8)
    small = [
        copy(dst_hbm, dst, 9),
        copy(old_hbm, own.at[32:40], 10),
        copy(diag_hbm, own.at[40:48], 11),
        copy(pattern_hbm, pattern, 16),
    ]
    inside = copy(blocks_hbm.at[pl.ds((1 - parity) * 2 * TILE_ROWS, 6 * TILE_ROWS)], staged_in.at[0 : 6 * TILE_ROWS], 12)
    outside = copy(blocks_hbm.at[pl.ds(parity * 6 * TILE_ROWS, 2 * TILE_ROWS)], staged_out.at[0 : 2 * TILE_ROWS], 13)
    before_z = lax.axis_index("gy") * 4 + lax.rem(lax.axis_index("gz") + 3, 4)
    after_z = lax.axis_index("gy") * 4 + lax.rem(lax.axis_index("gz") + 1, 4)
    load_fluid.wait()
    for block in range(8):
        turned = fluid[128 * block : 128 * block + 128, :].T
        high, low = two_parts(turned)
        table[0:128, 128 * block : 128 * block + 128] = high
        table[128:256, 128 * block : 128 * block + 128] = low
        at = slice(128 * block, 128 * block + 128)
        faces[before_z, :, at] = turned[0:1, :]
        faces[after_z, :, at] = turned[127:128, :]
    for each in small:
        each.wait()
    own[0:32, :] = dst[...].astype(F32)
    own[48:56, :] = jnp.zeros((8, WIDTH), F32)
    for offset in range(NB):
        own[48 + offset : 49 + offset, 0:TILES] = pattern[offset].astype(F32)
    first, last = fluid[0:64, :], fluid[960:1024, :]
    for packed, start, face in (
        (staged_in, 6 * TILE_ROWS, jnp.where(parity == 0, last, first)),
        (staged_out, 2 * TILE_ROWS, jnp.where(parity == 0, first, last)),
    ):
        packed[start : start + 56, :] = own[...]
        packed[start + 56 : start + SMALL, :] = face
    y, z = lax.axis_index("gy"), lax.axis_index("gz")
    after_y, before_y = lax.rem(y + 1, 4) * 4 + z, lax.rem(y + 3, 4) * 4 + z
    for slab in range(16):
        at = slice(128 * slab, 128 * slab + 128)
        faces[before_y, :, at] = fluid[64 * slab : 64 * slab + 1, :]
        faces[after_y, :, at] = fluid[64 * slab + 63 : 64 * slab + 64, :]
    load_src.wait()
    group = 4
    for start in range(0, RUNS, group):
        if start == RUNS // 2:
            inside.wait()
            outside.wait()
            inside = copy(staged_in, on_chip_hbm, 17)
            outside = copy(staged_out, across_hbm, 18)
        ids = lanes([src[r : r + 1, :] for r in range(start, start + group)])
        picked = jnp.dot(table[...], row_hots(ids >> 7, ROWS), preferred_element_type=F32)
        both = picked[0:128] + picked[128:256]
        mask = lax.broadcasted_iota(I32, (WIDTH, group * WIDTH), 0) == (ids & 127)
        value = jnp.sum(jnp.where(mask, both, 0.0), axis=0, keepdims=True)
        for r in range(start, start + group):
            mine = value[:, (r - start) * WIDTH : (r - start + 1) * WIDTH]
            outgoing[r : r + 1, :] = mine
            sent[r, :, 0:128] = mine
            sent[r ^ 1, :, 128:256] = mine
            beside = (r + 1) % RUNS if r % 2 else (r - 1) % RUNS
            sent[beside, :, 256:384] = mine
    for each in (inside, outside):
        each.wait()


def spread_run(ids_of, values_of):
    group = 8
    total = None
    for start in range(0, RUNS, group):
        cell = lanes([ids_of(r) for r in range(start, start + group)])
        value = lanes([values_of(r) for r in range(start, start + group)])
        row = jnp.where(cell >= 0, ((cell >> 5) & 3) * 8 + (cell >> 7), -1)
        hots = row_hots(row, 32)
        placed = placed_parts(cell & 31, 32, value)
        added = lax.dot_general(hots, placed, CONTRACT_LAST, preferred_element_type=F32)
        total = added if total is None else total + added
    total = total[:, 0:32] + total[:, 32:64]
    return lanes([total[8 * u : 8 * u + 8, :] for u in range(4)])


def window(parity, own, partner, beside):
    pad = jnp.zeros((4, own.shape[1]), F32)
    low = jnp.concatenate([beside[4:8], own, partner, pad], axis=0)
    high = jnp.concatenate([partner, own, beside[0:4], pad], axis=0)
    return jnp.where(parity == 0, low, high)


def neighbours(iterate, pats, first, count, shifted):
    for offset in range(NB):
        values = iterate[first - 2 + offset : first - 2 + offset + count, :]
        shifted[offset, first : first + count, :] = values * pats[offset, first : first + count, :]


def apply_tile(blocks, tile, shifted, place, coupled):
    total = None
    for offset in range(NB):
        start = pl.multiple_of(tile * TILE_ROWS + offset * WIDTH, WIDTH)
        term = blocks[pl.ds(start, WIDTH), :] * shifted[offset, pl.ds(place, 1), :]
        total = term if total is None else total + term
    coupled[pl.ds(place, 1), :] = jnp.sum(total.T, axis=0, keepdims=True)


RHO = [0.5]
for _ in range(3):
    RHO.append(1.0 / (4.0 - RHO[-1]))


def stepped(sweep, value, update, right, inverse, diagonal, coupled):
    residual = right - (diagonal * value + coupled)
    if sweep == 0:
        update = inverse * residual
    else:
        update = RHO[sweep] * RHO[sweep - 1] * update + 4.0 * RHO[sweep] * inverse * residual
    return value + update, update


def own_run_kernel(arrived, dst, added):
    added[...] = spread_run(lambda r: dst[r : r + 1, :], lambda r: arrived[r, :, 0:128])


def beside_run_kernel(arrived, across_hbm, added_own, added, small, sem):
    load = pltpu.make_async_copy(across_hbm.at[2 * TILE_ROWS : 2 * TILE_ROWS + SMALL], small, sem)
    load.start()
    added[0:TILES, :] = added_own[...]
    load.wait()
    added[TILES : 2 * TILES, :] = spread_run(
        lambda r: small[r : r + 1, :].astype(I32), lambda r: arrived[r, :, 256:384]
    )


def windows(parity, keep, own, partner, beside, added):
    holders = [own, partner, beside]
    diagonals = [each[40:48] for each in holders]
    rights = [d * each[32:40] + a for d, each, a in zip(diagonals, holders, added)]
    inverses = [1.0 / d for d in diagonals]
    rights[2], inverses[2] = rights[2] * keep, inverses[2] * keep
    present = window(parity, *[each[48:56].T[0:TILES] for each in holders])
    return window(parity, *rights), window(parity, *inverses), window(parity, *diagonals), present


def wall_edge_kernel(
    added_before, beside_small, own, own_blocks, across_hbm,
    products, swap,
    outer, pats, iterate, shifted, coupled, sem,
):
    load = pltpu.make_async_copy(across_hbm.at[0 : 2 * TILE_ROWS], outer, sem)
    load.start()
    me = lax.axis_index("gx")
    parity = lax.rem(me, 2)
    keep = jnp.where((me == 0) | (me == RUNS - 1), 0.0, 1.0)
    mine = own[...]
    added = [added_before[0:TILES, :], jnp.zeros((TILES, WIDTH), F32), added_before[TILES : 2 * TILES, :]]
    right, inverse, diagonal, present = windows(parity, keep, mine, mine, beside_small[...], added)
    for offset in range(NB):
        pats[offset] = jnp.broadcast_to(present[:, offset : offset + 1], (WIN, WIDTH))
    value = inverse * right
    iterate[...] = value
    shifted[...] = jnp.zeros((NB, WIN, WIDTH), F32)
    coupled[...] = jnp.zeros((WIN, WIDTH), F32)
    own_at = 4 + 4 * parity
    neighbours(iterate, pats, 2, 16, shifted)
    for index in range(6):
        tile = index + 2 * parity
        apply_tile(own_blocks, tile, shifted, own_at + tile, coupled)
    load.wait()
    for index in range(2):
        apply_tile(outer, index, shifted, 2 + 14 * parity + index, coupled)
    products[0] = coupled[...]
    value, update = stepped(0, value, None, right, inverse, diagonal, coupled[...])
    iterate[...] = value
    neighbours(iterate, pats, 4, 12, shifted)
    for index in range(4):
        tile = index + 4 * parity
        apply_tile(own_blocks, tile, shifted, own_at + tile, coupled)
    products[1] = coupled[...]
    value, update = stepped(1, value, update, right, inverse, diagonal, coupled[...])
    swap[0:4, :] = jnp.where(parity == 0, value[4:8], value[12:16])
    swap[4:8, :] = jnp.where(parity == 0, update[4:8], update[12:16])


def wall_inner_kernel(
    arrived, added_before, beside_small, own, products, own_blocks, on_chip_hbm,
    state, pats, inside, faces,
    inner, iterate, shifted, coupled, sems,
):
    at_in = 6 * TILE_ROWS
    loads = [
        pltpu.make_async_copy(on_chip_hbm.at[low:high], inner.at[low:high], sems.at[index])
        for index, (low, high) in enumerate(((at_in, at_in + SMALL), (0, at_in)))
    ]
    for each in loads:
        each.start()
    me = lax.axis_index("gx")
    parity = lax.rem(me, 2)
    keep = jnp.where((me == 0) | (me == RUNS - 1), 0.0, 1.0)
    loads[0].wait()
    partner, beside = inner[at_in : at_in + SMALL, :], beside_small[...]
    added = [
        added_before[0:TILES, :],
        spread_run(lambda r: inner[at_in + r : at_in + r + 1, :].astype(I32), lambda r: arrived[r, :, 128:256]),
        added_before[TILES : 2 * TILES, :],
    ]
    right, inverse, diagonal, present = windows(parity, keep, own[...], partner, beside, added)
    for offset in range(NB):
        pats[offset] = jnp.broadcast_to(present[:, offset : offset + 1], (WIN, WIDTH))
    faces[0] = jnp.where(parity == 0, beside[56:120], partner[56:120])
    faces[1] = jnp.where(parity == 0, partner[56:120], beside[56:120])
    place = lax.broadcasted_iota(I32, (WIN, WIDTH), 0)
    value = inverse * right
    iterate[...] = value
    shifted[...] = jnp.zeros((NB, WIN, WIDTH), F32)
    coupled[...] = jnp.zeros((WIN, WIDTH), F32)
    own_at = 4 + 4 * parity

    neighbours(iterate, pats, 2, 16, shifted)
    for index in range(2):
        tile = index + 6 - 6 * parity
        apply_tile(own_blocks, tile, shifted, own_at + tile, coupled)
    loads[1].wait()
    for index in range(6):
        apply_tile(inner, index, shifted, 12 - 10 * parity + index, coupled)
    low = 2 + 8 * parity
    product = jnp.where((place >= low) & (place < low + 8), products[0], coupled[...])
    value, update = stepped(0, value, None, right, inverse, diagonal, product)
    iterate[...] = value

    neighbours(iterate, pats, 4, 12, shifted)
    for index in range(4):
        tile = index + 4 - 4 * parity
        apply_tile(own_blocks, tile, shifted, own_at + tile, coupled)
    for index in range(4):
        apply_tile(inner, index + 2 * parity, shifted, 12 - 8 * parity + index, coupled)
    low = 4 + 8 * parity
    product = jnp.where((place >= low) & (place < low + 4), products[1], coupled[...])
    value, update = stepped(1, value, update, right, inverse, diagonal, product)
    state[0], state[1], state[2], state[3], state[4] = value, update, right, inverse, diagonal
    iterate[...] = value

    neighbours(iterate, pats, 6, 8, shifted)
    for index in range(6):
        tile = index + 2 - 2 * parity
        apply_tile(own_blocks, tile, shifted, own_at + tile, coupled)
    for index in range(2):
        apply_tile(inner, index + 4 * parity, shifted, 12 - 6 * parity + index, coupled)
    value, update = stepped(2, value, update, right, inverse, diagonal, coupled[...])
    inside[0], inside[1] = value, update
    iterate[...] = value
    neighbours(iterate, pats, 8, 4, shifted)
    for index in range(4):
        tile = index + 4 - 4 * parity
        apply_tile(own_blocks, tile, shifted, own_at + tile, coupled)
    inside[2] = coupled[...]


def wall_last_kernel(
    state, pats, inside, swapped, own, own_blocks, across_hbm,
    solid, returned, outer, iterate, shifted, coupled, sem,
):
    load = pltpu.make_async_copy(across_hbm.at[0 : 2 * TILE_ROWS], outer, sem)
    load.start()
    me = lax.axis_index("gx")
    parity = lax.rem(me, 2)
    keep = jnp.where((me == 0) | (me == RUNS - 1), 0.0, 1.0)
    value, update, right, inverse, diagonal = (state[i] for i in range(5))

    def with_swapped(inside, outside):
        low = jnp.concatenate([outside, inside[4:24]], axis=0)
        high = jnp.concatenate([inside[0:16], outside, inside[20:24]], axis=0)
        return jnp.where(parity == 0, low, high)

    value = with_swapped(value, swapped[0:4, :] * keep)
    update = with_swapped(update, swapped[4:8, :] * keep)
    place = lax.broadcasted_iota(I32, (WIN, WIDTH), 0)
    own_at = 4 + 4 * parity
    iterate[...] = value
    shifted[...] = jnp.zeros((NB, WIN, WIDTH), F32)
    coupled[...] = jnp.zeros((WIN, WIDTH), F32)
    neighbours(iterate, pats, 2, 16, shifted)
    for index in range(2):
        tile = index + 6 * parity
        apply_tile(own_blocks, tile, shifted, own_at + tile, coupled)
    load.wait()
    for index in range(2):
        apply_tile(outer, index, shifted, 2 + 14 * parity + index, coupled)
    value, update = stepped(2, value, update, right, inverse, diagonal, coupled[...])
    known = (place >= 6) & (place < 14)
    value, update = jnp.where(known, inside[0], value), jnp.where(known, inside[1], update)
    iterate[...] = value
    neighbours(iterate, pats, 4, 12, shifted)
    for index in range(4):
        tile = index + 4 * parity
        apply_tile(own_blocks, tile, shifted, own_at + tile, coupled)
    product = jnp.where((place >= 8) & (place < 12), inside[2], coupled[...])
    value, update = stepped(3, value, update, right, inverse, diagonal, product)
    mine = jnp.where(parity == 0, value[4:12], value[8:16])
    solid[...] = mine
    for block in range(4):
        cell = own[8 * block : 8 * block + 8, :].astype(I32)
        tile, lane = cell >> 7, cell & 127
        found = jnp.zeros((8, WIDTH), F32)
        for index in range(TILES):
            row = jnp.broadcast_to(mine[index : index + 1, :], (8, WIDTH))
            found = jnp.where(tile == index, jnp.take_along_axis(row, lane, axis=1, mode="promise_in_bounds"), found)
        for r in range(8):
            returned[8 * block + r] = found[r : r + 1, :]


def final_kernel(fluid, liquid, x_faces, faces, src, outgoing, returned, fluid_new):
    group = 4
    total = None
    for start in range(0, RUNS, group):
        rows = range(start, start + group)
        ids = lanes([src[r : r + 1, :] for r in rows])
        value = lanes([returned[r] - outgoing[r : r + 1, :] for r in rows])
        placed = placed_parts(ids & 127, WIDTH, value)
        added = lax.dot_general(row_hots(ids >> 7, ROWS), placed, CONTRACT_LAST, preferred_element_type=F32)
        total = added if total is None else total + added
    wall = total[:, 0:128] + total[:, 128:256]
    y, z = lax.axis_index("gy"), lax.axis_index("gz")
    after_y, before_y = lax.rem(y + 1, 4) * 4 + z, lax.rem(y + 3, 4) * 4 + z
    after_z, before_z = y * 4 + lax.rem(z + 1, 4), y * 4 + lax.rem(z + 3, 4)
    row = lax.broadcasted_iota(I32, (64, WIDTH), 0)
    lane = lax.broadcasted_iota(I32, (64, WIDTH), 1)
    for slab in range(16):
        start = 64 * slab
        at, at_z = slice(128 * slab, 128 * slab + 128), slice(128 * (slab // 2), 128 * (slab // 2) + 128)
        here = fluid[start : start + 64, :]
        total = (fluid[start - 64 : start, :] if slab else x_faces[0]) + (
            fluid[start + 64 : start + 128, :] if slab < 15 else x_faces[1]
        )
        total = total + jnp.where(row == 0, faces[before_y, :, at], pltpu.roll(here, 1, 0))
        total = total + jnp.where(row == 63, faces[after_y, :, at], pltpu.roll(here, 63, 0))
        half = 64 * (slab % 2)
        left = jnp.broadcast_to(faces[before_z, :, at_z], (WIDTH, WIDTH)).T[half : half + 64, :]
        right = jnp.broadcast_to(faces[after_z, :, at_z], (WIDTH, WIDTH)).T[half : half + 64, :]
        total = total + jnp.where(lane == 0, left, pltpu.roll(here, 1, 1))
        total = total + jnp.where(lane == 127, right, pltpu.roll(here, 127, 1))
        total = total - 6.0 * here
        share = liquid[start : start + 64, :].astype(F32)
        fluid_new[start : start + 64, :] = (
            here
            + DIFFUSION * total
            - EVAPORATION * share * jnp.maximum(here - SATURATION, 0.0)
            + WALL_COUPLING * wall[start : start + 64, :]
        )


def shape(*dims):
    return jax.ShapeDtypeStruct(dims, F32)


def call(kernel, mib, ins, outs, out_specs, scratch, flops, moved):
    return pl.pallas_call(
        kernel,
        in_specs=ins,
        out_shape=outs,
        out_specs=out_specs,
        scratch_shapes=scratch,
        compiler_params=params(mib),
        cost_estimate=pl.CostEstimate(flops=flops, bytes_accessed=moved, transcendentals=0),
    )


def vmem(*dims, kind=F32):
    return pltpu.VMEM(dims, kind)


def dma(*dims):
    return pltpu.SemaphoreType.DMA(dims) if dims else pltpu.SemaphoreType.DMA


def per_device(fluid_temp, liquid, face_src, face_dst, solid_old, solid_diag, blocks, pattern):
    inside_pairs = [(i, i ^ 1) for i in range(RUNS)]
    outside_pairs = [(i, (i - 1) % RUNS if i % 2 == 0 else (i + 1) % RUNS) for i in range(RUNS)]
    fluid = fluid_temp.reshape(ROWS, WIDTH)
    src = face_src.reshape(RUNS, WIDTH)
    dst = face_dst.reshape(RUNS, WIDTH)
    own_blocks = blocks.reshape(TILES * TILE_ROWS, WIDTH)
    in_rows, out_rows = 6 * TILE_ROWS + SMALL, 2 * TILE_ROWS + SMALL

    sent, outgoing, own, faces, on_chip, across = call(
        pick_kernel, 60,
        [HBM] * 7,
        (
            shape(RUNS, 1, 384), shape(RUNS, WIDTH), shape(56, WIDTH), shape(16, 1, 2048),
            shape(in_rows, WIDTH), shape(out_rows, WIDTH),
        ),
        (VMEM, VMEM, VMEM, VMEM, HBM, HBM),
        [
            vmem(ROWS, WIDTH), vmem(RUNS, WIDTH, kind=I32), vmem(RUNS, WIDTH, kind=I32), vmem(NB, 1, TILES, kind=I32),
            vmem(256, ROWS, kind=BF16), vmem(in_rows, WIDTH), vmem(out_rows, WIDTH), dma(19),
        ],
        2 * 256 * 1024 * 4096, 1 << 22,
    )(fluid, src, dst, solid_old[0], solid_diag[0], jnp.transpose(pattern, (2, 0, 1)), own_blocks)

    arrived = lax.all_to_all(sent, "gx", split_axis=0, concat_axis=0, tiled=True)
    on_chip = lax.ppermute(on_chip, "gx", inside_pairs)
    across = lax.ppermute(across, "gx", outside_pairs)
    faces = lax.all_to_all(faces, ("gy", "gz"), split_axis=0, concat_axis=0, tiled=True)

    work = [vmem(WIN, WIDTH), vmem(NB, WIN, WIDTH), vmem(WIN, WIDTH)]
    added_own = call(
        own_run_kernel, 12, [VMEM, VMEM], shape(TILES, WIDTH), VMEM, [], 20 * 10**9, 1 << 16
    )(arrived, dst)
    added_before, beside_small = call(
        beside_run_kernel, 12, [VMEM, ANY, VMEM], (shape(2 * TILES, WIDTH), shape(SMALL, WIDTH)), (VMEM, VMEM), [dma()],
        10**9, 1 << 16,
    )(arrived, across, added_own)
    products, swap = call(
        wall_edge_kernel, 12,
        [VMEM] * 4 + [ANY],
        (shape(2, WIN, WIDTH), shape(8, WIDTH)), (VMEM, VMEM),
        [vmem(2 * TILE_ROWS, WIDTH), vmem(NB, WIN, WIDTH)] + work + [dma()],
        1 << 23, 4 << 20,
    )(added_before, beside_small, own, own_blocks, across)
    swapped = lax.ppermute(swap, "gx", outside_pairs)
    state, pats, inside, x_faces = call(
        wall_inner_kernel, 16,
        [VMEM] * 6 + [ANY],
        (shape(5, WIN, WIDTH), shape(NB, WIN, WIDTH), shape(3, WIN, WIDTH), shape(2, 64, WIDTH)), (VMEM,) * 4,
        [vmem(in_rows, WIDTH)] + work + [dma(2)],
        1 << 24, 6 << 20,
    )(arrived, added_before, beside_small, own, products, own_blocks, on_chip)
    solid, sent_back = call(
        wall_last_kernel, 12,
        [VMEM] * 6 + [ANY],
        (shape(TILES, WIDTH), shape(RUNS, 1, WIDTH)), (VMEM, VMEM),
        [vmem(2 * TILE_ROWS, WIDTH)] + work + [dma()],
        1 << 23, 3 << 20,
    )(state, pats, inside, swapped, own, own_blocks, across)
    returned = lax.all_to_all(sent_back, "gx", split_axis=0, concat_axis=0, tiled=True)

    fluid_new = call(
        final_kernel, 16, [VMEM] * 7, shape(ROWS, WIDTH), VMEM, [], 2 * 256 * 1024 * 4096, 1 << 20
    )(fluid, liquid.reshape(ROWS, WIDTH), x_faces, faces, src, outgoing, returned)
    return fluid_new.reshape(fluid_temp.shape), solid[None]


def solution(mesh):
    return jax.shard_map(
        per_device,
        mesh=mesh,
        in_specs=(
            P("gx", "gy", "gz"),
            P("gx", "gy", "gz"),
            P("gx", "gy", "gz", None),
            P("gx", "gy", "gz", None),
            P(("gy", "gz"), "gx", None),
            P(("gy", "gz"), "gx", None),
            P(("gy", "gz"), "gx", None, None, None),
            P(("gy", "gz"), "gx", None),
        ),
        out_specs=(P("gx", "gy", "gz"), P(("gy", "gz"), "gx", None)),
        check_vma=False,
    )
```

```python
import jax
import jax.numpy as jnp
from jax import lax
from jax.experimental import pallas as pl
from jax.experimental.pallas import tpu as pltpu
from jax.sharding import PartitionSpec as P

F32 = jnp.float32
BF16 = jnp.bfloat16
I32 = jnp.int32
RUNS = 32
WIDTH = 128
ROWS = 1024
TILES = 8
NB = 5
WIN = 24
TILE_ROWS = NB * WIDTH
SMALL = 120

DIFFUSION = 0.12
EVAPORATION = 0.5
SATURATION = 0.25
WALL_COUPLING = 0.2

VMEM = pl.BlockSpec(memory_space=pltpu.VMEM)
HBM = pl.BlockSpec(memory_space=pltpu.HBM)
ANY = pl.BlockSpec(memory_space=pl.ANY)


def params(mib):
    return pltpu.CompilerParams(vmem_limit_bytes=mib << 20)


def two_parts(values):
    high = values.astype(BF16)
    return high, (values - high.astype(F32)).astype(BF16)


def lanes(rows):
    return jnp.concatenate(rows, axis=1)


def row_hots(row, count):
    width = row.shape[1]
    part = min(count, 256)
    level = lax.broadcasted_iota(I32, (part, width), 0).astype(F32).astype(BF16)
    one, zero = jnp.ones((), BF16), jnp.zeros((), BF16)
    parts = []
    for index in range(count // part):
        here = jnp.where((row >= index * part) & (row < (index + 1) * part), row - index * part, -1)
        parts.append(jnp.where(level == here.astype(F32).astype(BF16), one, zero))
    return parts[0] if len(parts) == 1 else jnp.concatenate(parts, axis=0)


def placed_parts(column, count, values):
    width = column.shape[1]
    mask = lax.broadcasted_iota(I32, (count, width), 0) == column
    high = values.astype(BF16).astype(F32)
    low = values - high
    both = [jnp.where(mask, part, 0.0) for part in (high, low)]
    return jnp.concatenate(both, axis=0).astype(BF16)


CONTRACT_LAST = (((1,), (1,)), ((), ()))


def pick_kernel(
    fluid_hbm, src_hbm, dst_hbm, old_hbm, diag_hbm, pattern_hbm, blocks_hbm,
    sent, outgoing, own, faces, on_chip_hbm, across_hbm,
    fluid, src, dst, pattern, table, staged_in, staged_out, sems,
):
    me = lax.axis_index("gx")
    parity = lax.rem(me, 2)

    def copy(source, target, index):
        started = pltpu.make_async_copy(source, target, sems.at[index])
        started.start()
        return started

    load_fluid = copy(fluid_hbm, fluid, 0)
    load_src = copy(src_hbm, src, 8)
    small = [
        copy(dst_hbm, dst, 9),
        copy(old_hbm, own.at[32:40], 10),
        copy(diag_hbm, own.at[40:48], 11),
        copy(pattern_hbm, pattern, 16),
    ]
    inside = copy(blocks_hbm.at[pl.ds((1 - parity) * 2 * TILE_ROWS, 6 * TILE_ROWS)], staged_in.at[0 : 6 * TILE_ROWS], 12)
    outside = copy(blocks_hbm.at[pl.ds(parity * 6 * TILE_ROWS, 2 * TILE_ROWS)], staged_out.at[0 : 2 * TILE_ROWS], 13)
    before_z = lax.axis_index("gy") * 4 + lax.rem(lax.axis_index("gz") + 3, 4)
    after_z = lax.axis_index("gy") * 4 + lax.rem(lax.axis_index("gz") + 1, 4)
    load_fluid.wait()
    for block in range(8):
        turned = fluid[128 * block : 128 * block + 128, :].T
        high, low = two_parts(turned)
        table[0:128, 128 * block : 128 * block + 128] = high
        table[128:256, 128 * block : 128 * block + 128] = low
        at = slice(128 * block, 128 * block + 128)
        faces[before_z, :, at] = turned[0:1, :]
        faces[after_z, :, at] = turned[127:128, :]
    for each in small:
        each.wait()
    own[0:32, :] = dst[...].astype(F32)
    own[48:56, :] = jnp.zeros((8, WIDTH), F32)
    for offset in range(NB):
        own[48 + offset : 49 + offset, 0:TILES] = pattern[offset].astype(F32)
    first, last = fluid[0:64, :], fluid[960:1024, :]
    for packed, start, face in (
        (staged_in, 6 * TILE_ROWS, jnp.where(parity == 0, last, first)),
        (staged_out, 2 * TILE_ROWS, jnp.where(parity == 0, first, last)),
    ):
        packed[start : start + 56, :] = own[...]
        packed[start + 56 : start + SMALL, :] = face
    y, z = lax.axis_index("gy"), lax.axis_index("gz")
    after_y, before_y = lax.rem(y + 1, 4) * 4 + z, lax.rem(y + 3, 4) * 4 + z
    for slab in range(16):
        at = slice(128 * slab, 128 * slab + 128)
        faces[before_y, :, at] = fluid[64 * slab : 64 * slab + 1, :]
        faces[after_y, :, at] = fluid[64 * slab + 63 : 64 * slab + 64, :]
    load_src.wait()
    group = 4
    for start in range(0, RUNS, group):
        if start == RUNS // 2:
            inside.wait()
            outside.wait()
            inside = copy(staged_in, on_chip_hbm, 17)
            outside = copy(staged_out, across_hbm, 18)
        ids = lanes([src[r : r + 1, :] for r in range(start, start + group)])
        picked = jnp.dot(table[...], row_hots(ids >> 7, ROWS), preferred_element_type=F32)
        both = picked[0:128] + picked[128:256]
        mask = lax.broadcasted_iota(I32, (WIDTH, group * WIDTH), 0) == (ids & 127)
        value = jnp.sum(jnp.where(mask, both, 0.0), axis=0, keepdims=True)
        for r in range(start, start + group):
            mine = value[:, (r - start) * WIDTH : (r - start + 1) * WIDTH]
            outgoing[r : r + 1, :] = mine
            sent[r, :, 0:128] = mine
            sent[r ^ 1, :, 128:256] = mine
            beside = (r + 1) % RUNS if r % 2 else (r - 1) % RUNS
            sent[beside, :, 256:384] = mine
    for each in (inside, outside):
        each.wait()


def spread_run(ids_of, values_of):
    group = 8
    total = None
    for start in range(0, RUNS, group):
        cell = lanes([ids_of(r) for r in range(start, start + group)])
        value = lanes([values_of(r) for r in range(start, start + group)])
        row = jnp.where(cell >= 0, ((cell >> 5) & 3) * 8 + (cell >> 7), -1)
        hots = row_hots(row, 32)
        placed = placed_parts(cell & 31, 32, value)
        added = lax.dot_general(hots, placed, CONTRACT_LAST, preferred_element_type=F32)
        total = added if total is None else total + added
    total = total[:, 0:32] + total[:, 32:64]
    return lanes([total[8 * u : 8 * u + 8, :] for u in range(4)])


def window(parity, own, partner, beside):
    pad = jnp.zeros((4, own.shape[1]), F32)
    low = jnp.concatenate([beside[4:8], own, partner, pad], axis=0)
    high = jnp.concatenate([partner, own, beside[0:4], pad], axis=0)
    return jnp.where(parity == 0, low, high)


def neighbours(iterate, pats, first, count, shifted):
    for offset in range(NB):
        values = iterate[first - 2 + offset : first - 2 + offset + count, :]
        shifted[offset, first : first + count, :] = values * pats[offset, first : first + count, :]


def apply_tile(blocks, tile, shifted, place, coupled):
    total = None
    for offset in range(NB):
        start = pl.multiple_of(tile * TILE_ROWS + offset * WIDTH, WIDTH)
        term = blocks[pl.ds(start, WIDTH), :] * shifted[offset, pl.ds(place, 1), :]
        total = term if total is None else total + term
    coupled[pl.ds(place, 1), :] = jnp.sum(total.T, axis=0, keepdims=True)


RHO = [0.5]
for _ in range(3):
    RHO.append(1.0 / (4.0 - RHO[-1]))


def stepped(sweep, value, update, right, inverse, diagonal, coupled):
    residual = right - (diagonal * value + coupled)
    if sweep == 0:
        update = inverse * residual
    else:
        update = RHO[sweep] * RHO[sweep - 1] * update + 4.0 * RHO[sweep] * inverse * residual
    return value + update, update


def own_run_kernel(arrived, dst, added):
    added[...] = spread_run(lambda r: dst[r : r + 1, :], lambda r: arrived[r, :, 0:128])


def beside_run_kernel(arrived, across_hbm, added_own, added, small, sem):
    load = pltpu.make_async_copy(across_hbm.at[2 * TILE_ROWS : 2 * TILE_ROWS + SMALL], small, sem)
    load.start()
    added[0:TILES, :] = added_own[...]
    load.wait()
    added[TILES : 2 * TILES, :] = spread_run(
        lambda r: small[r : r + 1, :].astype(I32), lambda r: arrived[r, :, 256:384]
    )


def windows(parity, keep, own, partner, beside, added):
    holders = [own, partner, beside]
    diagonals = [each[40:48] for each in holders]
    rights = [d * each[32:40] + a for d, each, a in zip(diagonals, holders, added)]
    inverses = [1.0 / d for d in diagonals]
    rights[2], inverses[2] = rights[2] * keep, inverses[2] * keep
    present = window(parity, *[each[48:56].T[0:TILES] for each in holders])
    return window(parity, *rights), window(parity, *inverses), window(parity, *diagonals), present


def wall_edge_kernel(
    added_before, beside_small, own, own_blocks, across_hbm,
    products, swap,
    outer, pats, iterate, shifted, coupled, sem,
):
    load = pltpu.make_async_copy(across_hbm.at[0 : 2 * TILE_ROWS], outer, sem)
    load.start()
    me = lax.axis_index("gx")
    parity = lax.rem(me, 2)
    keep = jnp.where((me == 0) | (me == RUNS - 1), 0.0, 1.0)
    mine = own[...]
    added = [added_before[0:TILES, :], jnp.zeros((TILES, WIDTH), F32), added_before[TILES : 2 * TILES, :]]
    right, inverse, diagonal, present = windows(parity, keep, mine, mine, beside_small[...], added)
    for offset in range(NB):
        pats[offset] = jnp.broadcast_to(present[:, offset : offset + 1], (WIN, WIDTH))
    value = inverse * right
    iterate[...] = value
    shifted[...] = jnp.zeros((NB, WIN, WIDTH), F32)
    coupled[...] = jnp.zeros((WIN, WIDTH), F32)
    own_at = 4 + 4 * parity
    neighbours(iterate, pats, 2, 16, shifted)
    for index in range(6):
        tile = index + 2 * parity
        apply_tile(own_blocks, tile, shifted, own_at + tile, coupled)
    load.wait()
    for index in range(2):
        apply_tile(outer, index, shifted, 2 + 14 * parity + index, coupled)
    products[0] = coupled[...]
    value, update = stepped(0, value, None, right, inverse, diagonal, coupled[...])
    iterate[...] = value
    neighbours(iterate, pats, 4, 12, shifted)
    for index in range(4):
        tile = index + 4 * parity
        apply_tile(own_blocks, tile, shifted, own_at + tile, coupled)
    products[1] = coupled[...]
    value, update = stepped(1, value, update, right, inverse, diagonal, coupled[...])
    swap[0:4, :] = jnp.where(parity == 0, value[4:8], value[12:16])
    swap[4:8, :] = jnp.where(parity == 0, update[4:8], update[12:16])


def wall_inner_kernel(
    arrived, added_before, beside_small, own, products, own_blocks, on_chip_hbm,
    state, pats, inside, faces,
    inner, iterate, shifted, coupled, sems,
):
    at_in = 6 * TILE_ROWS
    loads = [
        pltpu.make_async_copy(on_chip_hbm.at[low:high], inner.at[low:high], sems.at[index])
        for index, (low, high) in enumerate(((at_in, at_in + SMALL), (0, at_in)))
    ]
    for each in loads:
        each.start()
    me = lax.axis_index("gx")
    parity = lax.rem(me, 2)
    keep = jnp.where((me == 0) | (me == RUNS - 1), 0.0, 1.0)
    loads[0].wait()
    partner, beside = inner[at_in : at_in + SMALL, :], beside_small[...]
    added = [
        added_before[0:TILES, :],
        spread_run(lambda r: inner[at_in + r : at_in + r + 1, :].astype(I32), lambda r: arrived[r, :, 128:256]),
        added_before[TILES : 2 * TILES, :],
    ]
    right, inverse, diagonal, present = windows(parity, keep, own[...], partner, beside, added)
    for offset in range(NB):
        pats[offset] = jnp.broadcast_to(present[:, offset : offset + 1], (WIN, WIDTH))
    faces[0] = jnp.where(parity == 0, beside[56:120], partner[56:120])
    faces[1] = jnp.where(parity == 0, partner[56:120], beside[56:120])
    place = lax.broadcasted_iota(I32, (WIN, WIDTH), 0)
    value = inverse * right
    iterate[...] = value
    shifted[...] = jnp.zeros((NB, WIN, WIDTH), F32)
    coupled[...] = jnp.zeros((WIN, WIDTH), F32)
    own_at = 4 + 4 * parity

    neighbours(iterate, pats, 2, 16, shifted)
    for index in range(2):
        tile = index + 6 - 6 * parity
        apply_tile(own_blocks, tile, shifted, own_at + tile, coupled)
    loads[1].wait()
    for index in range(6):
        apply_tile(inner, index, shifted, 12 - 10 * parity + index, coupled)
    low = 2 + 8 * parity
    product = jnp.where((place >= low) & (place < low + 8), products[0], coupled[...])
    value, update = stepped(0, value, None, right, inverse, diagonal, product)
    iterate[...] = value

    neighbours(iterate, pats, 4, 12, shifted)
    for index in range(4):
        tile = index + 4 - 4 * parity
        apply_tile(own_blocks, tile, shifted, own_at + tile, coupled)
    for index in range(4):
        apply_tile(inner, index + 2 * parity, shifted, 12 - 8 * parity + index, coupled)
    low = 4 + 8 * parity
    product = jnp.where((place >= low) & (place < low + 4), products[1], coupled[...])
    value, update = stepped(1, value, update, right, inverse, diagonal, product)
    state[0], state[1], state[2], state[3], state[4] = value, update, right, inverse, diagonal
    iterate[...] = value

    neighbours(iterate, pats, 6, 8, shifted)
    for index in range(6):
        tile = index + 2 - 2 * parity
        apply_tile(own_blocks, tile, shifted, own_at + tile, coupled)
    for index in range(2):
        apply_tile(inner, index + 4 * parity, shifted, 12 - 6 * parity + index, coupled)
    value, update = stepped(2, value, update, right, inverse, diagonal, coupled[...])
    inside[0], inside[1] = value, update
    iterate[...] = value
    neighbours(iterate, pats, 8, 4, shifted)
    for index in range(4):
        tile = index + 4 - 4 * parity
        apply_tile(own_blocks, tile, shifted, own_at + tile, coupled)
    inside[2] = coupled[...]


def wall_last_kernel(
    state, pats, inside, swapped, own, own_blocks, across_hbm,
    solid, returned, outer, iterate, shifted, coupled, sem,
):
    load = pltpu.make_async_copy(across_hbm.at[0 : 2 * TILE_ROWS], outer, sem)
    load.start()
    me = lax.axis_index("gx")
    parity = lax.rem(me, 2)
    keep = jnp.where((me == 0) | (me == RUNS - 1), 0.0, 1.0)
    value, update, right, inverse, diagonal = (state[i] for i in range(5))

    def with_swapped(inside, outside):
        low = jnp.concatenate([outside, inside[4:24]], axis=0)
        high = jnp.concatenate([inside[0:16], outside, inside[20:24]], axis=0)
        return jnp.where(parity == 0, low, high)

    value = with_swapped(value, swapped[0:4, :] * keep)
    update = with_swapped(update, swapped[4:8, :] * keep)
    place = lax.broadcasted_iota(I32, (WIN, WIDTH), 0)
    own_at = 4 + 4 * parity
    iterate[...] = value
    shifted[...] = jnp.zeros((NB, WIN, WIDTH), F32)
    coupled[...] = jnp.zeros((WIN, WIDTH), F32)
    neighbours(iterate, pats, 2, 16, shifted)
    for index in range(2):
        tile = index + 6 * parity
        apply_tile(own_blocks, tile, shifted, own_at + tile, coupled)
    load.wait()
    for index in range(2):
        apply_tile(outer, index, shifted, 2 + 14 * parity + index, coupled)
    value, update = stepped(2, value, update, right, inverse, diagonal, coupled[...])
    known = (place >= 6) & (place < 14)
    value, update = jnp.where(known, inside[0], value), jnp.where(known, inside[1], update)
    iterate[...] = value
    neighbours(iterate, pats, 4, 12, shifted)
    for index in range(4):
        tile = index + 4 * parity
        apply_tile(own_blocks, tile, shifted, own_at + tile, coupled)
    product = jnp.where((place >= 8) & (place < 12), inside[2], coupled[...])
    value, update = stepped(3, value, update, right, inverse, diagonal, product)
    mine = jnp.where(parity == 0, value[4:12], value[8:16])
    solid[...] = mine
    for block in range(4):
        cell = own[8 * block : 8 * block + 8, :].astype(I32)
        tile, lane = cell >> 7, cell & 127
        found = jnp.zeros((8, WIDTH), F32)
        for index in range(TILES):
            row = jnp.broadcast_to(mine[index : index + 1, :], (8, WIDTH))
            found = jnp.where(tile == index, jnp.take_along_axis(row, lane, axis=1, mode="promise_in_bounds"), found)
        for r in range(8):
            returned[8 * block + r] = found[r : r + 1, :]


def final_kernel(fluid, liquid, x_faces, faces, src, outgoing, returned, fluid_new):
    group = 4
    total = None
    for start in range(0, RUNS, group):
        rows = range(start, start + group)
        ids = lanes([src[r : r + 1, :] for r in rows])
        value = lanes([returned[r] - outgoing[r : r + 1, :] for r in rows])
        placed = placed_parts(ids & 127, WIDTH, value)
        added = lax.dot_general(row_hots(ids >> 7, ROWS), placed, CONTRACT_LAST, preferred_element_type=F32)
        total = added if total is None else total + added
    wall = total[:, 0:128] + total[:, 128:256]
    y, z = lax.axis_index("gy"), lax.axis_index("gz")
    after_y, before_y = lax.rem(y + 1, 4) * 4 + z, lax.rem(y + 3, 4) * 4 + z
    after_z, before_z = y * 4 + lax.rem(z + 1, 4), y * 4 + lax.rem(z + 3, 4)
    row = lax.broadcasted_iota(I32, (64, WIDTH), 0)
    lane = lax.broadcasted_iota(I32, (64, WIDTH), 1)
    for slab in range(16):
        start = 64 * slab
        at, at_z = slice(128 * slab, 128 * slab + 128), slice(128 * (slab // 2), 128 * (slab // 2) + 128)
        here = fluid[start : start + 64, :]
        total = (fluid[start - 64 : start, :] if slab else x_faces[0]) + (
            fluid[start + 64 : start + 128, :] if slab < 15 else x_faces[1]
        )
        total = total + jnp.where(row == 0, faces[before_y, :, at], pltpu.roll(here, 1, 0))
        total = total + jnp.where(row == 63, faces[after_y, :, at], pltpu.roll(here, 63, 0))
        half = 64 * (slab % 2)
        left = jnp.broadcast_to(faces[before_z, :, at_z], (WIDTH, WIDTH)).T[half : half + 64, :]
        right = jnp.broadcast_to(faces[after_z, :, at_z], (WIDTH, WIDTH)).T[half : half + 64, :]
        total = total + jnp.where(lane == 0, left, pltpu.roll(here, 1, 1))
        total = total + jnp.where(lane == 127, right, pltpu.roll(here, 127, 1))
        total = total - 6.0 * here
        share = liquid[start : start + 64, :].astype(F32)
        fluid_new[start : start + 64, :] = (
            here
            + DIFFUSION * total
            - EVAPORATION * share * jnp.maximum(here - SATURATION, 0.0)
            + WALL_COUPLING * wall[start : start + 64, :]
        )


def shape(*dims):
    return jax.ShapeDtypeStruct(dims, F32)


def call(kernel, mib, ins, outs, out_specs, scratch, flops, moved):
    return pl.pallas_call(
        kernel,
        in_specs=ins,
        out_shape=outs,
        out_specs=out_specs,
        scratch_shapes=scratch,
        compiler_params=params(mib),
        cost_estimate=pl.CostEstimate(flops=flops, bytes_accessed=moved, transcendentals=0),
    )


def vmem(*dims, kind=F32):
    return pltpu.VMEM(dims, kind)


def dma(*dims):
    return pltpu.SemaphoreType.DMA(dims) if dims else pltpu.SemaphoreType.DMA


def per_device(fluid_temp, liquid, face_src, face_dst, solid_old, solid_diag, blocks, pattern):
    inside_pairs = [(i, i ^ 1) for i in range(RUNS)]
    outside_pairs = [(i, (i - 1) % RUNS if i % 2 == 0 else (i + 1) % RUNS) for i in range(RUNS)]
    fluid = fluid_temp.reshape(ROWS, WIDTH)
    src = face_src.reshape(RUNS, WIDTH)
    dst = face_dst.reshape(RUNS, WIDTH)
    own_blocks = blocks.reshape(TILES * TILE_ROWS, WIDTH)
    in_rows, out_rows = 6 * TILE_ROWS + SMALL, 2 * TILE_ROWS + SMALL

    sent, outgoing, own, faces, on_chip, across = call(
        pick_kernel, 60,
        [HBM] * 7,
        (
            shape(RUNS, 1, 384), shape(RUNS, WIDTH), shape(56, WIDTH), shape(16, 1, 2048),
            shape(in_rows, WIDTH), shape(out_rows, WIDTH),
        ),
        (VMEM, VMEM, VMEM, VMEM, HBM, HBM),
        [
            vmem(ROWS, WIDTH), vmem(RUNS, WIDTH, kind=I32), vmem(RUNS, WIDTH, kind=I32), vmem(NB, 1, TILES, kind=I32),
            vmem(256, ROWS, kind=BF16), vmem(in_rows, WIDTH), vmem(out_rows, WIDTH), dma(19),
        ],
        2 * 256 * 1024 * 4096, 1 << 22,
    )(fluid, src, dst, solid_old[0], solid_diag[0], jnp.transpose(pattern, (2, 0, 1)), own_blocks)

    arrived = lax.all_to_all(sent, "gx", split_axis=0, concat_axis=0, tiled=True)
    on_chip = lax.ppermute(on_chip, "gx", inside_pairs)
    across = lax.ppermute(across, "gx", outside_pairs)
    faces = lax.all_to_all(faces, ("gy", "gz"), split_axis=0, concat_axis=0, tiled=True)

    work = [vmem(WIN, WIDTH), vmem(NB, WIN, WIDTH), vmem(WIN, WIDTH)]
    added_own = call(
        own_run_kernel, 12, [VMEM, VMEM], shape(TILES, WIDTH), VMEM, [], 65 * 10**8, 1 << 16
    )(arrived, dst)
    added_before, beside_small = call(
        beside_run_kernel, 12, [VMEM, ANY, VMEM], (shape(2 * TILES, WIDTH), shape(SMALL, WIDTH)), (VMEM, VMEM), [dma()],
        14 * 10**9, 1 << 16,
    )(arrived, across, added_own)
    products, swap = call(
        wall_edge_kernel, 12,
        [VMEM] * 4 + [ANY],
        (shape(2, WIN, WIDTH), shape(8, WIDTH)), (VMEM, VMEM),
        [vmem(2 * TILE_ROWS, WIDTH), vmem(NB, WIN, WIDTH)] + work + [dma()],
        1 << 23, 4 << 20,
    )(added_before, beside_small, own, own_blocks, across)
    swapped = lax.ppermute(swap, "gx", outside_pairs)
    state, pats, inside, x_faces = call(
        wall_inner_kernel, 16,
        [VMEM] * 6 + [ANY],
        (shape(5, WIN, WIDTH), shape(NB, WIN, WIDTH), shape(3, WIN, WIDTH), shape(2, 64, WIDTH)), (VMEM,) * 4,
        [vmem(in_rows, WIDTH)] + work + [dma(2)],
        1 << 24, 6 << 20,
    )(arrived, added_before, beside_small, own, products, own_blocks, on_chip)
    solid, sent_back = call(
        wall_last_kernel, 12,
        [VMEM] * 6 + [ANY],
        (shape(TILES, WIDTH), shape(RUNS, 1, WIDTH)), (VMEM, VMEM),
        [vmem(2 * TILE_ROWS, WIDTH)] + work + [dma()],
        1 << 23, 3 << 20,
    )(state, pats, inside, swapped, own, own_blocks, across)
    returned = lax.all_to_all(sent_back, "gx", split_axis=0, concat_axis=0, tiled=True)

    fluid_new = call(
        final_kernel, 16, [VMEM] * 7, shape(ROWS, WIDTH), VMEM, [], 2 * 256 * 1024 * 4096, 1 << 20
    )(fluid, liquid.reshape(ROWS, WIDTH), x_faces, faces, src, outgoing, returned)
    return fluid_new.reshape(fluid_temp.shape), solid[None]


def solution(mesh):
    return jax.shard_map(
        per_device,
        mesh=mesh,
        in_specs=(
            P("gx", "gy", "gz"),
            P("gx", "gy", "gz"),
            P("gx", "gy", "gz", None),
            P("gx", "gy", "gz", None),
            P(("gy", "gz"), "gx", None),
            P(("gy", "gz"), "gx", None),
            P(("gy", "gz"), "gx", None, None, None),
            P(("gy", "gz"), "gx", None),
        ),
        out_specs=(P("gx", "gy", "gz"), P(("gy", "gz"), "gx", None)),
        check_vma=False,
    )
```

```python
import jax
import jax.numpy as jnp
from jax import lax
from jax.experimental import pallas as pl
from jax.experimental.pallas import tpu as pltpu
from jax.sharding import PartitionSpec as P

F32 = jnp.float32
BF16 = jnp.bfloat16
I32 = jnp.int32
RUNS = 32
WIDTH = 128
ROWS = 1024
TILES = 8
NB = 5
WIN = 24
TILE_ROWS = NB * WIDTH
SMALL = 120

DIFFUSION = 0.12
EVAPORATION = 0.5
SATURATION = 0.25
WALL_COUPLING = 0.2

VMEM = pl.BlockSpec(memory_space=pltpu.VMEM)
HBM = pl.BlockSpec(memory_space=pltpu.HBM)
ANY = pl.BlockSpec(memory_space=pl.ANY)


def params(mib):
    return pltpu.CompilerParams(vmem_limit_bytes=mib << 20)


def two_parts(values):
    high = values.astype(BF16)
    return high, (values - high.astype(F32)).astype(BF16)


def lanes(rows):
    return jnp.concatenate(rows, axis=1)


def row_hots(row, count):
    width = row.shape[1]
    part = min(count, 256)
    level = lax.broadcasted_iota(I32, (part, width), 0).astype(F32).astype(BF16)
    one, zero = jnp.ones((), BF16), jnp.zeros((), BF16)
    parts = []
    for index in range(count // part):
        here = jnp.where((row >= index * part) & (row < (index + 1) * part), row - index * part, -1)
        parts.append(jnp.where(level == here.astype(F32).astype(BF16), one, zero))
    return parts[0] if len(parts) == 1 else jnp.concatenate(parts, axis=0)


def placed_parts(column, count, values):
    width = column.shape[1]
    mask = lax.broadcasted_iota(I32, (count, width), 0) == column
    high = values.astype(BF16).astype(F32)
    low = values - high
    both = [jnp.where(mask, part, 0.0) for part in (high, low)]
    return jnp.concatenate(both, axis=0).astype(BF16)


CONTRACT_LAST = (((1,), (1,)), ((), ()))


def pick_kernel(
    fluid_hbm, src_hbm, dst_hbm, old_hbm, diag_hbm, pattern_hbm, blocks_hbm,
    sent, outgoing, own, faces_hbm, on_chip_hbm, across_hbm,
    fluid, src, dst, pattern, table, staged_in, staged_out, faces, sems,
):
    me = lax.axis_index("gx")
    parity = lax.rem(me, 2)

    def copy(source, target, index):
        started = pltpu.make_async_copy(source, target, sems.at[index])
        started.start()
        return started

    load_fluid = copy(fluid_hbm, fluid, 0)
    load_src = copy(src_hbm, src, 8)
    small = [
        copy(dst_hbm, dst, 9),
        copy(old_hbm, own.at[32:40], 10),
        copy(diag_hbm, own.at[40:48], 11),
        copy(pattern_hbm, pattern, 16),
    ]
    inside = copy(blocks_hbm.at[pl.ds((1 - parity) * 2 * TILE_ROWS, 6 * TILE_ROWS)], staged_in.at[0 : 6 * TILE_ROWS], 12)
    outside = copy(blocks_hbm.at[pl.ds(parity * 6 * TILE_ROWS, 2 * TILE_ROWS)], staged_out.at[0 : 2 * TILE_ROWS], 13)
    before_z = lax.axis_index("gy") * 4 + lax.rem(lax.axis_index("gz") + 3, 4)
    after_z = lax.axis_index("gy") * 4 + lax.rem(lax.axis_index("gz") + 1, 4)
    load_fluid.wait()
    for block in range(8):
        turned = fluid[128 * block : 128 * block + 128, :].T
        high, low = two_parts(turned)
        table[0:128, 128 * block : 128 * block + 128] = high
        table[128:256, 128 * block : 128 * block + 128] = low
        at = slice(128 * block, 128 * block + 128)
        faces[2, :, at] = turned[0:1, :]
        faces[3, :, at] = turned[127:128, :]
    for each in small:
        each.wait()
    own[0:32, :] = dst[...].astype(F32)
    own[48:56, :] = jnp.zeros((8, WIDTH), F32)
    for offset in range(NB):
        own[48 + offset : 49 + offset, 0:TILES] = pattern[offset].astype(F32)
    first, last = fluid[0:64, :], fluid[960:1024, :]
    for packed, start, face in (
        (staged_in, 6 * TILE_ROWS, jnp.where(parity == 0, last, first)),
        (staged_out, 2 * TILE_ROWS, jnp.where(parity == 0, first, last)),
    ):
        packed[start : start + 56, :] = own[...]
        packed[start + 56 : start + SMALL, :] = face
    y, z = lax.axis_index("gy"), lax.axis_index("gz")
    after_y, before_y = lax.rem(y + 1, 4) * 4 + z, lax.rem(y + 3, 4) * 4 + z
    for slab in range(16):
        at = slice(128 * slab, 128 * slab + 128)
        faces[0, :, at] = fluid[64 * slab : 64 * slab + 1, :]
        faces[1, :, at] = fluid[64 * slab + 63 : 64 * slab + 64, :]
    saves = [
        copy(faces.at[index], faces_hbm.at[place], 19 + index)
        for index, place in enumerate((before_y, after_y, before_z, after_z))
    ]
    load_src.wait()
    group = 4
    for start in range(0, RUNS, group):
        if start == RUNS // 2:
            inside.wait()
            outside.wait()
            inside = copy(staged_in, on_chip_hbm, 17)
            outside = copy(staged_out, across_hbm, 18)
        ids = lanes([src[r : r + 1, :] for r in range(start, start + group)])
        picked = jnp.dot(table[...], row_hots(ids >> 7, ROWS), preferred_element_type=F32)
        both = picked[0:128] + picked[128:256]
        mask = lax.broadcasted_iota(I32, (WIDTH, group * WIDTH), 0) == (ids & 127)
        value = jnp.sum(jnp.where(mask, both, 0.0), axis=0, keepdims=True)
        for r in range(start, start + group):
            mine = value[:, (r - start) * WIDTH : (r - start + 1) * WIDTH]
            outgoing[r : r + 1, :] = mine
            sent[r, :, 0:128] = mine
            sent[r ^ 1, :, 128:256] = mine
            beside = (r + 1) % RUNS if r % 2 else (r - 1) % RUNS
            sent[beside, :, 256:384] = mine
    for each in (inside, outside, *saves):
        each.wait()


def spread_run(ids_of, values_of):
    group = 8
    total = None
    for start in range(0, RUNS, group):
        cell = lanes([ids_of(r) for r in range(start, start + group)])
        value = lanes([values_of(r) for r in range(start, start + group)])
        row = jnp.where(cell >= 0, ((cell >> 5) & 3) * 8 + (cell >> 7), -1)
        hots = row_hots(row, 32)
        placed = placed_parts(cell & 31, 32, value)
        added = lax.dot_general(hots, placed, CONTRACT_LAST, preferred_element_type=F32)
        total = added if total is None else total + added
    total = total[:, 0:32] + total[:, 32:64]
    return lanes([total[8 * u : 8 * u + 8, :] for u in range(4)])


def window(parity, own, partner, beside):
    pad = jnp.zeros((4, own.shape[1]), F32)
    low = jnp.concatenate([beside[4:8], own, partner, pad], axis=0)
    high = jnp.concatenate([partner, own, beside[0:4], pad], axis=0)
    return jnp.where(parity == 0, low, high)


def neighbours(iterate, pats, first, count, shifted):
    for offset in range(NB):
        values = iterate[first - 2 + offset : first - 2 + offset + count, :]
        shifted[offset, first : first + count, :] = values * pats[offset, first : first + count, :]


def apply_tile(blocks, tile, shifted, place, coupled):
    total = None
    for offset in range(NB):
        start = pl.multiple_of(tile * TILE_ROWS + offset * WIDTH, WIDTH)
        term = blocks[pl.ds(start, WIDTH), :] * shifted[offset, pl.ds(place, 1), :]
        total = term if total is None else total + term
    coupled[pl.ds(place, 1), :] = jnp.sum(total.T, axis=0, keepdims=True)


RHO = [0.5]
for _ in range(3):
    RHO.append(1.0 / (4.0 - RHO[-1]))


def stepped(sweep, value, update, right, inverse, diagonal, coupled):
    residual = right - (diagonal * value + coupled)
    if sweep == 0:
        update = inverse * residual
    else:
        update = RHO[sweep] * RHO[sweep - 1] * update + 4.0 * RHO[sweep] * inverse * residual
    return value + update, update


def own_run_kernel(arrived, dst, added):
    added[...] = spread_run(lambda r: dst[r : r + 1, :], lambda r: arrived[r, :, 0:128])


def beside_run_kernel(arrived, across_hbm, added_own, added, small, sem):
    load = pltpu.make_async_copy(across_hbm.at[2 * TILE_ROWS : 2 * TILE_ROWS + SMALL], small, sem)
    load.start()
    added[0:TILES, :] = added_own[...]
    load.wait()
    added[TILES : 2 * TILES, :] = spread_run(
        lambda r: small[r : r + 1, :].astype(I32), lambda r: arrived[r, :, 256:384]
    )


def windows(parity, keep, own, partner, beside, added):
    holders = [own, partner, beside]
    diagonals = [each[40:48] for each in holders]
    rights = [d * each[32:40] + a for d, each, a in zip(diagonals, holders, added)]
    inverses = [1.0 / d for d in diagonals]
    rights[2], inverses[2] = rights[2] * keep, inverses[2] * keep
    present = window(parity, *[each[48:56].T[0:TILES] for each in holders])
    return window(parity, *rights), window(parity, *inverses), window(parity, *diagonals), present


def wall_edge_kernel(
    added_before, beside_small, own, own_blocks, across_hbm,
    products, swap,
    outer, pats, iterate, shifted, coupled, sem,
):
    load = pltpu.make_async_copy(across_hbm.at[0 : 2 * TILE_ROWS], outer, sem)
    load.start()
    me = lax.axis_index("gx")
    parity = lax.rem(me, 2)
    keep = jnp.where((me == 0) | (me == RUNS - 1), 0.0, 1.0)
    mine = own[...]
    added = [added_before[0:TILES, :], jnp.zeros((TILES, WIDTH), F32), added_before[TILES : 2 * TILES, :]]
    right, inverse, diagonal, present = windows(parity, keep, mine, mine, beside_small[...], added)
    for offset in range(NB):
        pats[offset] = jnp.broadcast_to(present[:, offset : offset + 1], (WIN, WIDTH))
    value = inverse * right
    iterate[...] = value
    shifted[...] = jnp.zeros((NB, WIN, WIDTH), F32)
    coupled[...] = jnp.zeros((WIN, WIDTH), F32)
    own_at = 4 + 4 * parity
    neighbours(iterate, pats, 2, 16, shifted)
    for index in range(6):
        tile = index + 2 * parity
        apply_tile(own_blocks, tile, shifted, own_at + tile, coupled)
    load.wait()
    for index in range(2):
        apply_tile(outer, index, shifted, 2 + 14 * parity + index, coupled)
    products[0] = coupled[...]
    value, update = stepped(0, value, None, right, inverse, diagonal, coupled[...])
    iterate[...] = value
    neighbours(iterate, pats, 4, 12, shifted)
    for index in range(4):
        tile = index + 4 * parity
        apply_tile(own_blocks, tile, shifted, own_at + tile, coupled)
    products[1] = coupled[...]
    value, update = stepped(1, value, update, right, inverse, diagonal, coupled[...])
    swap[0:4, :] = jnp.where(parity == 0, value[4:8], value[12:16])
    swap[4:8, :] = jnp.where(parity == 0, update[4:8], update[12:16])


def wall_inner_kernel(
    arrived, added_before, beside_small, own, products, own_blocks, on_chip_hbm,
    state, pats, inside, faces,
    inner, iterate, shifted, coupled, sems,
):
    at_in = 6 * TILE_ROWS
    loads = [
        pltpu.make_async_copy(on_chip_hbm.at[low:high], inner.at[low:high], sems.at[index])
        for index, (low, high) in enumerate(((at_in, at_in + SMALL), (0, at_in)))
    ]
    for each in loads:
        each.start()
    me = lax.axis_index("gx")
    parity = lax.rem(me, 2)
    keep = jnp.where((me == 0) | (me == RUNS - 1), 0.0, 1.0)
    loads[0].wait()
    partner, beside = inner[at_in : at_in + SMALL, :], beside_small[...]
    added = [
        added_before[0:TILES, :],
        spread_run(lambda r: inner[at_in + r : at_in + r + 1, :].astype(I32), lambda r: arrived[r, :, 128:256]),
        added_before[TILES : 2 * TILES, :],
    ]
    right, inverse, diagonal, present = windows(parity, keep, own[...], partner, beside, added)
    for offset in range(NB):
        pats[offset] = jnp.broadcast_to(present[:, offset : offset + 1], (WIN, WIDTH))
    faces[0] = jnp.where(parity == 0, beside[56:120], partner[56:120])
    faces[1] = jnp.where(parity == 0, partner[56:120], beside[56:120])
    place = lax.broadcasted_iota(I32, (WIN, WIDTH), 0)
    value = inverse * right
    iterate[...] = value
    shifted[...] = jnp.zeros((NB, WIN, WIDTH), F32)
    coupled[...] = jnp.zeros((WIN, WIDTH), F32)
    own_at = 4 + 4 * parity

    neighbours(iterate, pats, 2, 16, shifted)
    for index in range(2):
        tile = index + 6 - 6 * parity
        apply_tile(own_blocks, tile, shifted, own_at + tile, coupled)
    loads[1].wait()
    for index in range(6):
        apply_tile(inner, index, shifted, 12 - 10 * parity + index, coupled)
    low = 2 + 8 * parity
    product = jnp.where((place >= low) & (place < low + 8), products[0], coupled[...])
    value, update = stepped(0, value, None, right, inverse, diagonal, product)
    iterate[...] = value

    neighbours(iterate, pats, 4, 12, shifted)
    for index in range(4):
        tile = index + 4 - 4 * parity
        apply_tile(own_blocks, tile, shifted, own_at + tile, coupled)
    for index in range(4):
        apply_tile(inner, index + 2 * parity, shifted, 12 - 8 * parity + index, coupled)
    low = 4 + 8 * parity
    product = jnp.where((place >= low) & (place < low + 4), products[1], coupled[...])
    value, update = stepped(1, value, update, right, inverse, diagonal, product)
    state[0], state[1], state[2], state[3], state[4] = value, update, right, inverse, diagonal
    iterate[...] = value

    neighbours(iterate, pats, 6, 8, shifted)
    for index in range(6):
        tile = index + 2 - 2 * parity
        apply_tile(own_blocks, tile, shifted, own_at + tile, coupled)
    for index in range(2):
        apply_tile(inner, index + 4 * parity, shifted, 12 - 6 * parity + index, coupled)
    value, update = stepped(2, value, update, right, inverse, diagonal, coupled[...])
    inside[0], inside[1] = value, update
    iterate[...] = value
    neighbours(iterate, pats, 8, 4, shifted)
    for index in range(4):
        tile = index + 4 - 4 * parity
        apply_tile(own_blocks, tile, shifted, own_at + tile, coupled)
    inside[2] = coupled[...]


def wall_last_kernel(
    state, pats, inside, swapped, own, own_blocks, across_hbm,
    solid, returned, outer, iterate, shifted, coupled, sem,
):
    load = pltpu.make_async_copy(across_hbm.at[0 : 2 * TILE_ROWS], outer, sem)
    load.start()
    me = lax.axis_index("gx")
    parity = lax.rem(me, 2)
    keep = jnp.where((me == 0) | (me == RUNS - 1), 0.0, 1.0)
    value, update, right, inverse, diagonal = (state[i] for i in range(5))

    def with_swapped(inside, outside):
        low = jnp.concatenate([outside, inside[4:24]], axis=0)
        high = jnp.concatenate([inside[0:16], outside, inside[20:24]], axis=0)
        return jnp.where(parity == 0, low, high)

    value = with_swapped(value, swapped[0:4, :] * keep)
    update = with_swapped(update, swapped[4:8, :] * keep)
    place = lax.broadcasted_iota(I32, (WIN, WIDTH), 0)
    own_at = 4 + 4 * parity
    iterate[...] = value
    shifted[...] = jnp.zeros((NB, WIN, WIDTH), F32)
    coupled[...] = jnp.zeros((WIN, WIDTH), F32)
    neighbours(iterate, pats, 2, 16, shifted)
    for index in range(2):
        tile = index + 6 * parity
        apply_tile(own_blocks, tile, shifted, own_at + tile, coupled)
    load.wait()
    for index in range(2):
        apply_tile(outer, index, shifted, 2 + 14 * parity + index, coupled)
    value, update = stepped(2, value, update, right, inverse, diagonal, coupled[...])
    known = (place >= 6) & (place < 14)
    value, update = jnp.where(known, inside[0], value), jnp.where(known, inside[1], update)
    iterate[...] = value
    neighbours(iterate, pats, 4, 12, shifted)
    for index in range(4):
        tile = index + 4 * parity
        apply_tile(own_blocks, tile, shifted, own_at + tile, coupled)
    product = jnp.where((place >= 8) & (place < 12), inside[2], coupled[...])
    value, update = stepped(3, value, update, right, inverse, diagonal, product)
    mine = jnp.where(parity == 0, value[4:12], value[8:16])
    solid[...] = mine
    for block in range(4):
        cell = own[8 * block : 8 * block + 8, :].astype(I32)
        tile, lane = cell >> 7, cell & 127
        found = jnp.zeros((8, WIDTH), F32)
        for index in range(TILES):
            row = jnp.broadcast_to(mine[index : index + 1, :], (8, WIDTH))
            found = jnp.where(tile == index, jnp.take_along_axis(row, lane, axis=1, mode="promise_in_bounds"), found)
        for r in range(8):
            returned[8 * block + r] = found[r : r + 1, :]


def final_kernel(fluid, liquid, x_faces, faces, src, outgoing, returned, fluid_new):
    group = 4
    total = None
    for start in range(0, RUNS, group):
        rows = range(start, start + group)
        ids = lanes([src[r : r + 1, :] for r in rows])
        value = lanes([returned[r] - outgoing[r : r + 1, :] for r in rows])
        placed = placed_parts(ids & 127, WIDTH, value)
        added = lax.dot_general(row_hots(ids >> 7, ROWS), placed, CONTRACT_LAST, preferred_element_type=F32)
        total = added if total is None else total + added
    wall = total[:, 0:128] + total[:, 128:256]
    y, z = lax.axis_index("gy"), lax.axis_index("gz")
    after_y, before_y = lax.rem(y + 1, 4) * 4 + z, lax.rem(y + 3, 4) * 4 + z
    after_z, before_z = y * 4 + lax.rem(z + 1, 4), y * 4 + lax.rem(z + 3, 4)
    row = lax.broadcasted_iota(I32, (64, WIDTH), 0)
    lane = lax.broadcasted_iota(I32, (64, WIDTH), 1)
    for slab in range(16):
        start = 64 * slab
        at, at_z = slice(128 * slab, 128 * slab + 128), slice(128 * (slab // 2), 128 * (slab // 2) + 128)
        here = fluid[start : start + 64, :]
        total = (fluid[start - 64 : start, :] if slab else x_faces[0]) + (
            fluid[start + 64 : start + 128, :] if slab < 15 else x_faces[1]
        )
        total = total + jnp.where(row == 0, faces[before_y, :, at], pltpu.roll(here, 1, 0))
        total = total + jnp.where(row == 63, faces[after_y, :, at], pltpu.roll(here, 63, 0))
        half = 64 * (slab % 2)
        left = jnp.broadcast_to(faces[before_z, :, at_z], (WIDTH, WIDTH)).T[half : half + 64, :]
        right = jnp.broadcast_to(faces[after_z, :, at_z], (WIDTH, WIDTH)).T[half : half + 64, :]
        total = total + jnp.where(lane == 0, left, pltpu.roll(here, 1, 1))
        total = total + jnp.where(lane == 127, right, pltpu.roll(here, 127, 1))
        total = total - 6.0 * here
        share = liquid[start : start + 64, :].astype(F32)
        fluid_new[start : start + 64, :] = (
            here
            + DIFFUSION * total
            - EVAPORATION * share * jnp.maximum(here - SATURATION, 0.0)
            + WALL_COUPLING * wall[start : start + 64, :]
        )


def shape(*dims):
    return jax.ShapeDtypeStruct(dims, F32)


def call(kernel, mib, ins, outs, out_specs, scratch, flops, moved):
    return pl.pallas_call(
        kernel,
        in_specs=ins,
        out_shape=outs,
        out_specs=out_specs,
        scratch_shapes=scratch,
        compiler_params=params(mib),
        cost_estimate=pl.CostEstimate(flops=flops, bytes_accessed=moved, transcendentals=0),
    )


def vmem(*dims, kind=F32):
    return pltpu.VMEM(dims, kind)


def dma(*dims):
    return pltpu.SemaphoreType.DMA(dims) if dims else pltpu.SemaphoreType.DMA


def per_device(fluid_temp, liquid, face_src, face_dst, solid_old, solid_diag, blocks, pattern):
    inside_pairs = [(i, i ^ 1) for i in range(RUNS)]
    outside_pairs = [(i, (i - 1) % RUNS if i % 2 == 0 else (i + 1) % RUNS) for i in range(RUNS)]
    fluid = fluid_temp.reshape(ROWS, WIDTH)
    src = face_src.reshape(RUNS, WIDTH)
    dst = face_dst.reshape(RUNS, WIDTH)
    own_blocks = blocks.reshape(TILES * TILE_ROWS, WIDTH)
    in_rows, out_rows = 6 * TILE_ROWS + SMALL, 2 * TILE_ROWS + SMALL

    sent, outgoing, own, faces, on_chip, across = call(
        pick_kernel, 60,
        [HBM] * 7,
        (
            shape(RUNS, 1, 384), shape(RUNS, WIDTH), shape(56, WIDTH), shape(16, 1, 2048),
            shape(in_rows, WIDTH), shape(out_rows, WIDTH),
        ),
        (VMEM, VMEM, VMEM, HBM, HBM, HBM),
        [
            vmem(ROWS, WIDTH), vmem(RUNS, WIDTH, kind=I32), vmem(RUNS, WIDTH, kind=I32), vmem(NB, 1, TILES, kind=I32),
            vmem(256, ROWS, kind=BF16), vmem(in_rows, WIDTH), vmem(out_rows, WIDTH), vmem(4, 1, 2048), dma(23),
        ],
        2 * 256 * 1024 * 4096, 1 << 22,
    )(fluid, src, dst, solid_old[0], solid_diag[0], jnp.transpose(pattern, (2, 0, 1)), own_blocks)

    arrived = lax.all_to_all(sent, "gx", split_axis=0, concat_axis=0, tiled=True)
    on_chip = lax.ppermute(on_chip, "gx", inside_pairs)
    across = lax.ppermute(across, "gx", outside_pairs)
    faces = lax.all_to_all(faces, ("gy", "gz"), split_axis=0, concat_axis=0, tiled=True)

    work = [vmem(WIN, WIDTH), vmem(NB, WIN, WIDTH), vmem(WIN, WIDTH)]
    added_own = call(
        own_run_kernel, 12, [VMEM, VMEM], shape(TILES, WIDTH), VMEM, [], 65 * 10**8, 1 << 16
    )(arrived, dst)
    added_before, beside_small = call(
        beside_run_kernel, 12, [VMEM, ANY, VMEM], (shape(2 * TILES, WIDTH), shape(SMALL, WIDTH)), (VMEM, VMEM), [dma()],
        14 * 10**9, 1 << 16,
    )(arrived, across, added_own)
    products, swap = call(
        wall_edge_kernel, 12,
        [VMEM] * 4 + [ANY],
        (shape(2, WIN, WIDTH), shape(8, WIDTH)), (VMEM, VMEM),
        [vmem(2 * TILE_ROWS, WIDTH), vmem(NB, WIN, WIDTH)] + work + [dma()],
        1 << 23, 4 << 20,
    )(added_before, beside_small, own, own_blocks, across)
    swapped = lax.ppermute(swap, "gx", outside_pairs)
    state, pats, inside, x_faces = call(
        wall_inner_kernel, 16,
        [VMEM] * 6 + [ANY],
        (shape(5, WIN, WIDTH), shape(NB, WIN, WIDTH), shape(3, WIN, WIDTH), shape(2, 64, WIDTH)), (VMEM,) * 4,
        [vmem(in_rows, WIDTH)] + work + [dma(2)],
        1 << 24, 6 << 20,
    )(arrived, added_before, beside_small, own, products, own_blocks, on_chip)
    solid, sent_back = call(
        wall_last_kernel, 12,
        [VMEM] * 6 + [ANY],
        (shape(TILES, WIDTH), shape(RUNS, 1, WIDTH)), (VMEM, VMEM),
        [vmem(2 * TILE_ROWS, WIDTH)] + work + [dma()],
        1 << 23, 3 << 20,
    )(state, pats, inside, swapped, own, own_blocks, across)
    returned = lax.all_to_all(sent_back, "gx", split_axis=0, concat_axis=0, tiled=True)

    fluid_new = call(
        final_kernel, 16, [VMEM] * 7, shape(ROWS, WIDTH), VMEM, [], 2 * 256 * 1024 * 4096, 1 << 20
    )(fluid, liquid.reshape(ROWS, WIDTH), x_faces, faces, src, outgoing, returned)
    return fluid_new.reshape(fluid_temp.shape), solid[None]


def solution(mesh):
    return jax.shard_map(
        per_device,
        mesh=mesh,
        in_specs=(
            P("gx", "gy", "gz"),
            P("gx", "gy", "gz"),
            P("gx", "gy", "gz", None),
            P("gx", "gy", "gz", None),
            P(("gy", "gz"), "gx", None),
            P(("gy", "gz"), "gx", None),
            P(("gy", "gz"), "gx", None, None, None),
            P(("gy", "gz"), "gx", None),
        ),
        out_specs=(P("gx", "gy", "gz"), P(("gy", "gz"), "gx", None)),
        check_vma=False,
    )
```
